32 devices in a mesh: blocks: 2 (over x), slab: 16 (over z, y, core).
Axes of the slice: x: 2, y: 2, z: 4, core: 2. Of those that a mesh axis runs over, the one named last changes fastest.
Arguments:
- estimate: float32 [64, 256, 128], P('blocks', 'slab'), parts along dimension 0, may hold values from 0.25 to 8, as said below
- raw_views: float32 [6, 64, 256, 128], P(None, 'blocks', 'slab'), parts along dimension 1, may hold values from 0.1 to 30, as said below
- psf_taps: float32 [6, 3, 31], replicated, may hold values from 0 to 1, as said below
Outputs:
- restored: float32 [64, 256, 128], P('blocks', 'slab'), parts along dimension 0
The draws below stay inside these ranges and needn't reach their ends.
There are 2 independent parts, one for each index of `blocks`. The reference program is written for one: setup_inputs(seed, part) draws one part's arguments, and reference() takes and returns one part's arrays. A program takes and returns all parts, laid end to end along the dimension named above; an argument that names none is the same for every part. Nothing has to cross between parts.
Inputs may be any that keep to these rules, and one draw needn't show every extreme that they name: `estimate`: positive. `raw_views`: positive. `psf_taps`: every tap is positive, and each view's taps along each dimension sum to 1.
All inputs are finite; a program needn't handle non-finite values.
Results may differ from the reference program's by a relative error of at most 0.0001.
Values sent between devices are 32-bit elements; how exact they have to be, the bound alone decides.
No kernel may reach another device: no remote copies, remote signals or barrier semaphores. Data moves between devices by JAX's collectives and lax.ppermute only.
A program may use at most 64 MiB of HBM per device.

```python
import math
import jax
import jax.numpy as jnp
from jax import lax

VIEWS = 6
TAPS = 31
ITERS = 2
DEPTH = 32
X = 128
Y = 256


def ramp_rows():
    row_index = jnp.arange(Y, dtype=jnp.float32)
    return (1.0 + 2.0 * row_index / (Y - 1)).reshape(1, Y, 1)


def falling_rows():
    row_index = jnp.arange(Y, dtype=jnp.float32)
    return (3.0 - 2.0 * row_index / (Y - 1)).reshape(1, Y, 1)


def draw_estimate(key, part):
    key_base = jax.random.fold_in(key, 11)
    shape_full = (DEPTH, Y, X)
    base_values = jnp.exp(jax.random.uniform(key_base, shape_full, jnp.float32, math.log(0.5), math.log(2.0)))
    return base_values * ramp_rows()


def draw_raw_views(key, part):
    key_base = jax.random.fold_in(key, 23)
    key_factor = jax.random.fold_in(key, 29)
    shape_full = (VIEWS, DEPTH, Y, X)
    factor = jnp.exp(jax.random.uniform(key_factor, (VIEWS, 1, 1, 1), jnp.float32, math.log(0.5), math.log(2.0)))
    base_values = jnp.exp(jax.random.uniform(key_base, shape_full, jnp.float32, math.log(0.2), math.log(5.0)))
    return base_values * factor * falling_rows()[None]


def draw_psf_taps(key, part):
    key_sigma = jax.random.fold_in(key, 37)
    key_rough = jax.random.fold_in(key, 41)
    lows = jnp.array([3.0, 2.0, 1.5], jnp.float32).reshape(1, 3, 1)
    highs = jnp.array([8.0, 6.0, 4.0], jnp.float32).reshape(1, 3, 1)
    unit = jax.random.uniform(key_sigma, (VIEWS, 3, 1), jnp.float32)
    sigma = jnp.exp(jnp.log(lows) + unit * (jnp.log(highs) - jnp.log(lows)))
    offsets = (jnp.arange(TAPS, dtype=jnp.float32) - (TAPS - 1) / 2.0).reshape(1, 1, TAPS)
    bumps = jnp.exp(-offsets * offsets / (2.0 * sigma * sigma)) + 0.02
    rough = jax.random.uniform(key_rough, (VIEWS, 3, TAPS), jnp.float32, 0.6, 1.4)
    shaped = bumps * rough
    return shaped / jnp.sum(shaped, axis=2, keepdims=True)


def setup_inputs(seed: int = 0, part: int = 0) -> dict:
    splits = jax.random.split(jax.random.key(seed), 4)
    own_keys = jax.random.split(jax.random.fold_in(splits[3], part), 4)
    estimate = draw_estimate(jax.random.fold_in(jax.random.fold_in(splits[3], part), 71), part)
    raw_views = draw_raw_views(jax.random.fold_in(jax.random.fold_in(splits[3], part), 71), part)
    psf_taps = draw_psf_taps(jax.random.fold_in(splits[3], 71), part)
    return dict(estimate=estimate, raw_views=raw_views, psf_taps=psf_taps)


def along_dim(volume, coeffs, dim_index):
    extent = volume.shape[dim_index]
    margin = coeffs.shape[0] // 2
    widths = [(0, 0)] * volume.ndim
    widths[dim_index] = (margin, margin)
    padded = jnp.pad(volume, widths)
    running = jnp.zeros_like(volume)
    for offset in range(coeffs.shape[0]):
        running = running + coeffs[offset] * lax.slice_in_dim(padded, offset, offset + extent, axis=dim_index)
    return running


def forward(volume, kernel):
    volume = along_dim(volume, kernel[0], 0)
    volume = along_dim(volume, kernel[1], 1)
    return along_dim(volume, kernel[2], 2)


def adjoint(volume, kernel):
    return forward(volume, kernel[:, ::-1])


def reference(estimate, raw_views, psf_taps):
    view_total = jnp.sum(raw_views, axis=(1, 2, 3))
    current = estimate
    for iteration in range(ITERS):
        blurred = lax.map(lambda kernel: forward(current, kernel), psf_taps)
        scale = jnp.sum(blurred, axis=(1, 2, 3)) / view_total
        ratio = scale.reshape(-1, 1, 1, 1) * raw_views / blurred
        logs = lax.map(lambda pair: jnp.log(adjoint(pair[0], pair[1])), (ratio, psf_taps))
        current = current * jnp.exp(jnp.mean(logs, axis=0))
    return current
```

```python
import functools

import jax
import jax.numpy as jnp
import numpy as np
from jax import lax
from jax.experimental import pallas as pl
from jax.experimental.pallas import tpu as pltpu
from jax.sharding import PartitionSpec as P

ITERS = 2
F32 = jnp.float32
BF16 = jnp.bfloat16
VMEM = pltpu.MemorySpace.VMEM
SMEM = pltpu.MemorySpace.SMEM
FULL = pl.BlockSpec(memory_space=VMEM)
LIMIT = 56 * 1024 * 1024


def split(value):
    high = value.astype(BF16)
    low = (value - high.astype(F32)).astype(BF16)
    return high, low


def dot(a, b):
    return jnp.dot(a, b, preferred_element_type=F32)


def placed_row(taps, lane_of_tap, width):
    count = taps.shape[1]
    tap = lax.broadcasted_iota(jnp.int32, (count, width), 0)
    lane = lax.broadcasted_iota(jnp.int32, (count, width), 1)
    onehot = jnp.where(lane == lane_of_tap(tap), 1.0, 0.0).astype(F32)
    return jnp.dot(taps, onehot, precision=lax.Precision.HIGHEST, preferred_element_type=F32)


def slanted(row, height):
    full = jnp.broadcast_to(row, (height, row.shape[1]))
    return pltpu.roll(full, 0, 1, stride=1, stride_axis=0)


def weights_kernel(rows, taps_ref, *outs):
    views, _, count = taps_ref.shape
    margin = count // 2
    for flip in (False, True):
        wy, wx, wz = outs[3 * flip : 3 * flip + 3]
        order = (lambda k: count - 1 - k) if flip else (lambda k: k)
        out_rows = rows if flip else 3 * rows
        in_rows = out_rows + 2 * rows
        planes = wz.shape[1] // 8
        cols = wx.shape[1] // 2
        row_y = placed_row(taps_ref[:, 1, :], lambda k: order(k) + rows - margin, 256)
        high = row_y.astype(BF16).astype(F32)
        low = row_y - high
        row_y = high + pltpu.roll(high, in_rows, 1) + pltpu.roll(low, 2 * in_rows, 1)
        row_x = placed_row(taps_ref[:, 2, :], lambda k: lax.rem(margin - order(k) + 2 * cols, 2 * cols), 2 * cols)
        width_z = 16 * planes
        row_z = placed_row(
            taps_ref[:, 0, :], lambda k: lax.rem(8 * (order(k) - margin) + width_z, width_z), width_z
        )
        for v in range(views):
            band = slanted(row_y[v : v + 1], out_rows)
            wy[v * out_rows : (v + 1) * out_rows, :] = band[:, : 3 * in_rows].astype(BF16)
            high, low = split(slanted(row_x[v : v + 1], cols)[:, :cols])
            wx[v, :cols, :cols] = high
            wx[v, cols:, :cols] = high
            wx[v, :cols, cols:] = low
            wx[v, cols:, cols:] = low
            size = 8 * planes
            high, low = split(slanted(row_z[v : v + 1], size)[:, :size])
            wz[v, :, :size] = high
            wz[v, :, size : 2 * size] = high
            wz[v, :, 2 * size :] = low


def make_weights(taps, planes, rows, cols):
    views = taps.shape[0]
    shapes = []
    for out_rows in (3 * rows, rows):
        shapes += [
            jax.ShapeDtypeStruct((views * out_rows, 3 * (out_rows + 2 * rows)), BF16),
            jax.ShapeDtypeStruct((views, 2 * cols, 2 * cols), BF16),
            jax.ShapeDtypeStruct((views, 8 * planes, 24 * planes), BF16),
        ]
    outs = pl.pallas_call(
        functools.partial(weights_kernel, rows),
        out_shape=shapes,
        in_specs=[FULL],
        out_specs=[FULL] * 6,
        compiler_params=pltpu.CompilerParams(vmem_limit_bytes=LIMIT),
        cost_estimate=pl.CostEstimate(flops=10**7, bytes_accessed=10**7, transcendentals=0),
        name="weights",
    )(taps)
    return outs[:3], outs[3:]


def stacked(pieces):
    columns = []
    for piece in pieces:
        high, low = split(piece)
        columns.append(jnp.concatenate([high, low, high], axis=0))
    return jnp.concatenate(columns, axis=1)


def columns_then_planes(ys_ref, wx, wz, xs_ref, emit):
    planes, height, cols = xs_ref.shape
    both = dot(ys_ref[...], wx)
    xs_ref[...] = (both[:, :cols] + both[:, cols:]).reshape(planes, height, cols)
    for pair in range(height // 16):
        groups = (2 * pair, 2 * pair + 1)
        rhs = stacked([xs_ref[:, 8 * g : 8 * g + 8, :].reshape(planes * 8, cols) for g in groups])
        result = dot(wz, rhs)
        for j, g in enumerate(groups):
            emit(g, result[:, j * cols : (j + 1) * cols].reshape(planes, 8, cols))


def forward_kernel(e2a, e2b, e1, e0, f1, f2a, f2b, wy, wx, wz, out, ys, xs):
    planes, rows, cols = e0.shape
    views = out.shape[0]
    height = 3 * rows

    def plane(z):
        return jnp.concatenate([e2a[z] + e2b[z], e1[z], e0[z], f1[z], f2a[z] + f2b[z]], axis=0)

    def blur_rows(i, _):
        z = 2 * i
        result = dot(wy[...], stacked([plane(z), plane(z + 1)]))
        high, low = split(result)
        for j in range(2):
            for v in range(views):
                at = pl.ds(pl.multiple_of((z + j) * height, height), height)
                there = (slice(v * height, (v + 1) * height), slice(j * cols, (j + 1) * cols))
                ys[v, at, :cols] = high[there]
                ys[v, at, cols:] = low[there]
        return 0

    lax.fori_loop(0, planes // 2, blur_rows, 0)

    def per_view(v, _):
        def emit(group, values):
            out[v, :, 8 * group : 8 * group + 8, :] = values

        columns_then_planes(ys.at[v], wx[v], wz[v], xs, emit)
        return 0

    lax.fori_loop(0, views, per_view, 0)


def forward(slabs, weights):
    planes, rows, cols = slabs[0].shape
    views = weights[1].shape[0]
    return pl.pallas_call(
        forward_kernel,
        out_shape=jax.ShapeDtypeStruct((views, planes, 3 * rows, cols), F32),
        in_specs=[FULL] * 10,
        out_specs=FULL,
        scratch_shapes=[
            pltpu.VMEM((views, planes * 3 * rows, 2 * cols), BF16),
            pltpu.VMEM((planes, 3 * rows, cols), F32),
        ],
        compiler_params=pltpu.CompilerParams(vmem_limit_bytes=LIMIT),
        cost_estimate=pl.CostEstimate(flops=10**10, bytes_accessed=10**7, transcendentals=0),
        name="forward",
    )(*slabs, *weights)


def adjoint_kernel(first, last, current, blurred, before, raw, after, wy, wx, wz, acc_in, wzs, wyx, out, sums, ys, xs, acc):
    planes, rows, cols = current.shape
    step = pl.program_id(0)

    @pl.when(step == 0)
    def _():
        if first:
            acc[...] = jnp.zeros_like(acc)
        else:
            acc[...] = acc_in[...]

    def quotient(z):
        counts = jnp.concatenate([before[0, z], raw[0, z], after[0, z]], axis=0)
        inside = counts > 0.0
        return jnp.where(inside, counts / jnp.where(inside, blurred[0, z], 1.0), 0.0)

    def blur_rows(i, _):
        z = 2 * i
        result = dot(wy[0], stacked([quotient(z), quotient(z + 1)]))
        high, low = split(result)
        for j in range(2):
            at = pl.ds(pl.multiple_of((z + j) * rows, rows), rows)
            ys[at, :cols] = high[:, j * cols : (j + 1) * cols]
            ys[at, cols:] = low[:, j * cols : (j + 1) * cols]
        return 0

    lax.fori_loop(0, planes // 2, blur_rows, 0)

    def emit(group, values):
        acc[:, 8 * group : 8 * group + 8, :] += jnp.log(values)

    columns_then_planes(ys, wx[0], wz[0], xs, emit)

    @pl.when(step == pl.num_programs(0) - 1)
    def _():
        if last:
            views = wyx.shape[0]
            out[...] = current[...] * jnp.exp(acc[...] * (1.0 / views))
            for v in range(views):
                total = jnp.zeros((rows, cols), F32)
                for z in range(planes):
                    total = total + wzs[v, z] * out[z]
                sums[v : v + 1, :] = jnp.sum(total * wyx[v], axis=0, keepdims=True)
        else:
            out[...] = acc[...]
            sums[...] = jnp.zeros_like(sums)


def adjoint(views, start, total, current, blurred, before, raw, after, weights, acc, wzs, wyx):
    planes, rows, cols = current.shape
    wy, wx, wz = weights
    first, last = start == 0, start + views == total
    whole = lambda shape: pl.BlockSpec(shape, lambda v: (0,) * len(shape))
    one = lambda shape, at: pl.BlockSpec((1,) + shape, lambda v: (v + at,) + (0,) * len(shape))
    if acc is None:
        acc = jnp.zeros((8, 128), F32)
    return pl.pallas_call(
        functools.partial(adjoint_kernel, first, last),
        grid=(views,),
        out_shape=[jax.ShapeDtypeStruct(current.shape, F32), jax.ShapeDtypeStruct((total, cols), F32)],
        in_specs=[
            whole(current.shape),
            one((planes, 3 * rows, cols), start),
            one((planes, rows, cols), 0),
            one((planes, rows, cols), start),
            one((planes, rows, cols), 0),
            one((rows, wy.shape[2]), start),
            one(wx.shape[1:], start),
            one(wz.shape[1:], start),
            whole(acc.shape),
            pl.BlockSpec(memory_space=SMEM),
            whole(wyx.shape),
        ],
        out_specs=[whole(current.shape), whole((total, cols))],
        scratch_shapes=[
            pltpu.VMEM((planes * rows, 2 * cols), BF16),
            pltpu.VMEM((planes, rows, cols), F32),
            pltpu.VMEM((planes, rows, cols), F32),
        ],
        compiler_params=pltpu.CompilerParams(vmem_limit_bytes=LIMIT),
        cost_estimate=pl.CostEstimate(flops=views * 10**9, bytes_accessed=views * 3 * 10**6, transcendentals=10**5),
        name="adjoint",
    )(current, blurred, before, raw, after, wy, wx, wz, acc, wzs, wyx)


def neighbours(value, count):
    up = [(i, i + 1) for i in range(count - 1)]
    down = [(j, i) for i, j in up]
    up_two = [(i, i + 2) for i in range(0, count - 2, 2)]
    down_two = [(i, i - 2) for i in range(3, count, 2)]
    up_in = [(i, i + 1) for i in range(0, count - 1, 2)]
    down_in = [(i + 1, i) for i in range(0, count - 1, 2)]
    before = lax.ppermute(value, "slab", up)
    after = lax.ppermute(value, "slab", down)
    before_two = lax.ppermute(value, "slab", up_two)
    after_two = lax.ppermute(value, "slab", down_two)
    before_in = lax.ppermute(before, "slab", up_in)
    after_in = lax.ppermute(after, "slab", down_in)
    return before_two, before_in, before, value, after, after_two, after_in


def tap_sums(taps, offset, extent, total):
    count = taps.shape[1]
    target = offset + jnp.arange(extent)[None, :] - jnp.arange(count)[:, None] + count // 2
    reach = jnp.where((target >= 0) & (target < total), 1.0, 0.0).astype(F32)
    return jnp.sum(taps[:, :, None] * reach[None], axis=1)


def per_device(estimate, raw, taps):
    views = raw.shape[0]
    planes, rows, cols = estimate.shape
    count = lax.axis_size("slab")
    assert rows >= taps.shape[2] // 2 and count % 2 == 0
    up = [(i, i + 1) for i in range(count - 1)]
    down = [(j, i) for i, j in up]

    slabs = neighbours(estimate, count)
    chunks = [(0, 2), (2, 2), (4, 2)]
    before, after = [], []
    for start, size in chunks:
        part = raw[start : start + size]
        before.append(lax.ppermute(part, "slab", up))
        after.append(lax.ppermute(part, "slab", down))

    wzs = tap_sums(taps[:, 0], 0, planes, planes)
    wy_sums = tap_sums(taps[:, 1], lax.axis_index("slab") * rows, rows, count * rows)
    wx_sums = tap_sums(taps[:, 2], 0, cols, cols)
    wyx = wy_sums[:, :, None] * wx_sums[:, None, :]
    totals = jnp.sum(raw, axis=(1, 2))
    weighted = jnp.sum(estimate[None] * wzs[:, :, None, None], axis=1)
    first_sums = jnp.sum(weighted * wyx, axis=1)

    forward_weights, (wy, wx, wz) = make_weights(taps, planes, rows, cols)
    adjoint_weights = (wy.reshape(views, rows, -1), wx, wz)

    current = estimate
    for iteration in range(ITERS):
        if iteration:
            slabs = neighbours(current, count)
        blurred = forward(slabs, forward_weights)
        acc = None
        for c, (start, size) in enumerate(chunks):
            acc, sums = adjoint(
                size, start, views, current, blurred, before[c], raw, after[c], adjoint_weights, acc, wzs, wyx
            )
        current = acc
        if iteration == 0:
            gathered = lax.psum(jnp.stack([first_sums, totals, sums]), "slab")
    whole = jnp.sum(gathered, axis=2)
    scale = jnp.log(whole[0] / whole[1]) + jnp.log(whole[2] / whole[1])
    return current * jnp.exp(jnp.mean(scale))


def solution(mesh):
    placed = (P("blocks", "slab", None), P(None, "blocks", "slab", None), P())
    return jax.shard_map(
        per_device, mesh=mesh, in_specs=placed, out_specs=P("blocks", "slab", None), check_vma=False
    )
```

```python
import functools

import jax
import jax.numpy as jnp
import numpy as np
from jax import lax
from jax.experimental import pallas as pl
from jax.experimental.pallas import tpu as pltpu
from jax.sharding import PartitionSpec as P

F32 = jnp.float32
BF16 = jnp.bfloat16
VMEM = pltpu.MemorySpace.VMEM
SMEM = pltpu.MemorySpace.SMEM
FULL = pl.BlockSpec(memory_space=VMEM)
LIMIT = 56 * 1024 * 1024


def split(value):
    high = value.astype(BF16)
    low = (value - high.astype(F32)).astype(BF16)
    return high, low


def dot(a, b):
    return jnp.dot(a, b, preferred_element_type=F32)


def placed_row(taps, lane_of_tap, width):
    count = taps.shape[1]
    tap = lax.broadcasted_iota(jnp.int32, (count, width), 0)
    lane = lax.broadcasted_iota(jnp.int32, (count, width), 1)
    onehot = jnp.where(lane == lane_of_tap(tap), 1.0, 0.0).astype(F32)
    return jnp.dot(taps, onehot, precision=lax.Precision.HIGHEST, preferred_element_type=F32)


def slanted(row, height):
    full = jnp.broadcast_to(row, (height, row.shape[1]))
    return pltpu.roll(full, 0, 1, stride=1, stride_axis=0)


def weights_kernel(rows, taps_ref, *outs):
    views, _, count = taps_ref.shape
    margin = count // 2
    for flip in (False, True):
        wy, wx, wz = outs[3 * flip : 3 * flip + 3]
        order = (lambda k: count - 1 - k) if flip else (lambda k: k)
        out_rows = rows if flip else 3 * rows
        in_rows = out_rows + 2 * rows
        planes = wz.shape[1] // 8
        cols = wx.shape[1] // 2
        row_y = placed_row(taps_ref[:, 1, :], lambda k: order(k) + rows - margin, 256)
        high = row_y.astype(BF16).astype(F32)
        low = row_y - high
        row_y = high + pltpu.roll(high, in_rows, 1) + pltpu.roll(low, 2 * in_rows, 1)
        row_x = placed_row(taps_ref[:, 2, :], lambda k: lax.rem(margin - order(k) + 2 * cols, 2 * cols), 2 * cols)
        width_z = 16 * planes
        row_z = placed_row(
            taps_ref[:, 0, :], lambda k: lax.rem(8 * (order(k) - margin) + width_z, width_z), width_z
        )
        for v in range(views):
            band = slanted(row_y[v : v + 1], out_rows)
            wy[v * out_rows : (v + 1) * out_rows, :] = band[:, : 3 * in_rows].astype(BF16)
            high, low = split(slanted(row_x[v : v + 1], cols)[:, :cols])
            wx[v, :cols, :cols] = high
            wx[v, cols:, :cols] = high
            wx[v, :cols, cols:] = low
            wx[v, cols:, cols:] = low
            size = 8 * planes
            high, low = split(slanted(row_z[v : v + 1], size)[:, :size])
            wz[v, :, :size] = high
            wz[v, :, size : 2 * size] = high
            wz[v, :, 2 * size :] = low


def make_weights(taps, planes, rows, cols):
    views = taps.shape[0]
    shapes = []
    for out_rows in (3 * rows, rows):
        shapes += [
            jax.ShapeDtypeStruct((views * out_rows, 3 * (out_rows + 2 * rows)), BF16),
            jax.ShapeDtypeStruct((views, 2 * cols, 2 * cols), BF16),
            jax.ShapeDtypeStruct((views, 8 * planes, 24 * planes), BF16),
        ]
    outs = pl.pallas_call(
        functools.partial(weights_kernel, rows),
        out_shape=shapes,
        in_specs=[FULL],
        out_specs=[FULL] * 6,
        compiler_params=pltpu.CompilerParams(vmem_limit_bytes=LIMIT),
        cost_estimate=pl.CostEstimate(flops=10**7, bytes_accessed=10**7, transcendentals=0),
        name="weights",
    )(taps)
    return outs[:3], outs[3:]


def stacked(pieces):
    columns = []
    for piece in pieces:
        high, low = split(piece)
        columns.append(jnp.concatenate([high, low, high], axis=0))
    return jnp.concatenate(columns, axis=1)


def two_groups(rows_ref, wx, wz, planes, cols):
    both = dot(rows_ref.reshape(planes * 16, 2 * cols), wx)
    value = (both[:, :cols] + both[:, cols:]).reshape(planes, 16, cols)
    return dot(wz, stacked([value[:, 8 * g : 8 * g + 8, :].reshape(planes * 8, cols) for g in range(2)]))


def forward_rows(parity, far_before, near, own, far_after, wy, ys):
    planes, rows, cols = own.shape
    views = ys.shape[0]
    height = 3 * rows
    side = parity[0]

    def plane(z):
        return jnp.concatenate(
            [far_before[z], near[1 - side, z], own[z], near[side, z], far_after[z]], axis=0
        )

    for z in range(0, planes, 2):
        result = dot(wy[...], stacked([plane(z), plane(z + 1)]))
        high, low = split(result)
        for j in range(2):
            for v in range(views):
                there = (slice(v * height, (v + 1) * height), slice(j * cols, (j + 1) * cols))
                ys[v, z + j, :, :cols] = high[there]
                ys[v, z + j, :, cols:] = low[there]


def forward_view(view, ys, wx, wz, out):
    planes, height, cols = out.shape
    for pair in range(height // 16):
        result = two_groups(ys[view, :, 16 * pair : 16 * pair + 16, :], wx, wz, planes, cols)
        for j in range(2):
            at = 16 * pair + 8 * j
            out[:, at : at + 8, :] = result[:, j * cols : (j + 1) * cols].reshape(planes, 8, cols)


def adjoint_view(blurred, before, raw, after, wy, wx, wz, ya, acc):
    planes, rows, cols = raw.shape

    def quotient(z):
        counts = jnp.concatenate([before[z], raw[z], after[z]], axis=0)
        inside = counts > 0.0
        return jnp.where(inside, counts / jnp.where(inside, blurred[z], 1.0), 0.0)

    for z in range(0, planes, 2):
        high, low = split(dot(wy, stacked([quotient(z), quotient(z + 1)])))
        for j in range(2):
            ya[z + j, :, :cols] = high[:, j * cols : (j + 1) * cols]
            ya[z + j, :, cols:] = low[:, j * cols : (j + 1) * cols]
    for pair in range(rows // 16):
        result = two_groups(ya[:, 16 * pair : 16 * pair + 16, :], wx, wz, planes, cols)
        for j in range(2):
            at = 16 * pair + 8 * j
            acc[:, at : at + 8, :] += jnp.log(result[:, j * cols : (j + 1) * cols]).reshape(planes, 8, cols)


def forward_kernel(parity, far_before, near, own, far_after, wy, wx, wz, out, ys):
    @pl.when(pl.program_id(0) == 0)
    def _():
        forward_rows(parity, far_before, near, own, far_after, wy, ys)

    forward_view(pl.program_id(0), ys, wx[0], wz[0], out.at[0])


def weighted_sums(values, wzs, wyx, sums, at):
    planes, rows, cols = values.shape
    for v in range(wyx.shape[0]):
        total = jnp.zeros((rows, cols), F32)
        for z in range(planes):
            total = total + wzs[v, z] * values[z]
        sums[at + v : at + v + 1, :] = jnp.sum(total * wyx[v], axis=0, keepdims=True)


def first_adjoint_kernel(current, blurred, before, raw, after, wy, wx, wz, wzs, wyx, out, sums, ya, acc):
    view, views = pl.program_id(0), wyx.shape[0]

    @pl.when(view == 0)
    def _():
        acc[...] = jnp.zeros_like(acc)

    sums[pl.ds(view, 1), :] = jnp.sum(jnp.sum(raw[0], axis=0), axis=0, keepdims=True)
    adjoint_view(blurred.at[0], before.at[0], raw.at[0], after.at[0], wy[0], wx[0], wz[0], ya, acc)

    @pl.when(view == views - 1)
    def _():
        out[...] = current[...] * jnp.exp(acc[...] * (1.0 / views))
        weighted_sums(current, wzs, wyx, sums, views)
        weighted_sums(out, wzs, wyx, sums, 2 * views)


def iteration_kernel(
    parity, far_before, near, own, far_after, before, raw, after, wy, wx, wz, wya, wxa, wza, out, ys, blurred, ya, acc
):
    view = pl.program_id(0)

    @pl.when(view == 0)
    def _():
        acc[...] = jnp.zeros_like(acc)
        forward_rows(parity, far_before, near, own, far_after, wy, ys)

    forward_view(view, ys, wx[0], wz[0], blurred)
    adjoint_view(blurred, before.at[0], raw.at[0], after.at[0], wya[0], wxa[0], wza[0], ya, acc)

    @pl.when(view == pl.num_programs(0) - 1)
    def _():
        out[...] = own[...] * jnp.exp(acc[...] * (1.0 / ys.shape[0]))


def whole(array):
    return pl.BlockSpec(array.shape, lambda v: (0,) * array.ndim)


def one_view(array):
    return pl.BlockSpec((1,) + array.shape[1:], lambda v: (v,) + (0,) * (array.ndim - 1))


def params(flops, moved):
    return dict(
        compiler_params=pltpu.CompilerParams(vmem_limit_bytes=LIMIT),
        cost_estimate=pl.CostEstimate(flops=flops, bytes_accessed=moved, transcendentals=10**5),
    )


def row_scratch(views, planes, rows, cols):
    return pltpu.VMEM((views, planes, 3 * rows, 2 * cols), BF16)


def adjoint_scratch(planes, rows, cols):
    return [pltpu.VMEM((planes, rows, 2 * cols), BF16), pltpu.VMEM((planes, rows, cols), F32)]


def forward(parity, slabs, weights):
    planes, rows, cols = slabs[0].shape
    wy, wx, wz = weights
    views = wx.shape[0]
    out = jax.ShapeDtypeStruct((views, planes, 3 * rows, cols), F32)
    return pl.pallas_call(
        forward_kernel,
        grid=(views,),
        out_shape=out,
        in_specs=[pl.BlockSpec(memory_space=SMEM)]
        + [whole(s) for s in slabs]
        + [whole(wy), one_view(wx), one_view(wz)],
        out_specs=one_view(out),
        scratch_shapes=[row_scratch(views, planes, rows, cols)],
        name="forward",
        **params(10**10, 10**7),
    )(parity, *slabs, *weights)


def first_adjoint(current, blurred, before, raw, after, weights, wzs, wyx):
    wy, wx, wz = weights
    views = raw.shape[0]
    shapes = [jax.ShapeDtypeStruct(current.shape, F32), jax.ShapeDtypeStruct((3 * views, current.shape[2]), F32)]
    return pl.pallas_call(
        first_adjoint_kernel,
        grid=(views,),
        out_shape=shapes,
        in_specs=[whole(current)]
        + [one_view(a) for a in (blurred, before, raw, after, wy, wx, wz)]
        + [pl.BlockSpec(memory_space=SMEM), whole(wyx)],
        out_specs=[whole(s) for s in shapes],
        scratch_shapes=adjoint_scratch(*current.shape),
        name="adjoint",
        **params(10**10, 10**7),
    )(current, blurred, before, raw, after, wy, wx, wz, wzs, wyx)


def full_iteration(parity, slabs, before, raw, after, weights, adjoint_weights):
    current = slabs[2]
    planes, rows, cols = current.shape
    views = raw.shape[0]
    wy, wx, wz = weights
    return pl.pallas_call(
        iteration_kernel,
        grid=(views,),
        out_shape=jax.ShapeDtypeStruct(current.shape, F32),
        in_specs=[pl.BlockSpec(memory_space=SMEM)]
        + [whole(s) for s in slabs]
        + [one_view(a) for a in (before, raw, after)]
        + [whole(wy), one_view(wx), one_view(wz)]
        + [one_view(a) for a in adjoint_weights],
        out_specs=whole(current),
        scratch_shapes=[
            row_scratch(views, planes, rows, cols),
            pltpu.VMEM((planes, 3 * rows, cols), F32),
        ]
        + adjoint_scratch(planes, rows, cols),
        name="iteration",
        **params(2 * 10**10, 2 * 10**7),
    )(parity, *slabs, before, raw, after, *weights, *adjoint_weights)


def two_slabs_away(value, count):
    up = [(i, i + 2) for i in range(count - 2)]
    down = [(j, i) for i, j in up]
    return lax.ppermute(value, "slab", up), lax.ppermute(value, "slab", down)


def with_near(value, far_before, far_after, parity, count):
    swap = [(i, i + 1 - 2 * (i % 2)) for i in range(count)]
    passed = jnp.stack([value, jnp.where(parity[0] == 0, far_after, far_before)])
    near = lax.ppermute(passed, "slab", swap)
    return far_before, near, value, far_after


def tap_sums(taps, offset, extent, total):
    count = taps.shape[1]
    target = offset + jnp.arange(extent)[None, :] - jnp.arange(count)[:, None] + count // 2
    reach = jnp.where((target >= 0) & (target < total), 1.0, 0.0).astype(F32)
    return jnp.sum(taps[:, :, None] * reach[None], axis=1)


def per_device(estimate, raw, taps):
    views = raw.shape[0]
    planes, rows, cols = estimate.shape
    count = lax.axis_size("slab")
    assert rows >= taps.shape[2] // 2 and count % 2 == 0
    up = [(i, i + 1) for i in range(count - 1)]
    down = [(j, i) for i, j in up]
    place = lax.axis_index("slab")
    parity = (place % 2).reshape(1)

    far = two_slabs_away(estimate, count)
    before = lax.ppermute(raw, "slab", up)
    after = lax.ppermute(raw, "slab", down)

    wzs = tap_sums(taps[:, 0], 0, planes, planes)
    wy_sums = tap_sums(taps[:, 1], place * rows, rows, count * rows)
    wx_sums = tap_sums(taps[:, 2], 0, cols, cols)
    wyx = wy_sums[:, :, None] * wx_sums[:, None, :]

    forward_weights, (wy, wx, wz) = make_weights(taps, planes, rows, cols)
    adjoint_weights = (wy.reshape(views, rows, -1), wx, wz)

    slabs = with_near(estimate, *far, parity, count)
    blurred = forward(parity, slabs, forward_weights)
    current, sums = first_adjoint(estimate, blurred, before, raw, after, adjoint_weights, wzs, wyx)
    gathered = lax.all_gather(sums, "slab", tiled=True)

    slabs = with_near(current, *two_slabs_away(current, count), parity, count)
    current = full_iteration(parity, slabs, before, raw, after, forward_weights, adjoint_weights)

    current, gathered = lax.optimization_barrier((current, gathered))
    total, first, second = jnp.sum(gathered.reshape(count, 3, views, cols), axis=(0, 3))
    scale = jnp.log(first / total) + jnp.log(second / total)
    return current * jnp.exp(jnp.mean(scale))


def solution(mesh):
    placed = (P("blocks", "slab", None), P(None, "blocks", "slab", None), P())
    return jax.shard_map(
        per_device, mesh=mesh, in_specs=placed, out_specs=P("blocks", "slab", None), check_vma=False
    )
```

```python
import functools

import jax
import jax.numpy as jnp
import numpy as np
from jax import lax
from jax.experimental import pallas as pl
from jax.experimental.pallas import tpu as pltpu
from jax.sharding import PartitionSpec as P

F32 = jnp.float32
BF16 = jnp.bfloat16
VMEM = pltpu.MemorySpace.VMEM
SMEM = pltpu.MemorySpace.SMEM
FULL = pl.BlockSpec(memory_space=VMEM)
LIMIT = 24 * 1024 * 1024
TINY = float(np.finfo(np.float32).tiny)


def split(value):
    high = value.astype(BF16)
    low = (value - high.astype(F32)).astype(BF16)
    return high, low


def dot(a, b):
    return jnp.dot(a, b, preferred_element_type=F32)


def placed_row(taps, lane_of_tap, width):
    count = taps.shape[1]
    tap = lax.broadcasted_iota(jnp.int32, (count, width), 0)
    lane = lax.broadcasted_iota(jnp.int32, (count, width), 1)
    onehot = jnp.where(lane == lane_of_tap(tap), 1.0, 0.0).astype(F32)
    return jnp.dot(taps, onehot, precision=lax.Precision.HIGHEST, preferred_element_type=F32)


def slanted(row, height):
    full = jnp.broadcast_to(row, (height, row.shape[1]))
    return pltpu.roll(full, 0, 1, stride=1, stride_axis=0)


def weights_kernel(rows, taps_ref, *outs):
    views, _, count = taps_ref.shape
    margin = count // 2
    for flip in (False, True):
        wy, wx, wz = outs[3 * flip : 3 * flip + 3]
        order = (lambda k: count - 1 - k) if flip else (lambda k: k)
        out_rows = rows if flip else 3 * rows
        in_rows = out_rows + 2 * rows
        planes = wz.shape[1] // 8
        cols = wx.shape[1] // 2
        row_y = placed_row(taps_ref[:, 1, :], lambda k: order(k) + rows - margin, 256)
        high = row_y.astype(BF16).astype(F32)
        low = row_y - high
        row_y = high + pltpu.roll(high, in_rows, 1) + pltpu.roll(low, 2 * in_rows, 1)
        row_x = placed_row(taps_ref[:, 2, :], lambda k: lax.rem(margin - order(k) + 2 * cols, 2 * cols), 2 * cols)
        width_z = 16 * planes
        row_z = placed_row(
            taps_ref[:, 0, :], lambda k: lax.rem(8 * (order(k) - margin) + width_z, width_z), width_z
        )
        for v in range(views):
            band = slanted(row_y[v : v + 1], out_rows)
            wy[v * out_rows : (v + 1) * out_rows, :] = band[:, : 3 * in_rows].astype(BF16)
            high, low = split(slanted(row_x[v : v + 1], cols)[:, :cols])
            wx[v, :cols, :cols] = high
            wx[v, cols:, :cols] = high
            wx[v, :cols, cols:] = low
            wx[v, cols:, cols:] = low
            size = 8 * planes
            high, low = split(slanted(row_z[v : v + 1], size)[:, :size])
            wz[v, :, :size] = high
            wz[v, :, size : 2 * size] = high
            wz[v, :, 2 * size :] = low


def make_weights(taps, planes, rows, cols):
    views = taps.shape[0]
    shapes = []
    for out_rows in (3 * rows, rows):
        shapes += [
            jax.ShapeDtypeStruct((views * out_rows, 3 * (out_rows + 2 * rows)), BF16),
            jax.ShapeDtypeStruct((views, 2 * cols, 2 * cols), BF16),
            jax.ShapeDtypeStruct((views, 8 * planes, 24 * planes), BF16),
        ]
    outs = pl.pallas_call(
        functools.partial(weights_kernel, rows),
        out_shape=shapes,
        in_specs=[FULL],
        out_specs=[FULL] * 6,
        compiler_params=pltpu.CompilerParams(vmem_limit_bytes=LIMIT),
        cost_estimate=pl.CostEstimate(flops=10**7, bytes_accessed=10**7, transcendentals=0),
        name="weights",
    )(taps)
    return outs[:3], outs[3:]


def stacked(pieces):
    columns = []
    for piece in pieces:
        high, low = split(piece)
        columns.append(jnp.concatenate([high, low, high], axis=0))
    return jnp.concatenate(columns, axis=1)


def two_groups(rows_ref, wx, wz, planes, cols):
    both = dot(rows_ref.reshape(planes * 16, 2 * cols), wx)
    value = (both[:, :cols] + both[:, cols:]).reshape(planes, 16, cols)
    return dot(wz, stacked([value[:, 8 * g : 8 * g + 8, :].reshape(planes * 8, cols) for g in range(2)]))


def forward_rows(parity, far_before, near, own, far_after, wy, ys):
    planes, rows, cols = own.shape
    views = ys.shape[0]
    height = 3 * rows
    side = parity[0]

    def plane(z):
        return jnp.concatenate(
            [far_before[z], near[1 - side, z], own[z], near[side, z], far_after[z]], axis=0
        )

    for z in range(0, planes, 2):
        result = dot(wy[...], stacked([plane(z), plane(z + 1)]))
        high, low = split(result)
        for j in range(2):
            for v in range(views):
                there = (slice(v * height, (v + 1) * height), slice(j * cols, (j + 1) * cols))
                ys[v, z + j, :, :cols] = high[there]
                ys[v, z + j, :, cols:] = low[there]


def forward_view(view, ys, wx, wz, out):
    planes, height, cols = out.shape
    for pair in range(height // 16):
        result = two_groups(ys[view, :, 16 * pair : 16 * pair + 16, :], wx, wz, planes, cols)
        for j in range(2):
            at = 16 * pair + 8 * j
            out[:, at : at + 8, :] = result[:, j * cols : (j + 1) * cols].reshape(planes, 8, cols)


def adjoint_view(blurred, before, raw, after, wy, wx, wz, ya, acc):
    planes, rows, cols = raw.shape

    def quotient(z):
        counts = jnp.concatenate([before[z], raw[z], after[z]], axis=0)
        below = jnp.maximum(blurred[z], TINY)
        inverse = pl.reciprocal(below, approx=True)
        return counts * (inverse * (2.0 - below * inverse))

    for z in range(0, planes, 2):
        high, low = split(dot(wy, stacked([quotient(z), quotient(z + 1)])))
        for j in range(2):
            ya[z + j, :, :cols] = high[:, j * cols : (j + 1) * cols]
            ya[z + j, :, cols:] = low[:, j * cols : (j + 1) * cols]
    for pair in range(rows // 16):
        result = two_groups(ya[:, 16 * pair : 16 * pair + 16, :], wx, wz, planes, cols)
        for j in range(2):
            at = 16 * pair + 8 * j
            acc[:, at : at + 8, :] += jnp.log(result[:, j * cols : (j + 1) * cols]).reshape(planes, 8, cols)


def forward_kernel(parity, far_before, near, own, far_after, wy, wx, wz, out, ys):
    @pl.when(pl.program_id(0) == 0)
    def _():
        forward_rows(parity, far_before, near, own, far_after, wy, ys)

    forward_view(pl.program_id(0), ys, wx[0], wz[0], out.at[0])


def weighted_sums(values, wzs, wyx, sums, at):
    planes, rows, cols = values.shape
    for v in range(wyx.shape[0]):
        total = jnp.zeros((rows, cols), F32)
        for z in range(planes):
            total = total + wzs[v, z] * values[z]
        sums[at + v : at + v + 1, :] = jnp.sum(total * wyx[v], axis=0, keepdims=True)


def first_adjoint_kernel(current, blurred, before, raw, after, wy, wx, wz, wzs, wyx, out, sums, ya, acc):
    view, views = pl.program_id(0), wyx.shape[0]

    @pl.when(view == 0)
    def _():
        acc[...] = jnp.zeros_like(acc)

    sums[pl.ds(view, 1), :] = jnp.sum(jnp.sum(raw[0], axis=0), axis=0, keepdims=True)
    adjoint_view(blurred.at[0], before.at[0], raw.at[0], after.at[0], wy[0], wx[0], wz[0], ya, acc)

    @pl.when(view == views - 1)
    def _():
        out[...] = current[...] * jnp.exp(acc[...] * (1.0 / views))
        weighted_sums(current, wzs, wyx, sums, views)
        weighted_sums(out, wzs, wyx, sums, 2 * views)


def iteration_kernel(
    parity, far_before, near, own, far_after, before, raw, after, wy, wx, wz, wya, wxa, wza, out, ys, blurred, ya, acc
):
    view = pl.program_id(0)

    @pl.when(view == 0)
    def _():
        acc[...] = jnp.zeros_like(acc)
        forward_rows(parity, far_before, near, own, far_after, wy, ys)

    forward_view(view, ys, wx[0], wz[0], blurred)
    adjoint_view(blurred, before.at[0], raw.at[0], after.at[0], wya[0], wxa[0], wza[0], ya, acc)

    @pl.when(view == pl.num_programs(0) - 1)
    def _():
        out[...] = own[...] * jnp.exp(acc[...] * (1.0 / ys.shape[0]))


def whole(array):
    return pl.BlockSpec(array.shape, lambda v: (0,) * array.ndim)


def one_view(array):
    return pl.BlockSpec((1,) + array.shape[1:], lambda v: (v,) + (0,) * (array.ndim - 1))


def params(flops, moved):
    return dict(
        compiler_params=pltpu.CompilerParams(vmem_limit_bytes=LIMIT),
        cost_estimate=pl.CostEstimate(flops=flops, bytes_accessed=moved, transcendentals=10**5),
    )


def row_scratch(views, planes, rows, cols):
    return pltpu.VMEM((views, planes, 3 * rows, 2 * cols), BF16)


def adjoint_scratch(planes, rows, cols):
    return [pltpu.VMEM((planes, rows, 2 * cols), BF16), pltpu.VMEM((planes, rows, cols), F32)]


def forward(parity, slabs, weights):
    planes, rows, cols = slabs[0].shape
    wy, wx, wz = weights
    views = wx.shape[0]
    out = jax.ShapeDtypeStruct((views, planes, 3 * rows, cols), F32)
    return pl.pallas_call(
        forward_kernel,
        grid=(views,),
        out_shape=out,
        in_specs=[pl.BlockSpec(memory_space=SMEM)]
        + [whole(s) for s in slabs]
        + [whole(wy), one_view(wx), one_view(wz)],
        out_specs=one_view(out),
        scratch_shapes=[row_scratch(views, planes, rows, cols)],
        name="forward",
        **params(10**10, 10**7),
    )(parity, *slabs, *weights)


def first_adjoint(current, blurred, before, raw, after, weights, wzs, wyx):
    wy, wx, wz = weights
    views = raw.shape[0]
    shapes = [jax.ShapeDtypeStruct(current.shape, F32), jax.ShapeDtypeStruct((3 * views, current.shape[2]), F32)]
    return pl.pallas_call(
        first_adjoint_kernel,
        grid=(views,),
        out_shape=shapes,
        in_specs=[whole(current)]
        + [one_view(a) for a in (blurred, before, raw, after, wy, wx, wz)]
        + [pl.BlockSpec(memory_space=SMEM), whole(wyx)],
        out_specs=[whole(s) for s in shapes],
        scratch_shapes=adjoint_scratch(*current.shape),
        name="adjoint",
        **params(10**10, 10**7),
    )(current, blurred, before, raw, after, wy, wx, wz, wzs, wyx)


def full_iteration(parity, slabs, before, raw, after, weights, adjoint_weights):
    current = slabs[2]
    planes, rows, cols = current.shape
    views = raw.shape[0]
    wy, wx, wz = weights
    return pl.pallas_call(
        iteration_kernel,
        grid=(views,),
        out_shape=jax.ShapeDtypeStruct(current.shape, F32),
        in_specs=[pl.BlockSpec(memory_space=SMEM)]
        + [whole(s) for s in slabs]
        + [one_view(a) for a in (before, raw, after)]
        + [whole(wy), one_view(wx), one_view(wz)]
        + [one_view(a) for a in adjoint_weights],
        out_specs=whole(current),
        scratch_shapes=[
            row_scratch(views, planes, rows, cols),
            pltpu.VMEM((planes, 3 * rows, cols), F32),
        ]
        + adjoint_scratch(planes, rows, cols),
        name="iteration",
        **params(2 * 10**10, 2 * 10**7),
    )(parity, *slabs, before, raw, after, *weights, *adjoint_weights)


def two_slabs_away(value, count):
    up = [(i, i + 2) for i in range(count - 2)]
    down = [(j, i) for i, j in up]
    return lax.ppermute(value, "slab", up), lax.ppermute(value, "slab", down)


def with_near(value, far_before, far_after, parity, count):
    swap = [(i, i + 1 - 2 * (i % 2)) for i in range(count)]
    passed = jnp.stack([value, jnp.where(parity[0] == 0, far_after, far_before)])
    near = lax.ppermute(passed, "slab", swap)
    return far_before, near, value, far_after


def tap_sums(taps, offset, extent, total):
    count = taps.shape[1]
    target = offset + jnp.arange(extent)[None, :] - jnp.arange(count)[:, None] + count // 2
    reach = jnp.where((target >= 0) & (target < total), 1.0, 0.0).astype(F32)
    return jnp.sum(taps[:, :, None] * reach[None], axis=1)


def per_device(estimate, raw, taps):
    views = raw.shape[0]
    planes, rows, cols = estimate.shape
    count = lax.axis_size("slab")
    assert rows >= taps.shape[2] // 2 and count & (count - 1) == 0
    up = [(i, i + 1) for i in range(count - 1)]
    down = [(j, i) for i, j in up]
    place = lax.axis_index("slab")
    parity = (place % 2).reshape(1)

    far = two_slabs_away(estimate, count)
    before = lax.ppermute(raw, "slab", up)
    after = lax.ppermute(raw, "slab", down)

    wzs = tap_sums(taps[:, 0], 0, planes, planes)
    wy_sums = tap_sums(taps[:, 1], place * rows, rows, count * rows)
    wx_sums = tap_sums(taps[:, 2], 0, cols, cols)
    wyx = wy_sums[:, :, None] * wx_sums[:, None, :]

    forward_weights, (wy, wx, wz) = make_weights(taps, planes, rows, cols)
    adjoint_weights = (wy.reshape(views, rows, -1), wx, wz)

    slabs = with_near(estimate, *far, parity, count)
    blurred = forward(parity, slabs, forward_weights)
    current, sums = first_adjoint(estimate, blurred, before, raw, after, adjoint_weights, wzs, wyx)

    far = two_slabs_away(current, count)
    sums, others, distance = sums, None, 1
    while distance < count:
        sums = sums if others is None else sums + others
        others = lax.ppermute(sums, "slab", [(i, i ^ distance) for i in range(count)])
        distance *= 2
        if distance == 8:
            *far, sums, others = lax.optimization_barrier((*far, sums, others))
    slabs = with_near(current, *far, parity, count)
    current = full_iteration(parity, slabs, before, raw, after, forward_weights, adjoint_weights)

    current, sums, others = lax.optimization_barrier((current, sums, others))
    total, first, second = jnp.sum((sums + others).reshape(3, views, cols), axis=2)
    scale = jnp.log(first / total) + jnp.log(second / total)
    return current * jnp.exp(jnp.mean(scale))


def solution(mesh):
    placed = (P("blocks", "slab", None), P(None, "blocks", "slab", None), P())
    return jax.shard_map(
        per_device, mesh=mesh, in_specs=placed, out_specs=P("blocks", "slab", None), check_vma=False
    )
```

```python
import functools

import jax
import jax.numpy as jnp
import numpy as np
from jax import lax
from jax.experimental import pallas as pl
from jax.experimental.pallas import tpu as pltpu
from jax.sharding import PartitionSpec as P

F32 = jnp.float32
BF16 = jnp.bfloat16
VMEM = pltpu.MemorySpace.VMEM
SMEM = pltpu.MemorySpace.SMEM
FULL = pl.BlockSpec(memory_space=VMEM)
LIMIT = 30 * 1024 * 1024
STEP = 2
TINY = float(np.finfo(np.float32).tiny)


def split(value):
    high = value.astype(BF16)
    low = (value - high.astype(F32)).astype(BF16)
    return high, low


def dot(a, b):
    return jnp.dot(a, b, preferred_element_type=F32)


def placed_row(taps, lane_of_tap, width):
    count = taps.shape[1]
    tap = lax.broadcasted_iota(jnp.int32, (count, width), 0)
    lane = lax.broadcasted_iota(jnp.int32, (count, width), 1)
    onehot = jnp.where(lane == lane_of_tap(tap), 1.0, 0.0).astype(F32)
    return jnp.dot(taps, onehot, precision=lax.Precision.HIGHEST, preferred_element_type=F32)


def slanted(row, height):
    full = jnp.broadcast_to(row, (height, row.shape[1]))
    return pltpu.roll(full, 0, 1, stride=1, stride_axis=0)


def weights_kernel(rows, taps_ref, *outs):
    views, _, count = taps_ref.shape
    margin = count // 2
    for flip in (False, True):
        wy, wx, wz = outs[3 * flip : 3 * flip + 3]
        order = (lambda k: count - 1 - k) if flip else (lambda k: k)
        out_rows = rows if flip else 3 * rows
        in_rows = out_rows + 2 * rows
        planes = wz.shape[1] // 8
        cols = wx.shape[1] // 2
        row_y = placed_row(taps_ref[:, 1, :], lambda k: order(k) + rows - margin, 256)
        high = row_y.astype(BF16).astype(F32)
        low = row_y - high
        if flip:
            row_y = [part + pltpu.roll(part, in_rows, 1) for part in (high, low)]
        else:
            row_y = high + pltpu.roll(high, in_rows, 1) + pltpu.roll(low, 2 * in_rows, 1)
        row_x = placed_row(taps_ref[:, 2, :], lambda k: lax.rem(margin - order(k) + 2 * cols, 2 * cols), 2 * cols)
        width_z = 16 * planes
        row_z = placed_row(
            taps_ref[:, 0, :], lambda k: lax.rem(8 * (order(k) - margin) + width_z, width_z), width_z
        )
        for v in range(views):
            if flip:
                for j, row in enumerate(row_y):
                    wy[v, j * rows : (j + 1) * rows, :] = slanted(row[v : v + 1], rows)[:, : 2 * in_rows].astype(BF16)
            else:
                band = slanted(row_y[v : v + 1], out_rows)
                wy[v * out_rows : (v + 1) * out_rows, :] = band[:, : 3 * in_rows].astype(BF16)
            high, low = split(slanted(row_x[v : v + 1], cols)[:, :cols])
            wx[v, :cols, :cols] = high
            wx[v, cols:, :cols] = high
            wx[v, :cols, cols:] = low
            wx[v, cols:, cols:] = low
            size = 8 * planes
            high, low = split(slanted(row_z[v : v + 1], size)[:, :size])
            wz[v, :, :size] = high
            wz[v, :, size : 2 * size] = high
            wz[v, :, 2 * size :] = low


def make_weights(taps, planes, rows, cols):
    views = taps.shape[0]
    shapes = []
    for row_weights in ((views * 3 * rows, 15 * rows), (views, 2 * rows, 6 * rows)):
        shapes += [
            jax.ShapeDtypeStruct(row_weights, BF16),
            jax.ShapeDtypeStruct((views, 2 * cols, 2 * cols), BF16),
            jax.ShapeDtypeStruct((views, 8 * planes, 24 * planes), BF16),
        ]
    outs = pl.pallas_call(
        functools.partial(weights_kernel, rows),
        out_shape=shapes,
        in_specs=[FULL],
        out_specs=[FULL] * 6,
        compiler_params=pltpu.CompilerParams(vmem_limit_bytes=LIMIT),
        cost_estimate=pl.CostEstimate(flops=10**7, bytes_accessed=10**7, transcendentals=0),
        name="weights",
    )(taps)
    return outs[:3], outs[3:]


def stacked(pieces):
    columns = []
    for piece in pieces:
        high, low = split(piece)
        columns.append(jnp.concatenate([high, low, high], axis=0))
    return jnp.concatenate(columns, axis=1)


def two_groups(rows_ref, wx, wz, planes, cols):
    both = dot(rows_ref.reshape(planes * 16, 2 * cols), wx)
    value = (both[:, :cols] + both[:, cols:]).reshape(planes, 16, cols)
    return dot(wz, stacked([value[:, 8 * g : 8 * g + 8, :].reshape(planes * 8, cols) for g in range(2)]))


def forward_rows(parity, far_before, near, own, far_after, wy, ys):
    planes, rows, cols = own.shape
    views = ys.shape[0]
    height = 3 * rows
    side = parity[0]

    def plane(z):
        return jnp.concatenate(
            [far_before[z], near[1 - side, z], own[z], near[side, z], far_after[z]], axis=0
        )

    for z in range(0, planes, 2):
        result = dot(wy[...], stacked([plane(z), plane(z + 1)]))
        high, low = split(result)
        for j in range(2):
            for v in range(views):
                there = (slice(v * height, (v + 1) * height), slice(j * cols, (j + 1) * cols))
                ys[v, z + j, :, :cols] = high[there]
                ys[v, z + j, :, cols:] = low[there]


def forward_view(view, ys, wx, wz, out):
    planes, height, cols = out.shape
    for pair in range(height // 16):
        result = two_groups(ys[view, :, 16 * pair : 16 * pair + 16, :], wx, wz, planes, cols)
        for j in range(2):
            at = 16 * pair + 8 * j
            out[:, at : at + 8, :] = result[:, j * cols : (j + 1) * cols].reshape(planes, 8, cols)


def adjoint_views(blurred, before, raw, after, wy, wx, wz, ya, acc):
    _, planes, rows, cols = raw.shape

    def quotient(v, z):
        counts = jnp.concatenate([before[v, z], raw[v, z], after[v, z]], axis=0)
        below = jnp.maximum(blurred[v, z], TINY)
        inverse = pl.reciprocal(below, approx=True)
        return counts * (inverse * (2.0 - below * inverse))

    for v in range(STEP):
        for z in range(0, planes, 2):
            high, low = split(jnp.concatenate([quotient(v, z), quotient(v, z + 1)], axis=1))
            both = dot(wy[v], jnp.concatenate([high, low], axis=0))
            high, low = split(both[:rows] + both[rows:])
            for j in range(2):
                ya[v, z + j, :, :cols] = high[:, j * cols : (j + 1) * cols]
                ya[v, z + j, :, cols:] = low[:, j * cols : (j + 1) * cols]
    for pair in range(rows // 16):
        chosen = slice(16 * pair, 16 * pair + 16)
        logs = 0.0
        for v in range(STEP):
            logs = logs + jnp.log(two_groups(ya[v, :, chosen, :], wx[v], wz[v], planes, cols))
        for j in range(2):
            at = 16 * pair + 8 * j
            acc[:, at : at + 8, :] += logs[:, j * cols : (j + 1) * cols].reshape(planes, 8, cols)


def forward_kernel(parity, far_before, near, own, far_after, wy, wx, wz, out, ys):
    @pl.when(pl.program_id(0) == 0)
    def _():
        forward_rows(parity, far_before, near, own, far_after, wy, ys)

    for v in range(STEP):
        forward_view(STEP * pl.program_id(0) + v, ys, wx[v], wz[v], out.at[v])


def weighted_sums(values, wzs, wyx, sums, at):
    planes, rows, cols = values.shape
    for v in range(wyx.shape[0]):
        total = jnp.zeros((rows, cols), F32)
        for z in range(planes):
            total = total + wzs[v, z] * values[z]
        sums[at + v : at + v + 1, :] = jnp.sum(total * wyx[v], axis=0, keepdims=True)


def first_adjoint_kernel(current, blurred, before, raw, after, wy, wx, wz, wzs, wyx, out, sums, ya, acc):
    step, views = pl.program_id(0), wyx.shape[0]

    @pl.when(step == 0)
    def _():
        acc[...] = jnp.zeros_like(acc)
        sums[...] = jnp.zeros_like(sums)

    for v in range(STEP):
        total = jnp.sum(jnp.sum(raw[v], axis=0), axis=0, keepdims=True)
        sums[pl.ds(STEP * step + v, 1), :] = total
    adjoint_views(blurred, before, raw, after, wy, wx, wz, ya, acc)

    @pl.when(step == pl.num_programs(0) - 1)
    def _():
        out[...] = current[...] * jnp.exp(acc[...] * (1.0 / views))
        weighted_sums(current, wzs, wyx, sums, sums.shape[0] // 3)
        weighted_sums(out, wzs, wyx, sums, 2 * sums.shape[0] // 3)


def iteration_kernel(
    parity, far_before, near, own, far_after, before, raw, after, wy, wx, wz, wya, wxa, wza, part, rest,
    out, ys, blurred, ya, acc,
):
    step, views = pl.program_id(0), ys.shape[0]

    @pl.when(step == 0)
    def _():
        acc[...] = jnp.zeros_like(acc)
        forward_rows(parity, far_before, near, own, far_after, wy, ys)

    for v in range(STEP):
        forward_view(STEP * step + v, ys, wx[v], wz[v], blurred.at[v])
    adjoint_views(blurred, before, raw, after, wya, wxa, wza, ya, acc)

    @pl.when(step == pl.num_programs(0) - 1)
    def _():
        sums = jnp.sum(part[...] + rest[...], axis=1, keepdims=True)
        space = sums.shape[0] // 3
        total, first, second = (sums[i * space : i * space + views] for i in range(3))
        scale = jnp.sum(jnp.log(first / total) + jnp.log(second / total), axis=0, keepdims=True)
        out[...] = own[...] * jnp.exp((acc[...] + scale[None]) * (1.0 / views))


def whole(array):
    return pl.BlockSpec(array.shape, lambda v: (0,) * array.ndim)


def step_views(array):
    return pl.BlockSpec((STEP,) + array.shape[1:], lambda v: (v,) + (0,) * (array.ndim - 1))


def params(flops, moved):
    return dict(
        compiler_params=pltpu.CompilerParams(vmem_limit_bytes=LIMIT),
        cost_estimate=pl.CostEstimate(flops=flops, bytes_accessed=moved, transcendentals=10**5),
    )


def row_scratch(views, planes, rows, cols):
    return pltpu.VMEM((views, planes, 3 * rows, 2 * cols), BF16)


def adjoint_scratch(planes, rows, cols):
    return [pltpu.VMEM((STEP, planes, rows, 2 * cols), BF16), pltpu.VMEM((planes, rows, cols), F32)]


def forward(parity, slabs, weights):
    planes, rows, cols = slabs[0].shape
    wy, wx, wz = weights
    views = wx.shape[0]
    out = jax.ShapeDtypeStruct((views, planes, 3 * rows, cols), F32)
    return pl.pallas_call(
        forward_kernel,
        grid=(views // STEP,),
        out_shape=out,
        in_specs=[pl.BlockSpec(memory_space=SMEM)]
        + [whole(s) for s in slabs]
        + [whole(wy), step_views(wx), step_views(wz)],
        out_specs=step_views(out),
        scratch_shapes=[row_scratch(views, planes, rows, cols)],
        name="forward",
        **params(10**10, 10**7),
    )(parity, *slabs, *weights)


def first_adjoint(current, blurred, before, raw, after, weights, wzs, wyx):
    wy, wx, wz = weights
    views = raw.shape[0]
    shapes = [jax.ShapeDtypeStruct(current.shape, F32), jax.ShapeDtypeStruct((24 * -(-views // 8), current.shape[2]), F32)]
    return pl.pallas_call(
        first_adjoint_kernel,
        grid=(views // STEP,),
        out_shape=shapes,
        in_specs=[whole(current)]
        + [step_views(a) for a in (blurred, before, raw, after, wy, wx, wz)]
        + [pl.BlockSpec(memory_space=SMEM), whole(wyx)],
        out_specs=[whole(s) for s in shapes],
        scratch_shapes=adjoint_scratch(*current.shape),
        name="adjoint",
        **params(10**10, 10**7),
    )(current, blurred, before, raw, after, wy, wx, wz, wzs, wyx)


def full_iteration(parity, slabs, before, raw, after, weights, adjoint_weights, part, rest):
    current = slabs[2]
    planes, rows, cols = current.shape
    views = raw.shape[0]
    wy, wx, wz = weights
    return pl.pallas_call(
        iteration_kernel,
        grid=(views // STEP,),
        out_shape=jax.ShapeDtypeStruct(current.shape, F32),
        in_specs=[pl.BlockSpec(memory_space=SMEM)]
        + [whole(s) for s in slabs]
        + [step_views(a) for a in (before, raw, after)]
        + [whole(wy), step_views(wx), step_views(wz)]
        + [step_views(a) for a in adjoint_weights]
        + [whole(part), whole(rest)],
        out_specs=whole(current),
        scratch_shapes=[
            row_scratch(views, planes, rows, cols),
            pltpu.VMEM((STEP, planes, 3 * rows, cols), F32),
        ]
        + adjoint_scratch(planes, rows, cols),
        name="iteration",
        **params(2 * 10**10, 2 * 10**7),
    )(parity, *slabs, before, raw, after, *weights, *adjoint_weights, part, rest)


def two_slabs_away(value, count):
    up = [(i, i + 2) for i in range(count - 2)]
    down = [(j, i) for i, j in up]
    return lax.ppermute(value, "slab", up), lax.ppermute(value, "slab", down)


def with_near(value, far_before, far_after, parity, count):
    swap = [(i, i + 1 - 2 * (i % 2)) for i in range(count)]
    passed = jnp.stack([value, jnp.where(parity[0] == 0, far_after, far_before)])
    near = lax.ppermute(passed, "slab", swap)
    return far_before, near, value, far_after


def tap_sums(taps, offset, extent, total):
    count = taps.shape[1]
    target = offset + jnp.arange(extent)[None, :] - jnp.arange(count)[:, None] + count // 2
    reach = jnp.where((target >= 0) & (target < total), 1.0, 0.0).astype(F32)
    return jnp.sum(taps[:, :, None] * reach[None], axis=1)


def per_device(estimate, raw, taps):
    views = raw.shape[0]
    planes, rows, cols = estimate.shape
    count = lax.axis_size("slab")
    assert rows >= taps.shape[2] // 2 and count & (count - 1) == 0
    up = [(i, i + 1) for i in range(count - 1)]
    down = [(j, i) for i, j in up]
    place = lax.axis_index("slab")
    parity = (place % 2).reshape(1)

    far = two_slabs_away(estimate, count)
    before = lax.ppermute(raw, "slab", up)
    after = lax.ppermute(raw, "slab", down)

    wzs = tap_sums(taps[:, 0], 0, planes, planes)
    wy_sums = tap_sums(taps[:, 1], place * rows, rows, count * rows)
    wx_sums = tap_sums(taps[:, 2], 0, cols, cols)
    wyx = wy_sums[:, :, None] * wx_sums[:, None, :]

    forward_weights, adjoint_weights = make_weights(taps, planes, rows, cols)

    slabs = with_near(estimate, *far, parity, count)
    blurred = forward(parity, slabs, forward_weights)
    current, sums = first_adjoint(estimate, blurred, before, raw, after, adjoint_weights, wzs, wyx)

    far = two_slabs_away(current, count)
    rounds = [1 << b for b in range(count.bit_length() - 1)]
    rounds = rounds[:1] + rounds[2:] + rounds[1:2]
    others = None
    for r, distance in enumerate(rounds):
        sums = sums if others is None else sums + others
        others = lax.ppermute(sums, "slab", [(i, i ^ distance) for i in range(count)])
        if r == 1:
            *far, sums, others = lax.optimization_barrier((*far, sums, others))
    slabs = with_near(current, *far, parity, count)
    return full_iteration(
        parity, slabs, before, raw, after, forward_weights, adjoint_weights, sums, others
    )


def solution(mesh):
    placed = (P("blocks", "slab", None), P(None, "blocks", "slab", None), P())
    return jax.shard_map(
        per_device, mesh=mesh, in_specs=placed, out_specs=P("blocks", "slab", None), check_vma=False
    )
```

```python
import functools

import jax
import jax.numpy as jnp
import numpy as np
from jax import lax
from jax.experimental import pallas as pl
from jax.experimental.pallas import tpu as pltpu
from jax.sharding import PartitionSpec as P

F32 = jnp.float32
BF16 = jnp.bfloat16
VMEM = pltpu.MemorySpace.VMEM
SMEM = pltpu.MemorySpace.SMEM
FULL = pl.BlockSpec(memory_space=VMEM)
LIMIT = 30 * 1024 * 1024
STEP = 2
TINY = float(np.finfo(np.float32).tiny)


def split(value):
    high = value.astype(BF16)
    low = (value - high.astype(F32)).astype(BF16)
    return high, low


def dot(a, b):
    return jnp.dot(a, b, preferred_element_type=F32)


def placed_row(taps, lane_of_tap, width):
    count = taps.shape[1]
    tap = lax.broadcasted_iota(jnp.int32, (count, width), 0)
    lane = lax.broadcasted_iota(jnp.int32, (count, width), 1)
    onehot = jnp.where(lane == lane_of_tap(tap), 1.0, 0.0).astype(F32)
    return jnp.dot(taps, onehot, precision=lax.Precision.HIGHEST, preferred_element_type=F32)


def slanted(row, height):
    full = jnp.broadcast_to(row, (height, row.shape[1]))
    return pltpu.roll(full, 0, 1, stride=1, stride_axis=0)


def weights_kernel(rows, taps_ref, *outs):
    views, _, count = taps_ref.shape
    margin = count // 2
    for flip in (False, True):
        wy, wx, wz = outs[3 * flip : 3 * flip + 3]
        order = (lambda k: count - 1 - k) if flip else (lambda k: k)
        out_rows = rows if flip else 3 * rows
        in_rows = out_rows + 2 * rows
        planes = wz.shape[1]
        cols = wx.shape[1] // 2
        row_y = placed_row(taps_ref[:, 1, :], lambda k: order(k) + rows - margin, 256)
        high = row_y.astype(BF16).astype(F32)
        low = row_y - high
        if flip:
            row_y = [part + pltpu.roll(part, in_rows, 1) for part in (high, low)]
        else:
            row_y = high + pltpu.roll(high, in_rows, 1) + pltpu.roll(low, 2 * in_rows, 1)
        row_x = placed_row(taps_ref[:, 2, :], lambda k: lax.rem(margin - order(k) + 2 * cols, 2 * cols), 2 * cols)
        row_z = placed_row(taps_ref[:, 0, :], lambda k: lax.rem(order(k) - margin + 128, 128), 128)
        inside = lax.broadcasted_iota(jnp.int32, (planes, 128), 1) < planes
        for v in range(views):
            if flip:
                for j, row in enumerate(row_y):
                    wy[v, j * rows : (j + 1) * rows, :] = slanted(row[v : v + 1], rows)[:, : 2 * in_rows].astype(BF16)
            else:
                band = slanted(row_y[v : v + 1], out_rows)
                wy[v * out_rows : (v + 1) * out_rows, :] = band[:, : 3 * in_rows].astype(BF16)
            high, low = split(slanted(row_x[v : v + 1], cols)[:, :cols])
            wx[v, :cols, :cols] = high
            wx[v, cols:, :cols] = high
            wx[v, :cols, cols:] = low
            wx[v, cols:, cols:] = low
            band = jnp.where(inside, slanted(row_z[v : v + 1], planes), 0.0)
            high = band.astype(BF16).astype(F32)
            band = high + pltpu.roll(high, planes, 1) + pltpu.roll(band - high, 2 * planes, 1)
            wz[v] = band[:, : 3 * planes].astype(BF16)


def make_weights(taps, planes, rows, cols):
    views = taps.shape[0]
    shapes = []
    for row_weights in ((views * 3 * rows, 15 * rows), (views, 2 * rows, 6 * rows)):
        shapes += [
            jax.ShapeDtypeStruct(row_weights, BF16),
            jax.ShapeDtypeStruct((views, 2 * cols, 2 * cols), BF16),
            jax.ShapeDtypeStruct((views, planes, 3 * planes), BF16),
        ]
    outs = pl.pallas_call(
        functools.partial(weights_kernel, rows),
        out_shape=shapes,
        in_specs=[FULL],
        out_specs=[FULL] * 6,
        compiler_params=pltpu.CompilerParams(vmem_limit_bytes=LIMIT),
        cost_estimate=pl.CostEstimate(flops=10**7, bytes_accessed=10**7, transcendentals=0),
        name="weights",
    )(taps)
    return outs[:3], outs[3:]


def stacked(pieces):
    columns = []
    for piece in pieces:
        high, low = split(piece)
        columns.append(jnp.concatenate([high, low, high], axis=0))
    return jnp.concatenate(columns, axis=1)


def row_pairs(rows_ref, wx, wz, xs):
    planes, height, lanes = rows_ref.shape
    cols = lanes // 2
    both = dot(rows_ref.reshape(planes * height, lanes), wx)
    xs[...] = both[:, :cols] + both[:, cols:]
    for y in range(0, height, 2):
        yield y, dot(wz, stacked([xs[pl.ds(y + j, planes, stride=height), :] for j in range(2)]))


def forward_rows(parity, far_before, near, own, far_after, wy, ys):
    planes, rows, cols = far_before.shape
    views = ys.shape[0]
    height = 3 * rows
    side = parity[0]

    def plane(z):
        return jnp.concatenate(
            [far_before[z], near[1 - side, z], own[z * rows : (z + 1) * rows, :], near[side, z], far_after[z]], axis=0
        )

    for z in range(0, planes, 2):
        result = dot(wy[...], stacked([plane(z), plane(z + 1)]))
        high, low = split(result)
        for j in range(2):
            for v in range(views):
                there = (slice(v * height, (v + 1) * height), slice(j * cols, (j + 1) * cols))
                ys[v, z + j, :, :cols] = high[there]
                ys[v, z + j, :, cols:] = low[there]


def forward_view(view, ys, wx, wz, xs, out):
    _, planes, height, lanes = ys.shape
    cols = lanes // 2
    for pair in range(height // 16):
        rows_ref = ys[view, :, 16 * pair : 16 * pair + 16, :]
        for y, values in row_pairs(rows_ref, wx, wz, xs.at[pair]):
            for j in range(2):
                at = pl.ds(16 * pair + y + j, planes, stride=height)
                out[at, :] = values[:, j * cols : (j + 1) * cols]


def adjoint_views(blurred, before, raw, after, wy, wx, wz, ya, xs, acc):
    _, planes, rows, cols = raw.shape

    def quotient(v, z):
        counts = jnp.concatenate([before[v, z], raw[v, z], after[v, z]], axis=0)
        below = jnp.maximum(blurred[v, 3 * rows * z : 3 * rows * (z + 1), :], TINY)
        inverse = pl.reciprocal(below, approx=True)
        return counts * (inverse * (2.0 - below * inverse))

    for v in range(STEP):
        for z in range(0, planes, 2):
            high, low = split(jnp.concatenate([quotient(v, z), quotient(v, z + 1)], axis=1))
            both = dot(wy[v], jnp.concatenate([high, low], axis=0))
            high, low = split(both[:rows] + both[rows:])
            for j in range(2):
                ya[v, z + j, :, :cols] = high[:, j * cols : (j + 1) * cols]
                ya[v, z + j, :, cols:] = low[:, j * cols : (j + 1) * cols]
    for pair in range(rows // 16):
        chosen = slice(16 * pair, 16 * pair + 16)
        found = [row_pairs(ya[v, :, chosen, :], wx[v], wz[v], xs.at[v]) for v in range(STEP)]
        for results in zip(*found):
            at = 8 * pair + results[0][0] // 2
            acc[at] += sum(jnp.log(values) for _, values in results)


def updated(current, exponents, out):
    pairs, planes, lanes = exponents.shape
    cols = lanes // 2
    for y in range(2 * pairs):
        at = pl.ds(y, planes, stride=2 * pairs)
        half = slice((y % 2) * cols, (y % 2 + 1) * cols)
        out[at, :] = current[at, :] * jnp.exp(exponents[y // 2, :, half])


def forward_kernel(parity, far_before, near, own, far_after, wy, wx, wz, out, ys, xs):
    @pl.when(pl.program_id(0) == 0)
    def _():
        forward_rows(parity, far_before, near, own, far_after, wy, ys)

    for v in range(STEP):
        forward_view(STEP * pl.program_id(0) + v, ys, wx[v], wz[v], xs.at[v], out.at[v])


def weighted_sums(values, wzs, wyx, sums, at):
    planes, (_, rows, cols) = wzs.shape[1], wyx.shape
    for v in range(wyx.shape[0]):
        total = jnp.zeros((rows, cols), F32)
        for z in range(planes):
            total = total + wzs[v, z] * values[z * rows : (z + 1) * rows, :]
        sums[at + v : at + v + 1, :] = jnp.sum(total * wyx[v], axis=0, keepdims=True)


def first_adjoint_kernel(current, blurred, before, raw, after, wy, wx, wz, wzs, wyx, out, sums, ya, xs, acc):
    step, views = pl.program_id(0), wyx.shape[0]

    @pl.when(step == 0)
    def _():
        acc[...] = jnp.zeros_like(acc)
        sums[...] = jnp.zeros_like(sums)

    for v in range(STEP):
        total = jnp.sum(jnp.sum(raw[v], axis=0), axis=0, keepdims=True)
        sums[pl.ds(STEP * step + v, 1), :] = total
    adjoint_views(blurred, before, raw, after, wy, wx, wz, ya, xs, acc)

    @pl.when(step == pl.num_programs(0) - 1)
    def _():
        updated(current, acc[...] * (1.0 / views), out)
        weighted_sums(current, wzs, wyx, sums, sums.shape[0] // 3)
        weighted_sums(out, wzs, wyx, sums, 2 * sums.shape[0] // 3)


def iteration_kernel(
    parity, far_before, near, own, far_after, before, raw, after, wy, wx, wz, wya, wxa, wza, part, rest,
    out, ys, xs, blurred, ya, xa, acc,
):
    step, views = pl.program_id(0), ys.shape[0]

    @pl.when(step == 0)
    def _():
        acc[...] = jnp.zeros_like(acc)
        forward_rows(parity, far_before, near, own, far_after, wy, ys)

    for v in range(STEP):
        forward_view(STEP * step + v, ys, wx[v], wz[v], xs.at[v], blurred.at[v])
    adjoint_views(blurred, before, raw, after, wya, wxa, wza, ya, xa, acc)

    @pl.when(step == pl.num_programs(0) - 1)
    def _():
        sums = jnp.sum(part[...] + rest[...], axis=1, keepdims=True)
        space = sums.shape[0] // 3
        total, first, second = (sums[i * space : i * space + views] for i in range(3))
        scale = jnp.sum(jnp.log(first / total) + jnp.log(second / total), axis=0, keepdims=True)
        updated(own, (acc[...] + scale[None]) * (1.0 / views), out)


def whole(array):
    return pl.BlockSpec(array.shape, lambda v: (0,) * array.ndim)


def step_views(array):
    return pl.BlockSpec((STEP,) + array.shape[1:], lambda v: (v,) + (0,) * (array.ndim - 1))


def params(flops, moved):
    return dict(
        compiler_params=pltpu.CompilerParams(vmem_limit_bytes=LIMIT),
        cost_estimate=pl.CostEstimate(flops=flops, bytes_accessed=moved, transcendentals=10**5),
    )


def forward_scratch(views, planes, rows, cols):
    return [
        pltpu.VMEM((views, planes, 3 * rows, 2 * cols), BF16),
        pltpu.VMEM((STEP, 3 * rows // 16, planes * 16, cols), F32),
    ]


def adjoint_scratch(planes, rows, cols):
    return [
        pltpu.VMEM((STEP, planes, rows, 2 * cols), BF16),
        pltpu.VMEM((STEP, planes * 16, cols), F32),
        pltpu.VMEM((rows // 2, planes, 2 * cols), F32),
    ]


def forward(parity, slabs, weights):
    planes, rows, cols = slabs[0].shape
    wy, wx, wz = weights
    views = wx.shape[0]
    slabs = [s.reshape(-1, cols) if i == 2 else s for i, s in enumerate(slabs)]
    out = jax.ShapeDtypeStruct((views, planes * 3 * rows, cols), F32)
    return pl.pallas_call(
        forward_kernel,
        grid=(views // STEP,),
        out_shape=out,
        in_specs=[pl.BlockSpec(memory_space=SMEM)]
        + [whole(s) for s in slabs]
        + [whole(wy), step_views(wx), step_views(wz)],
        out_specs=step_views(out),
        scratch_shapes=forward_scratch(views, planes, rows, cols),
        name="forward",
        **params(10**10, 10**7),
    )(parity, *slabs, *weights)


def first_adjoint(current, blurred, before, raw, after, weights, wzs, wyx):
    wy, wx, wz = weights
    views = raw.shape[0]
    planes, rows, cols = current.shape
    current = current.reshape(planes * rows, cols)
    shapes = [
        jax.ShapeDtypeStruct(current.shape, F32),
        jax.ShapeDtypeStruct((24 * -(-views // 8), cols), F32),
    ]
    out, sums = pl.pallas_call(
        first_adjoint_kernel,
        grid=(views // STEP,),
        out_shape=shapes,
        in_specs=[whole(current)]
        + [step_views(a) for a in (blurred, before, raw, after, wy, wx, wz)]
        + [pl.BlockSpec(memory_space=SMEM), whole(wyx)],
        out_specs=[whole(s) for s in shapes],
        scratch_shapes=adjoint_scratch(planes, rows, cols),
        name="adjoint",
        **params(10**10, 10**7),
    )(current, blurred, before, raw, after, wy, wx, wz, wzs, wyx)
    return out.reshape(planes, rows, cols), sums


def full_iteration(parity, slabs, before, raw, after, weights, adjoint_weights, part, rest):
    planes, rows, cols = slabs[0].shape
    views = raw.shape[0]
    wy, wx, wz = weights
    slabs = [s.reshape(-1, cols) if i == 2 else s for i, s in enumerate(slabs)]
    out = jax.ShapeDtypeStruct((planes * rows, cols), F32)
    return pl.pallas_call(
        iteration_kernel,
        grid=(views // STEP,),
        out_shape=out,
        in_specs=[pl.BlockSpec(memory_space=SMEM)]
        + [whole(s) for s in slabs]
        + [step_views(a) for a in (before, raw, after)]
        + [whole(wy), step_views(wx), step_views(wz)]
        + [step_views(a) for a in adjoint_weights]
        + [whole(part), whole(rest)],
        out_specs=whole(out),
        scratch_shapes=forward_scratch(views, planes, rows, cols)
        + [pltpu.VMEM((STEP, planes * 3 * rows, cols), F32)]
        + adjoint_scratch(planes, rows, cols),
        name="iteration",
        **params(2 * 10**10, 2 * 10**7),
    )(parity, *slabs, before, raw, after, *weights, *adjoint_weights, part, rest).reshape(planes, rows, cols)


def two_slabs_away(value, count):
    up = [(i, i + 2) for i in range(count - 2)]
    down = [(j, i) for i, j in up]
    return lax.ppermute(value, "slab", up), lax.ppermute(value, "slab", down)


def with_near(value, far_before, far_after, parity, count):
    swap = [(i, i + 1 - 2 * (i % 2)) for i in range(count)]
    passed = jnp.stack([value, jnp.where(parity[0] == 0, far_after, far_before)])
    near = lax.ppermute(passed, "slab", swap)
    return far_before, near, value, far_after


def tap_sums(taps, offset, extent, total):
    count = taps.shape[1]
    target = offset + jnp.arange(extent)[None, :] - jnp.arange(count)[:, None] + count // 2
    reach = jnp.where((target >= 0) & (target < total), 1.0, 0.0).astype(F32)
    return jnp.sum(taps[:, :, None] * reach[None], axis=1)


def per_device(estimate, raw, taps):
    views = raw.shape[0]
    planes, rows, cols = estimate.shape
    count = lax.axis_size("slab")
    assert rows >= taps.shape[2] // 2 and count & (count - 1) == 0
    up = [(i, i + 1) for i in range(count - 1)]
    down = [(j, i) for i, j in up]
    place = lax.axis_index("slab")
    parity = (place % 2).reshape(1)

    far = two_slabs_away(estimate, count)
    before = lax.ppermute(raw, "slab", up)
    after = lax.ppermute(raw, "slab", down)

    wzs = tap_sums(taps[:, 0], 0, planes, planes)
    wy_sums = tap_sums(taps[:, 1], place * rows, rows, count * rows)
    wx_sums = tap_sums(taps[:, 2], 0, cols, cols)
    wyx = wy_sums[:, :, None] * wx_sums[:, None, :]

    forward_weights, adjoint_weights = make_weights(taps, planes, rows, cols)

    slabs = with_near(estimate, *far, parity, count)
    blurred = forward(parity, slabs, forward_weights)
    current, sums = first_adjoint(estimate, blurred, before, raw, after, adjoint_weights, wzs, wyx)

    far = two_slabs_away(current, count)
    bits = [1 << b for b in range(count.bit_length() - 1)]
    rounds = [bits[:1], bits[2:4] + [sum(bits[2:4])], *([b] for b in bits[4:]), bits[1:2]]
    for r, distances in enumerate(rounds):
        others = [lax.ppermute(sums, "slab", [(i, i ^ d) for i in range(count)]) for d in distances]
        if r == 1:
            *far, sums = lax.optimization_barrier((*far, sums + sum(others)))
        elif r < len(rounds) - 1:
            sums = sums + sum(others)
    slabs = with_near(current, *far, parity, count)
    return full_iteration(
        parity, slabs, before, raw, after, forward_weights, adjoint_weights, sums, others[0]
    )


def solution(mesh):
    placed = (P("blocks", "slab", None), P(None, "blocks", "slab", None), P())
    return jax.shard_map(
        per_device, mesh=mesh, in_specs=placed, out_specs=P("blocks", "slab", None), check_vma=False
    )
```

```python
import functools

import jax
import jax.numpy as jnp
import numpy as np
from jax import lax
from jax.experimental import pallas as pl
from jax.experimental.pallas import tpu as pltpu
from jax.sharding import PartitionSpec as P

F32 = jnp.float32
BF16 = jnp.bfloat16
VMEM = pltpu.MemorySpace.VMEM
SMEM = pltpu.MemorySpace.SMEM
FULL = pl.BlockSpec(memory_space=VMEM)
LIMIT = 30 * 1024 * 1024
STEP = 2
TINY = float(np.finfo(np.float32).tiny)


def split(value):
    high = value.astype(BF16)
    low = (value - high.astype(F32)).astype(BF16)
    return high, low


def dot(a, b):
    return jnp.dot(a, b, preferred_element_type=F32)


def placed_row(taps, lane_of_tap, width):
    count = taps.shape[1]
    tap = lax.broadcasted_iota(jnp.int32, (count, width), 0)
    lane = lax.broadcasted_iota(jnp.int32, (count, width), 1)
    onehot = jnp.where(lane == lane_of_tap(tap), 1.0, 0.0).astype(F32)
    return jnp.dot(taps, onehot, precision=lax.Precision.HIGHEST, preferred_element_type=F32)


def slanted(row, height):
    full = jnp.broadcast_to(row, (height, row.shape[1]))
    return pltpu.roll(full, 0, 1, stride=1, stride_axis=0)


def weights_kernel(rows, taps_ref, *outs):
    views, _, count = taps_ref.shape
    margin = count // 2
    for flip in (False, True):
        wy, wx, wz = outs[3 * flip : 3 * flip + 3]
        order = (lambda k: count - 1 - k) if flip else (lambda k: k)
        out_rows = rows if flip else 3 * rows
        in_rows = out_rows + 2 * rows
        planes = wz.shape[1] // (1 if flip else 8)
        cols = wx.shape[1] // 2
        row_y = placed_row(taps_ref[:, 1, :], lambda k: order(k) + rows - margin, 256)
        high = row_y.astype(BF16).astype(F32)
        low = row_y - high
        if flip:
            row_y = [part + pltpu.roll(part, in_rows, 1) for part in (high, low)]
        else:
            row_y = high + pltpu.roll(high, in_rows, 1) + pltpu.roll(low, 2 * in_rows, 1)
        row_x = placed_row(taps_ref[:, 2, :], lambda k: lax.rem(margin - order(k) + 2 * cols, 2 * cols), 2 * cols)
        apart = 1 if flip else 8
        width_z = 128 if flip else 16 * planes
        row_z = placed_row(
            taps_ref[:, 0, :], lambda k: lax.rem(apart * (order(k) - margin) + width_z, width_z), width_z
        )
        inside = lax.broadcasted_iota(jnp.int32, (planes, 128), 1) < planes
        for v in range(views):
            if flip:
                for j, row in enumerate(row_y):
                    wy[v, j * rows : (j + 1) * rows, :] = slanted(row[v : v + 1], rows)[:, : 2 * in_rows].astype(BF16)
            else:
                band = slanted(row_y[v : v + 1], out_rows)
                wy[v * out_rows : (v + 1) * out_rows, :] = band[:, : 3 * in_rows].astype(BF16)
            high, low = split(slanted(row_x[v : v + 1], cols)[:, :cols])
            wx[v, :cols, :cols] = high
            wx[v, cols:, :cols] = high
            wx[v, :cols, cols:] = low
            wx[v, cols:, cols:] = low
            if flip:
                band = jnp.where(inside, slanted(row_z[v : v + 1], planes), 0.0)
                high = band.astype(BF16).astype(F32)
                band = high + pltpu.roll(high, planes, 1) + pltpu.roll(band - high, 2 * planes, 1)
                wz[v] = band[:, : 3 * planes].astype(BF16)
            else:
                size = 8 * planes
                high, low = split(slanted(row_z[v : v + 1], size)[:, :size])
                wz[v, :, :size] = high
                wz[v, :, size : 2 * size] = high
                wz[v, :, 2 * size :] = low


def call(kernel, outs, smem, arrays, scratch, name, flops):
    arrays = [pltpu.with_memory_space_constraint(a, VMEM) for a in arrays]
    return pl.pallas_call(
        kernel,
        out_shape=outs,
        in_specs=[pl.BlockSpec(memory_space=SMEM)] * len(smem) + [FULL] * len(arrays),
        out_specs=jax.tree.map(lambda _: FULL, outs),
        scratch_shapes=scratch,
        compiler_params=pltpu.CompilerParams(vmem_limit_bytes=LIMIT),
        cost_estimate=pl.CostEstimate(flops=flops, bytes_accessed=10**7, transcendentals=10**5),
        name=name,
    )(*smem, *arrays)


def make_weights(taps, planes, rows, cols):
    views = taps.shape[0]
    outs = [
        pltpu.VMEM((views * 3 * rows, 15 * rows), BF16),
        pltpu.VMEM((views, 2 * cols, 2 * cols), BF16),
        pltpu.VMEM((views, 8 * planes, 24 * planes), BF16),
        pltpu.VMEM((views, 2 * rows, 6 * rows), BF16),
        pltpu.VMEM((views, 2 * cols, 2 * cols), BF16),
        pltpu.VMEM((views, planes, 3 * planes), BF16),
    ]
    made = call(functools.partial(weights_kernel, rows), outs, [], [taps], [], "weights", 10**7)
    return made[:3], made[3:]


def stacked(pieces):
    columns = []
    for piece in pieces:
        high, low = split(piece)
        columns.append(jnp.concatenate([high, low, high], axis=0))
    return jnp.concatenate(columns, axis=1)


def two_groups(rows_ref, wx, wz, planes, cols):
    both = dot(rows_ref.reshape(planes * 16, 2 * cols), wx)
    value = (both[:, :cols] + both[:, cols:]).reshape(planes, 16, cols)
    return dot(wz, stacked([value[:, 8 * g : 8 * g + 8, :].reshape(planes * 8, cols) for g in range(2)]))


def row_pairs(rows_ref, wx, wz, xs):
    planes, height, lanes = rows_ref.shape
    cols = lanes // 2
    both = dot(rows_ref.reshape(planes * height, lanes), wx)
    xs[...] = both[:, :cols] + both[:, cols:]
    for y in range(0, height, 2):
        yield y, dot(wz, stacked([xs[pl.ds(y + j, planes, stride=height), :] for j in range(2)]))


def forward_rows(parity, far_before, near, own, far_after, wy, ys):
    planes, rows, cols = far_before.shape
    views = ys.shape[0]
    height = 3 * rows
    side = parity[0]

    def plane(z):
        return jnp.concatenate(
            [far_before[z], near[1 - side, z], own[z * rows : (z + 1) * rows, :], near[side, z], far_after[z]], axis=0
        )

    for z in range(0, planes, 2):
        result = dot(wy[...], stacked([plane(z), plane(z + 1)]))
        high, low = split(result)
        for j in range(2):
            for v in range(views):
                there = (slice(v * height, (v + 1) * height), slice(j * cols, (j + 1) * cols))
                ys[v, z + j, :, :cols] = high[there]
                ys[v, z + j, :, cols:] = low[there]


def forward_view(ys, wx, wz, out):
    planes, height, lanes = ys.shape
    cols = lanes // 2
    for pair in range(height // 16):
        result = two_groups(ys[:, 16 * pair : 16 * pair + 16, :], wx, wz, planes, cols)
        for j in range(2):
            at = 16 * pair + 8 * j
            out[:, at : at + 8, :] = result[:, j * cols : (j + 1) * cols].reshape(planes, 8, cols)


def adjoint_views(blurred, before, raw, after, wy, wx, wz, ya, xs, acc):
    _, planes, rows, cols = raw.shape

    def quotient(v, z):
        counts = jnp.concatenate([before[v, z], raw[v, z], after[v, z]], axis=0)
        below = jnp.maximum(blurred[v, z], TINY)
        inverse = pl.reciprocal(below, approx=True)
        return counts * (inverse * (2.0 - below * inverse))

    for v in range(STEP):
        for z in range(0, planes, 2):
            high, low = split(jnp.concatenate([quotient(v, z), quotient(v, z + 1)], axis=1))
            both = dot(wy[v], jnp.concatenate([high, low], axis=0))
            high, low = split(both[:rows] + both[rows:])
            for j in range(2):
                ya[v, z + j, :, :cols] = high[:, j * cols : (j + 1) * cols]
                ya[v, z + j, :, cols:] = low[:, j * cols : (j + 1) * cols]
    for pair in range(rows // 16):
        chosen = slice(16 * pair, 16 * pair + 16)
        found = [row_pairs(ya[v, :, chosen, :], wx[v], wz[v], xs.at[v]) for v in range(STEP)]
        for results in zip(*found):
            at = 8 * pair + results[0][0] // 2
            acc[at] += sum(jnp.log(values) for _, values in results)


def updated(current, exponents, out):
    pairs, planes, lanes = exponents.shape
    cols = lanes // 2
    for y in range(2 * pairs):
        at = pl.ds(y, planes, stride=2 * pairs)
        half = slice((y % 2) * cols, (y % 2 + 1) * cols)
        out[at, :] = current[at, :] * jnp.exp(exponents[y // 2, :, half])


def each_step(views, body):
    def run(step, _):
        body(pl.ds(STEP * step, STEP))
        return 0

    lax.fori_loop(0, views // STEP, run, 0)


def forward_kernel(parity, far_before, near, own, far_after, wy, wx, wz, out, ys):
    forward_rows(parity, far_before, near, own, far_after, wy, ys)

    def step(chosen):
        fields = [ref.at[chosen] for ref in (ys, wx, wz, out)]
        for v in range(STEP):
            f = [ref.at[v] for ref in fields]
            forward_view(f[0], f[1][...], f[2][...], f[3])

    each_step(ys.shape[0], step)


def weighted_sums(values, wzs, wyx, sums, at):
    planes, (_, rows, cols) = wzs.shape[1], wyx.shape
    for v in range(wyx.shape[0]):
        total = jnp.zeros((rows, cols), F32)
        for z in range(planes):
            total = total + wzs[v, z] * values[z * rows : (z + 1) * rows, :]
        sums[at + v : at + v + 1, :] = jnp.sum(total * wyx[v], axis=0, keepdims=True)


def first_adjoint_kernel(wzs, current, blurred, before, raw, after, wy, wx, wz, wyx, out, sums, ya, xs, acc):
    views = wyx.shape[0]
    acc[...] = jnp.zeros_like(acc)
    sums[...] = jnp.zeros_like(sums)

    def step(chosen):
        fields = [ref.at[chosen] for ref in (blurred, before, raw, after, wy, wx, wz)]
        adjoint_views(*fields, ya, xs, acc)
        total = [jnp.sum(jnp.sum(fields[2][v], axis=0), axis=0, keepdims=True) for v in range(STEP)]
        sums[chosen, :] = jnp.concatenate(total, axis=0)

    each_step(views, step)
    updated(current, acc[...] * (1.0 / views), out)
    weighted_sums(current, wzs, wyx, sums, sums.shape[0] // 3)
    weighted_sums(out, wzs, wyx, sums, 2 * sums.shape[0] // 3)


def iteration_kernel(
    parity, far_before, near, own, far_after, before, raw, after, wy, wx, wz, wya, wxa, wza, part, rest,
    out, ys, blurred, ya, xs, acc,
):
    views = ys.shape[0]
    acc[...] = jnp.zeros_like(acc)
    forward_rows(parity, far_before, near, own, far_after, wy, ys)

    def step(chosen):
        fields = [ref.at[chosen] for ref in (ys, wx, wz)]
        for v in range(STEP):
            f = [ref.at[v] for ref in fields]
            forward_view(f[0], f[1][...], f[2][...], blurred.at[v])
        fields = [ref.at[chosen] for ref in (before, raw, after, wya, wxa, wza)]
        adjoint_views(blurred, *fields, ya, xs, acc)

    each_step(views, step)
    sums = jnp.sum(part[...] + rest[...], axis=1, keepdims=True)
    space = sums.shape[0] // 3
    total, first, second = (sums[i * space : i * space + views] for i in range(3))
    scale = jnp.sum(jnp.log(first / total) + jnp.log(second / total), axis=0, keepdims=True)
    updated(own, (acc[...] + scale[None]) * (1.0 / views), out)


def adjoint_scratch(planes, rows, cols):
    return [
        pltpu.VMEM((STEP, planes, rows, 2 * cols), BF16),
        pltpu.VMEM((STEP, planes * 16, cols), F32),
        pltpu.VMEM((rows // 2, planes, 2 * cols), F32),
    ]


def forward(parity, slabs, weights):
    planes, rows, cols = slabs[0].shape
    views = weights[1].shape[0]
    slabs = [s.reshape(-1, cols) if i == 2 else s for i, s in enumerate(slabs)]
    out = pltpu.VMEM((views, planes, 3 * rows, cols), F32)
    scratch = [pltpu.VMEM((views, planes, 3 * rows, 2 * cols), BF16)]
    return call(forward_kernel, out, [parity], [*slabs, *weights], scratch, "forward", 10**10)


def first_adjoint(current, blurred, before, raw, after, weights, wzs, wyx):
    planes, rows, cols = current.shape
    views = raw.shape[0]
    current = current.reshape(planes * rows, cols)
    outs = [pltpu.VMEM(current.shape, F32), pltpu.VMEM((24 * -(-views // 8), cols), F32)]
    out, sums = call(
        first_adjoint_kernel,
        outs,
        [wzs],
        [current, blurred, before, raw, after, *weights, wyx],
        adjoint_scratch(planes, rows, cols),
        "adjoint",
        10**10,
    )
    return out.reshape(planes, rows, cols), sums


def full_iteration(parity, slabs, before, raw, after, weights, adjoint_weights, part, rest):
    planes, rows, cols = slabs[0].shape
    views = raw.shape[0]
    slabs = [s.reshape(-1, cols) if i == 2 else s for i, s in enumerate(slabs)]
    scratch = [
        pltpu.VMEM((views, planes, 3 * rows, 2 * cols), BF16),
        pltpu.VMEM((STEP, planes, 3 * rows, cols), F32),
    ]
    return call(
        iteration_kernel,
        jax.ShapeDtypeStruct((planes * rows, cols), F32),
        [parity],
        [*slabs, before, raw, after, *weights, *adjoint_weights, part, rest],
        scratch + adjoint_scratch(planes, rows, cols),
        "iteration",
        2 * 10**10,
    ).reshape(planes, rows, cols)


def two_slabs_away(value, count):
    up = [(i, i + 2) for i in range(count - 2)]
    down = [(j, i) for i, j in up]
    return lax.ppermute(value, "slab", up), lax.ppermute(value, "slab", down)


def with_near(value, far_before, far_after, parity, count):
    swap = [(i, i + 1 - 2 * (i % 2)) for i in range(count)]
    passed = jnp.stack([value, jnp.where(parity[0] == 0, far_after, far_before)])
    near = lax.ppermute(passed, "slab", swap)
    return far_before, near, value, far_after


def tap_sums(taps, offset, extent, total):
    count = taps.shape[1]
    target = offset + jnp.arange(extent)[None, :] - jnp.arange(count)[:, None] + count // 2
    reach = jnp.where((target >= 0) & (target < total), 1.0, 0.0).astype(F32)
    return jnp.sum(taps[:, :, None] * reach[None], axis=1)


def per_device(estimate, raw, taps):
    views = raw.shape[0]
    planes, rows, cols = estimate.shape
    count = lax.axis_size("slab")
    assert rows >= taps.shape[2] // 2 and count & (count - 1) == 0
    up = [(i, i + 1) for i in range(count - 1)]
    down = [(j, i) for i, j in up]
    place = lax.axis_index("slab")
    parity = (place % 2).reshape(1)

    far = two_slabs_away(estimate, count)
    before = lax.ppermute(raw, "slab", up)
    after = lax.ppermute(raw, "slab", down)

    wzs = tap_sums(taps[:, 0], 0, planes, planes)
    wy_sums = tap_sums(taps[:, 1], place * rows, rows, count * rows)
    wx_sums = tap_sums(taps[:, 2], 0, cols, cols)
    wyx = wy_sums[:, :, None] * wx_sums[:, None, :]

    forward_weights, adjoint_weights = make_weights(taps, planes, rows, cols)

    slabs = with_near(estimate, *far, parity, count)
    blurred = forward(parity, slabs, forward_weights)
    current, sums = first_adjoint(estimate, blurred, before, raw, after, adjoint_weights, wzs, wyx)

    far = two_slabs_away(current, count)
    bits = [1 << b for b in range(count.bit_length() - 1)]
    rounds = [bits[:1], bits[2:4] + [sum(bits[2:4])], *([b] for b in bits[4:]), bits[1:2]]
    for r, distances in enumerate(rounds):
        others = [lax.ppermute(sums, "slab", [(i, i ^ d) for i in range(count)]) for d in distances]
        if r == 1:
            *far, sums = lax.optimization_barrier((*far, sums + sum(others)))
        elif r < len(rounds) - 1:
            sums = sums + sum(others)
    slabs = with_near(current, *far, parity, count)
    return full_iteration(
        parity, slabs, before, raw, after, forward_weights, adjoint_weights, sums, others[0]
    )


def solution(mesh):
    placed = (P("blocks", "slab", None), P(None, "blocks", "slab", None), P())
    return jax.shard_map(
        per_device, mesh=mesh, in_specs=placed, out_specs=P("blocks", "slab", None), check_vma=False
    )
```

```python
import functools

import jax
import jax.numpy as jnp
import numpy as np
from jax import lax
from jax.experimental import pallas as pl
from jax.experimental.pallas import tpu as pltpu
from jax.sharding import PartitionSpec as P

F32 = jnp.float32
BF16 = jnp.bfloat16
VMEM = pltpu.MemorySpace.VMEM
SMEM = pltpu.MemorySpace.SMEM
FULL = pl.BlockSpec(memory_space=VMEM)
LIMIT = 30 * 1024 * 1024
STEP = 2
TINY = float(np.finfo(np.float32).tiny)


def split(value):
    high = value.astype(BF16)
    low = (value - high.astype(F32)).astype(BF16)
    return high, low


def dot(a, b):
    return jnp.dot(a, b, preferred_element_type=F32)


def placed_row(taps, lane_of_tap, width):
    count = taps.shape[1]
    tap = lax.broadcasted_iota(jnp.int32, (count, width), 0)
    lane = lax.broadcasted_iota(jnp.int32, (count, width), 1)
    onehot = jnp.where(lane == lane_of_tap(tap), 1.0, 0.0).astype(F32)
    return jnp.dot(taps, onehot, precision=lax.Precision.HIGHEST, preferred_element_type=F32)


def slanted(row, height):
    full = jnp.broadcast_to(row, (height, row.shape[1]))
    return pltpu.roll(full, 0, 1, stride=1, stride_axis=0)


def weights_kernel(rows, taps_ref, *outs):
    views, _, count = taps_ref.shape
    margin = count // 2
    for flip in (False, True):
        wy, wx, wz = outs[3 * flip : 3 * flip + 3]
        order = (lambda k: count - 1 - k) if flip else (lambda k: k)
        out_rows = rows if flip else 3 * rows
        in_rows = out_rows + 2 * rows
        planes = wz.shape[1] // (1 if flip else 8)
        cols = wx.shape[1] // 2
        row_y = placed_row(taps_ref[:, 1, :], lambda k: order(k) + rows - margin, 256)
        high = row_y.astype(BF16).astype(F32)
        low = row_y - high
        if flip:
            row_y = [part + pltpu.roll(part, in_rows, 1) for part in (high, low)]
            row_y = [part if j == 0 else pltpu.roll(part, 2 * in_rows, 1) for part in row_y for j in range(2)]
        else:
            row_y = high + pltpu.roll(high, in_rows, 1) + pltpu.roll(low, 2 * in_rows, 1)
        row_x = placed_row(taps_ref[:, 2, :], lambda k: lax.rem(margin - order(k) + 2 * cols, 2 * cols), 2 * cols)
        apart = 1 if flip else 8
        width_z = 128 if flip else 16 * planes
        row_z = placed_row(
            taps_ref[:, 0, :], lambda k: lax.rem(apart * (order(k) - margin) + width_z, width_z), width_z
        )
        inside = lax.broadcasted_iota(jnp.int32, (planes, 128), 1) < planes
        for v in range(views):
            if flip:
                for j, row in enumerate(row_y):
                    wy[v, j * rows : (j + 1) * rows, :] = slanted(row[v : v + 1], rows)[:, : 4 * in_rows].astype(BF16)
            else:
                band = slanted(row_y[v : v + 1], out_rows)
                wy[v * out_rows : (v + 1) * out_rows, :] = band[:, : 3 * in_rows].astype(BF16)
            high, low = split(slanted(row_x[v : v + 1], cols)[:, :cols])
            wx[v, :cols, :cols] = high
            wx[v, cols:, :cols] = high
            wx[v, :cols, cols:] = low
            wx[v, cols:, cols:] = low
            if flip:
                band = jnp.where(inside, slanted(row_z[v : v + 1], planes), 0.0)
                high = band.astype(BF16).astype(F32)
                band = high + pltpu.roll(high, planes, 1) + pltpu.roll(band - high, 2 * planes, 1)
                wz[v] = band[:, : 3 * planes].astype(BF16)
            else:
                size = 8 * planes
                high, low = split(slanted(row_z[v : v + 1], size)[:, :size])
                wz[v, :, :size] = high
                wz[v, :, size : 2 * size] = high
                wz[v, :, 2 * size :] = low


def call(kernel, outs, smem, arrays, scratch, name, flops):
    arrays = [pltpu.with_memory_space_constraint(a, VMEM) for a in arrays]
    return pl.pallas_call(
        kernel,
        out_shape=outs,
        in_specs=[pl.BlockSpec(memory_space=SMEM)] * len(smem) + [FULL] * len(arrays),
        out_specs=jax.tree.map(lambda _: FULL, outs),
        scratch_shapes=scratch,
        compiler_params=pltpu.CompilerParams(vmem_limit_bytes=LIMIT),
        cost_estimate=pl.CostEstimate(flops=flops, bytes_accessed=10**7, transcendentals=10**5),
        name=name,
    )(*smem, *arrays)


def make_weights(taps, planes, rows, cols):
    views = taps.shape[0]
    outs = [
        pltpu.VMEM((views * 3 * rows, 15 * rows), BF16),
        pltpu.VMEM((views, 2 * cols, 2 * cols), BF16),
        pltpu.VMEM((views, 8 * planes, 24 * planes), BF16),
        pltpu.VMEM((views, 4 * rows, 12 * rows), BF16),
        pltpu.VMEM((views, 2 * cols, 2 * cols), BF16),
        pltpu.VMEM((views, planes, 3 * planes), BF16),
    ]
    made = call(functools.partial(weights_kernel, rows), outs, [], [taps], [], "weights", 10**7)
    return made[:3], made[3:]


def stacked(pieces):
    columns = []
    for piece in pieces:
        high, low = split(piece)
        columns.append(jnp.concatenate([high, low, high], axis=0))
    return jnp.concatenate(columns, axis=1)


def two_groups(rows_ref, wx, wz, planes, cols):
    both = dot(rows_ref.reshape(planes * 16, 2 * cols), wx)
    value = (both[:, :cols] + both[:, cols:]).reshape(planes, 16, cols)
    return dot(wz, stacked([value[:, 8 * g : 8 * g + 8, :].reshape(planes * 8, cols) for g in range(2)]))


def row_pairs(rows_ref, wx, wz, xs):
    planes, height, lanes = rows_ref.shape
    cols = lanes // 2
    both = dot(rows_ref.reshape(planes * height, lanes), wx)
    xs[...] = both[:, :cols] + both[:, cols:]
    for y in range(0, height, 2):
        yield y, dot(wz, stacked([xs[pl.ds(y + j, planes, stride=height), :] for j in range(2)]))


def forward_rows(parity, far_before, near, own, far_after, wy, ys):
    planes, rows, cols = far_before.shape
    views = ys.shape[0]
    height = 3 * rows
    side = parity[0]

    def plane(z):
        return jnp.concatenate(
            [far_before[z], near[1 - side, z], own[z * rows : (z + 1) * rows, :], near[side, z], far_after[z]], axis=0
        )

    for z in range(0, planes, 2):
        result = dot(wy[...], stacked([plane(z), plane(z + 1)]))
        high, low = split(result)
        for j in range(2):
            for v in range(views):
                there = (slice(v * height, (v + 1) * height), slice(j * cols, (j + 1) * cols))
                ys[v, z + j, :, :cols] = high[there]
                ys[v, z + j, :, cols:] = low[there]


def forward_view(ys, wx, wz, out):
    planes, height, lanes = ys.shape
    cols = lanes // 2
    for pair in range(height // 16):
        result = two_groups(ys[:, 16 * pair : 16 * pair + 16, :], wx, wz, planes, cols)
        for j in range(2):
            at = 16 * pair + 8 * j
            out[:, at : at + 8, :] = result[:, j * cols : (j + 1) * cols].reshape(planes, 8, cols)


def adjoint_views(blurred, before, raw, after, wy, wx, wz, ya, xs, acc):
    _, planes, rows, cols = raw.shape

    def quotient(v, z):
        counts = jnp.concatenate([before[v, z], raw[v, z], after[v, z]], axis=0)
        below = jnp.maximum(blurred[v, z], TINY)
        inverse = pl.reciprocal(below, approx=True)
        return counts * (inverse * (2.0 - below * inverse))

    for v in range(STEP):
        for z in range(0, planes, 4):
            parts = []
            for first in (z, z + 2):
                parts += split(jnp.concatenate([quotient(v, first), quotient(v, first + 1)], axis=1))
            both = dot(wy[v], jnp.concatenate(parts, axis=0))
            high, low = split(both[: 2 * rows] + both[2 * rows :])
            for j in range(4):
                here = (slice(j // 2 * rows, (j // 2 + 1) * rows), slice(j % 2 * cols, (j % 2 + 1) * cols))
                ya[v, z + j, :, :cols] = high[here]
                ya[v, z + j, :, cols:] = low[here]
    for pair in range(rows // 16):
        chosen = slice(16 * pair, 16 * pair + 16)
        found = [row_pairs(ya[v, :, chosen, :], wx[v], wz[v], xs.at[v]) for v in range(STEP)]
        for results in zip(*found):
            at = 8 * pair + results[0][0] // 2
            acc[at] += sum(jnp.log(values) for _, values in results)


def updated(current, exponents, out):
    pairs, planes, lanes = exponents.shape
    cols = lanes // 2
    for y in range(2 * pairs):
        at = pl.ds(y, planes, stride=2 * pairs)
        half = slice((y % 2) * cols, (y % 2 + 1) * cols)
        out[at, :] = current[at, :] * jnp.exp(exponents[y // 2, :, half])


def each_step(steps, body):
    def run(step, _):
        body(step)
        return 0

    lax.fori_loop(0, steps, run, 0)


def forward_kernel(parity, wzs, far_before, near, own, far_after, wy, wx, wz, raw, wyx, out, sums, ys):
    views = ys.shape[0]
    forward_rows(parity, far_before, near, own, far_after, wy, ys)
    each_step(views, lambda v: forward_view(ys.at[v], wx[v], wz[v], out.at[v]))
    sums[...] = jnp.zeros_like(sums)
    for v in range(views):
        sums[v : v + 1, :] = jnp.sum(jnp.sum(raw[v], axis=0), axis=0, keepdims=True)
    weighted_sums(own, wzs, wyx, sums, sums.shape[0] // 3)


def weighted_sums(values, wzs, wyx, sums, at):
    planes, (_, rows, cols) = wzs.shape[1], wyx.shape
    for v in range(wyx.shape[0]):
        total = jnp.zeros((rows, cols), F32)
        for z in range(planes):
            total = total + wzs[v, z] * values[z * rows : (z + 1) * rows, :]
        sums[at + v : at + v + 1, :] = jnp.sum(total * wyx[v], axis=0, keepdims=True)


def first_adjoint_kernel(wzs, current, blurred, before, raw, after, wy, wx, wz, wyx, known, out, sums, ya, xs, acc):
    views = wyx.shape[0]
    acc[...] = jnp.zeros_like(acc)

    def step(i):
        chosen = pl.ds(STEP * i, STEP)
        fields = [ref.at[chosen] for ref in (blurred, before, raw, after, wy, wx, wz)]
        adjoint_views(*fields, ya, xs, acc)

    each_step(views // STEP, step)
    updated(current, acc[...] * (1.0 / views), out)
    sums[...] = known[...]
    weighted_sums(out, wzs, wyx, sums, 2 * sums.shape[0] // 3)


def iteration_kernel(
    parity, far_before, near, own, far_after, before, raw, after, wy, wx, wz, wya, wxa, wza, part, rest,
    out, ys, blurred, ya, xs, acc,
):
    views = ys.shape[0]
    acc[...] = jnp.zeros_like(acc)
    forward_rows(parity, far_before, near, own, far_after, wy, ys)

    def step(i):
        def one_view(j):
            v = STEP * i + j
            forward_view(ys.at[v], wx[v], wz[v], blurred.at[j])

        each_step(STEP, one_view)
        chosen = pl.ds(STEP * i, STEP)
        fields = [ref.at[chosen] for ref in (before, raw, after, wya, wxa, wza)]
        adjoint_views(blurred, *fields, ya, xs, acc)

    each_step(views // STEP, step)
    sums = jnp.sum(part[...] + rest[...], axis=1, keepdims=True)
    space = sums.shape[0] // 3
    total, first, second = (sums[i * space : i * space + views] for i in range(3))
    scale = jnp.sum(jnp.log(first / total) + jnp.log(second / total), axis=0, keepdims=True)
    updated(own, (acc[...] + scale[None]) * (1.0 / views), out)


def adjoint_scratch(planes, rows, cols):
    return [
        pltpu.VMEM((STEP, planes, rows, 2 * cols), BF16),
        pltpu.VMEM((STEP, planes * 16, cols), F32),
        pltpu.VMEM((rows // 2, planes, 2 * cols), F32),
    ]


def forward(parity, slabs, weights, raw, wzs, wyx):
    planes, rows, cols = slabs[0].shape
    views = raw.shape[0]
    slabs = [s.reshape(-1, cols) if i == 2 else s for i, s in enumerate(slabs)]
    outs = [pltpu.VMEM((views, planes, 3 * rows, cols), F32), pltpu.VMEM((24 * -(-views // 8), cols), F32)]
    scratch = [pltpu.VMEM((views, planes, 3 * rows, 2 * cols), BF16)]
    return call(forward_kernel, outs, [parity, wzs], [*slabs, *weights, raw, wyx], scratch, "forward", 10**10)


def first_adjoint(current, blurred, before, raw, after, weights, wzs, wyx, known):
    planes, rows, cols = current.shape
    current = current.reshape(planes * rows, cols)
    out, sums = call(
        first_adjoint_kernel,
        [pltpu.VMEM(current.shape, F32), pltpu.VMEM(known.shape, F32)],
        [wzs],
        [current, blurred, before, raw, after, *weights, wyx, known],
        adjoint_scratch(planes, rows, cols),
        "adjoint",
        10**10,
    )
    return out.reshape(planes, rows, cols), sums


def full_iteration(parity, slabs, before, raw, after, weights, adjoint_weights, part, rest):
    planes, rows, cols = slabs[0].shape
    views = raw.shape[0]
    slabs = [s.reshape(-1, cols) if i == 2 else s for i, s in enumerate(slabs)]
    scratch = [
        pltpu.VMEM((views, planes, 3 * rows, 2 * cols), BF16),
        pltpu.VMEM((STEP, planes, 3 * rows, cols), F32),
    ]
    return call(
        iteration_kernel,
        jax.ShapeDtypeStruct((planes * rows, cols), F32),
        [parity],
        [*slabs, before, raw, after, *weights, *adjoint_weights, part, rest],
        scratch + adjoint_scratch(planes, rows, cols),
        "iteration",
        2 * 10**10,
    ).reshape(planes, rows, cols)


def two_slabs_away(value, count):
    up = [(i, i + 2) for i in range(count - 2)]
    down = [(j, i) for i, j in up]
    return lax.ppermute(value, "slab", up), lax.ppermute(value, "slab", down)


def with_near(value, far_before, far_after, parity, count):
    swap = [(i, i + 1 - 2 * (i % 2)) for i in range(count)]
    passed = jnp.stack([value, jnp.where(parity[0] == 0, far_after, far_before)])
    near = lax.ppermute(passed, "slab", swap)
    return far_before, near, value, far_after


def tap_sums(taps, offset, extent, total):
    count = taps.shape[1]
    target = offset + jnp.arange(extent)[None, :] - jnp.arange(count)[:, None] + count // 2
    reach = jnp.where((target >= 0) & (target < total), 1.0, 0.0).astype(F32)
    return jnp.sum(taps[:, :, None] * reach[None], axis=1)


def per_device(estimate, raw, taps):
    views = raw.shape[0]
    planes, rows, cols = estimate.shape
    count = lax.axis_size("slab")
    assert rows >= taps.shape[2] // 2 and count & (count - 1) == 0
    up = [(i, i + 1) for i in range(count - 1)]
    down = [(j, i) for i, j in up]
    place = lax.axis_index("slab")
    parity = (place % 2).reshape(1)

    far = two_slabs_away(estimate, count)
    before = lax.ppermute(raw, "slab", up)
    after = lax.ppermute(raw, "slab", down)

    wzs = tap_sums(taps[:, 0], 0, planes, planes)
    wy_sums = tap_sums(taps[:, 1], place * rows, rows, count * rows)
    wx_sums = tap_sums(taps[:, 2], 0, cols, cols)
    wyx = wy_sums[:, :, None] * wx_sums[:, None, :]

    forward_weights, adjoint_weights = make_weights(taps, planes, rows, cols)

    slabs = with_near(estimate, *far, parity, count)
    blurred, known = forward(parity, slabs, forward_weights, raw, wzs, wyx)
    current, sums = first_adjoint(estimate, blurred, before, raw, after, adjoint_weights, wzs, wyx, known)

    far = two_slabs_away(current, count)
    bits = [1 << b for b in range(count.bit_length() - 1)]
    rounds = [bits[:1], bits[2:4] + [sum(bits[2:4])], *([b] for b in bits[4:]), bits[1:2]]
    for r, distances in enumerate(rounds):
        others = [lax.ppermute(sums, "slab", [(i, i ^ d) for i in range(count)]) for d in distances]
        if r == 1:
            *far, sums = lax.optimization_barrier((*far, sums + sum(others)))
        elif r < len(rounds) - 1:
            sums = sums + sum(others)
    slabs = with_near(current, *far, parity, count)
    return full_iteration(
        parity, slabs, before, raw, after, forward_weights, adjoint_weights, sums, others[0]
    )


def solution(mesh):
    placed = (P("blocks", "slab", None), P(None, "blocks", "slab", None), P())
    return jax.shard_map(
        per_device, mesh=mesh, in_specs=placed, out_specs=P("blocks", "slab", None), check_vma=False
    )
```

```python
import functools

import jax
import jax.numpy as jnp
import numpy as np
from jax import lax
from jax.experimental import pallas as pl
from jax.experimental.pallas import tpu as pltpu
from jax.sharding import PartitionSpec as P

F32 = jnp.float32
BF16 = jnp.bfloat16
VMEM = pltpu.MemorySpace.VMEM
SMEM = pltpu.MemorySpace.SMEM
FULL = pl.BlockSpec(memory_space=VMEM)
LIMIT = 30 * 1024 * 1024
TINY = float(np.finfo(np.float32).tiny)


def split(value):
    high = value.astype(BF16)
    low = (value - high.astype(F32)).astype(BF16)
    return high, low


def dot(a, b):
    return jnp.dot(a, b, preferred_element_type=F32)


def placed_row(taps, lane_of_tap, width):
    count = taps.shape[1]
    tap = lax.broadcasted_iota(jnp.int32, (count, width), 0)
    lane = lax.broadcasted_iota(jnp.int32, (count, width), 1)
    onehot = jnp.where(lane == lane_of_tap(tap), 1.0, 0.0).astype(F32)
    return jnp.dot(taps, onehot, precision=lax.Precision.HIGHEST, preferred_element_type=F32)


def slanted(row, height):
    full = jnp.broadcast_to(row, (height, row.shape[1]))
    return pltpu.roll(full, 0, 1, stride=1, stride_axis=0)


def weights_kernel(rows, taps_ref, *outs):
    views, _, count = taps_ref.shape
    margin = count // 2
    for flip in (False, True):
        wy, wx, wz = outs[3 * flip : 3 * flip + 3]
        order = (lambda k: count - 1 - k) if flip else (lambda k: k)
        out_rows = rows if flip else 3 * rows
        in_rows = out_rows + 2 * rows
        planes = wz.shape[1] // (1 if flip else 8)
        cols = wx.shape[1] // 2
        row_y = placed_row(taps_ref[:, 1, :], lambda k: order(k) + rows - margin, 256)
        high = row_y.astype(BF16).astype(F32)
        low = row_y - high
        if flip:
            row_y = [part + pltpu.roll(part, in_rows, 1) for part in (high, low)]
        else:
            row_y = high + pltpu.roll(high, in_rows, 1) + pltpu.roll(low, 2 * in_rows, 1)
        row_x = placed_row(taps_ref[:, 2, :], lambda k: lax.rem(margin - order(k) + 2 * cols, 2 * cols), 2 * cols)
        apart = 1 if flip else 8
        width_z = 128 if flip else 16 * planes
        row_z = placed_row(
            taps_ref[:, 0, :], lambda k: lax.rem(apart * (order(k) - margin) + width_z, width_z), width_z
        )
        inside = lax.broadcasted_iota(jnp.int32, (planes, 128), 1) < planes
        for v in range(views):
            if flip:
                for j, row in enumerate(row_y):
                    wy[v, j * rows : (j + 1) * rows, :] = slanted(row[v : v + 1], rows)[:, : 2 * in_rows].astype(BF16)
            else:
                band = slanted(row_y[v : v + 1], out_rows)
                wy[v * out_rows : (v + 1) * out_rows, :] = band[:, : 3 * in_rows].astype(BF16)
            high, low = split(slanted(row_x[v : v + 1], cols)[:, :cols])
            wx[v, :cols, :cols] = high
            wx[v, cols:, :cols] = high
            wx[v, :cols, cols:] = low
            wx[v, cols:, cols:] = low
            if flip:
                band = jnp.where(inside, slanted(row_z[v : v + 1], planes), 0.0)
                high = band.astype(BF16).astype(F32)
                band = high + pltpu.roll(high, planes, 1) + pltpu.roll(band - high, 2 * planes, 1)
                wz[v] = band[:, : 3 * planes].astype(BF16)
            else:
                size = 8 * planes
                high, low = split(slanted(row_z[v : v + 1], size)[:, :size])
                wz[v, :, :size] = high
                wz[v, :, size : 2 * size] = high
                wz[v, :, 2 * size :] = low


def call(kernel, outs, smem, arrays, scratch, name, flops):
    arrays = [pltpu.with_memory_space_constraint(a, VMEM) for a in arrays]
    return pl.pallas_call(
        kernel,
        out_shape=outs,
        in_specs=[pl.BlockSpec(memory_space=SMEM)] * len(smem) + [FULL] * len(arrays),
        out_specs=jax.tree.map(lambda _: FULL, outs),
        scratch_shapes=scratch,
        compiler_params=pltpu.CompilerParams(vmem_limit_bytes=LIMIT),
        cost_estimate=pl.CostEstimate(flops=flops, bytes_accessed=10**7, transcendentals=10**5),
        name=name,
    )(*smem, *arrays)


def make_weights(taps, planes, rows, cols):
    views = taps.shape[0]
    outs = [
        pltpu.VMEM((views * 3 * rows, 15 * rows), BF16),
        pltpu.VMEM((views, 2 * cols, 2 * cols), BF16),
        pltpu.VMEM((views, 8 * planes, 24 * planes), BF16),
        pltpu.VMEM((views, 2 * rows, 6 * rows), BF16),
        pltpu.VMEM((views, 2 * cols, 2 * cols), BF16),
        pltpu.VMEM((views, planes, 3 * planes), BF16),
    ]
    made = call(functools.partial(weights_kernel, rows), outs, [], [taps], [], "weights", 10**7)
    return made[:3], made[3:]


def stacked(pieces):
    columns = []
    for piece in pieces:
        high, low = split(piece)
        columns.append(jnp.concatenate([high, low, high], axis=0))
    return jnp.concatenate(columns, axis=1)


def two_groups(rows_ref, wx, wz, planes, cols):
    both = dot(rows_ref.reshape(planes * 16, 2 * cols), wx)
    value = (both[:, :cols] + both[:, cols:]).reshape(planes, 16, cols)
    return dot(wz, stacked([value[:, 8 * g : 8 * g + 8, :].reshape(planes * 8, cols) for g in range(2)]))


def interleaved(*streams):
    keyed = [((i + 0.5) / len(s), n, piece) for n, s in enumerate(streams) for i, piece in enumerate(s)]
    for _, _, piece in sorted(keyed, key=lambda k: k[:2]):
        piece()


def along_x(rows_ref, wx, out):
    planes, height, lanes = rows_ref.shape
    cols, part = lanes // 2, planes // 4

    def piece(z):
        both = dot(rows_ref[z : z + part].reshape(part * height, lanes), wx[...])
        out[z * height : (z + part) * height, :] = both[:, :cols] + both[:, cols:]

    return [functools.partial(piece, z) for z in range(0, planes, part)]


def forward_rows(parity, far_before, near, own, far_after, wy, ys):
    planes, rows, cols = far_before.shape
    views = ys.shape[0]
    height = 3 * rows
    side = parity[0]

    def plane(z):
        return jnp.concatenate(
            [far_before[z], near[1 - side, z], own[z * rows : (z + 1) * rows, :], near[side, z], far_after[z]], axis=0
        )

    for z in range(0, planes, 2):
        result = dot(wy[...], stacked([plane(z), plane(z + 1)]))
        high, low = split(result)
        for j in range(2):
            for v in range(views):
                there = (slice(v * height, (v + 1) * height), slice(j * cols, (j + 1) * cols))
                ys[v, z + j, :, :cols] = high[there]
                ys[v, z + j, :, cols:] = low[there]


def forward_view(ys, wx, wz, out):
    planes, height, lanes = ys.shape
    cols = lanes // 2
    for pair in range(height // 16):
        result = two_groups(ys[:, 16 * pair : 16 * pair + 16, :], wx, wz, planes, cols)
        for j in range(2):
            at = 16 * pair + 8 * j
            out[:, at : at + 8, :] = result[:, j * cols : (j + 1) * cols].reshape(planes, 8, cols)


def forward_pieces(ys, wx, wz, xs, out):
    planes, height, lanes = ys.shape
    cols = lanes // 2

    def along_z(pair):
        value = xs[pair].reshape(planes, 16, cols)
        groups = [value[:, 8 * g : 8 * g + 8, :].reshape(planes * 8, cols) for g in range(2)]
        result = dot(wz[...], stacked(groups))
        for j in range(2):
            at = 16 * pair + 8 * j
            out[:, at : at + 8, :] = result[:, j * cols : (j + 1) * cols].reshape(planes, 8, cols)

    pieces = []
    for pair in range(height // 16):
        pieces += along_x(ys.at[:, 16 * pair : 16 * pair + 16, :], wx, xs.at[pair])
        pieces.append(functools.partial(along_z, pair))
    return pieces


def adjoint_rows(blurred, before, raw, after, wy, ya):
    planes, rows, cols = raw.shape

    def quotient(z):
        counts = jnp.concatenate([before[z], raw[z], after[z]], axis=0)
        return counts * pl.reciprocal(jnp.maximum(blurred[z], TINY), approx=True)

    def piece(z):
        high, low = split(jnp.concatenate([quotient(z), quotient(z + 1)], axis=1))
        both = dot(wy[...], jnp.concatenate([high, low], axis=0))
        high, low = split(both[:rows] + both[rows:])
        for j in range(2):
            ya[z + j, :, :cols] = high[:, j * cols : (j + 1) * cols]
            ya[z + j, :, cols:] = low[:, j * cols : (j + 1) * cols]

    return [functools.partial(piece, z) for z in range(0, planes, 2)]


def adjoint_logs(first, ya, wx, wz, xs, acc):
    planes, rows, lanes = ya.shape

    def piece(y):
        result = jnp.log(dot(wz[...], stacked([xs[pl.ds(y + j, planes, stride=rows), :] for j in range(2)])))
        acc[y // 2] = result if first else acc[y // 2] + result

    return along_x(ya, wx, xs) + [functools.partial(piece, y) for y in range(0, rows, 2)]


def updated(current, exponents, out):
    pairs, planes, lanes = exponents.shape
    cols = lanes // 2
    for y in range(2 * pairs):
        at = pl.ds(y, planes, stride=2 * pairs)
        half = slice((y % 2) * cols, (y % 2 + 1) * cols)
        out[at, :] = current[at, :] * jnp.exp(exponents[y // 2, :, half])


def each_step(steps, body):
    def run(step, _):
        body(step)
        return 0

    lax.fori_loop(0, steps, run, 0)


def forward_kernel(parity, wzs, far_before, near, own, far_after, wy, wx, wz, raw, wyx, out, sums, ys):
    views = ys.shape[0]
    forward_rows(parity, far_before, near, own, far_after, wy, ys)
    each_step(views, lambda v: forward_view(ys.at[v], wx[v], wz[v], out.at[v]))
    sums[...] = jnp.zeros_like(sums)
    for v in range(views):
        sums[v : v + 1, :] = jnp.sum(jnp.sum(raw[v], axis=0), axis=0, keepdims=True)
    weighted_sums(own, wzs, wyx, sums, sums.shape[0] // 3)


def weighted_sums(values, wzs, wyx, sums, at):
    planes, (_, rows, cols) = wzs.shape[1], wyx.shape
    for v in range(wyx.shape[0]):
        total = jnp.zeros((rows, cols), F32)
        for z in range(planes):
            total = total + wzs[v, z] * values[z * rows : (z + 1) * rows, :]
        sums[at + v : at + v + 1, :] = jnp.sum(total * wyx[v], axis=0, keepdims=True)


def first_adjoint_kernel(
    wzs, current, blurred, before, raw, after, wy, wx, wz, wyx, known, out, sums, ya, yb, xs, acc
):
    views = wyx.shape[0]

    def rows_of(v):
        fields = [ref.at[v] for ref in (blurred, before, raw, after, wy)] if v < views else None
        return adjoint_rows(*fields, (ya, yb)[v % 2]) if fields else []

    interleaved(rows_of(0))
    for v in range(views):
        logs = adjoint_logs(v == 0, (ya, yb)[v % 2], wx.at[v], wz.at[v], xs.at[v % 2], acc)
        interleaved(logs, rows_of(v + 1))
    updated(current, acc[...] * (1.0 / views), out)
    sums[...] = known[...]
    weighted_sums(out, wzs, wyx, sums, 2 * sums.shape[0] // 3)


def iteration_kernel(
    parity, far_before, near, own, far_after, before, raw, after, wy, wx, wz, wya, wxa, wza, part, rest,
    out, ys, xf, blurred_a, blurred_b, ya, yb, xs, acc,
):
    views = ys.shape[0]
    blurred = (blurred_a, blurred_b)
    forward_rows(parity, far_before, near, own, far_after, wy, ys)

    def forward_of(v):
        return forward_pieces(ys.at[v], wx.at[v], wz.at[v], xf, blurred[v % 2]) if v < views else []

    interleaved(forward_of(0))
    for v in range(views):
        fields = [ref.at[v] for ref in (before, raw, after, wya)]
        y = (ya, yb)[v % 2]
        steps = adjoint_rows(blurred[v % 2], *fields, y)
        steps += adjoint_logs(v == 0, y, wxa.at[v], wza.at[v], xs.at[v % 2], acc)
        interleaved(steps, forward_of(v + 1))
    sums = jnp.sum(part[...] + rest[...], axis=1, keepdims=True)
    space = sums.shape[0] // 3
    total, first, second = (sums[i * space : i * space + views] for i in range(3))
    scale = jnp.sum(jnp.log(first / total) + jnp.log(second / total), axis=0, keepdims=True)
    updated(own, (acc[...] + scale[None]) * (1.0 / views), out)


def adjoint_scratch(planes, rows, cols):
    return [
        pltpu.VMEM((planes, rows, 2 * cols), BF16),
        pltpu.VMEM((planes, rows, 2 * cols), BF16),
        pltpu.VMEM((2, planes * 16, cols), F32),
        pltpu.VMEM((rows // 2, planes, 2 * cols), F32),
    ]


def forward(parity, slabs, weights, raw, wzs, wyx):
    planes, rows, cols = slabs[0].shape
    views = raw.shape[0]
    slabs = [s.reshape(-1, cols) if i == 2 else s for i, s in enumerate(slabs)]
    outs = [pltpu.VMEM((views, planes, 3 * rows, cols), F32), pltpu.VMEM((24 * -(-views // 8), cols), F32)]
    scratch = [pltpu.VMEM((views, planes, 3 * rows, 2 * cols), BF16)]
    return call(forward_kernel, outs, [parity, wzs], [*slabs, *weights, raw, wyx], scratch, "forward", 10**10)


def first_adjoint(current, blurred, before, raw, after, weights, wzs, wyx, known):
    planes, rows, cols = current.shape
    current = current.reshape(planes * rows, cols)
    out, sums = call(
        first_adjoint_kernel,
        [pltpu.VMEM(current.shape, F32), pltpu.VMEM(known.shape, F32)],
        [wzs],
        [current, blurred, before, raw, after, *weights, wyx, known],
        adjoint_scratch(planes, rows, cols),
        "adjoint",
        10**10,
    )
    return out.reshape(planes, rows, cols), sums


def full_iteration(parity, slabs, before, raw, after, weights, adjoint_weights, part, rest):
    planes, rows, cols = slabs[0].shape
    views = raw.shape[0]
    slabs = [s.reshape(-1, cols) if i == 2 else s for i, s in enumerate(slabs)]
    scratch = [
        pltpu.VMEM((views, planes, 3 * rows, 2 * cols), BF16),
        pltpu.VMEM((3 * rows // 16, planes * 16, cols), F32),
        pltpu.VMEM((planes, 3 * rows, cols), F32),
        pltpu.VMEM((planes, 3 * rows, cols), F32),
    ]
    return call(
        iteration_kernel,
        jax.ShapeDtypeStruct((planes * rows, cols), F32),
        [parity],
        [*slabs, before, raw, after, *weights, *adjoint_weights, part, rest],
        scratch + adjoint_scratch(planes, rows, cols),
        "iteration",
        2 * 10**10,
    ).reshape(planes, rows, cols)


def two_slabs_away(value, count):
    up = [(i, i + 2) for i in range(count - 2)]
    down = [(j, i) for i, j in up]
    return lax.ppermute(value, "slab", up), lax.ppermute(value, "slab", down)


def with_near(value, far_before, far_after, parity, count):
    swap = [(i, i + 1 - 2 * (i % 2)) for i in range(count)]
    passed = jnp.stack([value, jnp.where(parity[0] == 0, far_after, far_before)])
    near = lax.ppermute(passed, "slab", swap)
    return far_before, near, value, far_after


def tap_sums(taps, offset, extent, total):
    count = taps.shape[1]
    target = offset + jnp.arange(extent)[None, :] - jnp.arange(count)[:, None] + count // 2
    reach = jnp.where((target >= 0) & (target < total), 1.0, 0.0).astype(F32)
    return jnp.sum(taps[:, :, None] * reach[None], axis=1)


def per_device(estimate, raw, taps):
    views = raw.shape[0]
    planes, rows, cols = estimate.shape
    count = lax.axis_size("slab")
    assert 16 == rows >= taps.shape[2] // 2 and count & (count - 1) == 0
    up = [(i, i + 1) for i in range(count - 1)]
    down = [(j, i) for i, j in up]
    place = lax.axis_index("slab")
    parity = (place % 2).reshape(1)

    far = two_slabs_away(estimate, count)
    before = lax.ppermute(raw, "slab", up)
    after = lax.ppermute(raw, "slab", down)

    wzs = tap_sums(taps[:, 0], 0, planes, planes)
    wy_sums = tap_sums(taps[:, 1], place * rows, rows, count * rows)
    wx_sums = tap_sums(taps[:, 2], 0, cols, cols)
    wyx = wy_sums[:, :, None] * wx_sums[:, None, :]

    forward_weights, adjoint_weights = make_weights(taps, planes, rows, cols)

    slabs = with_near(estimate, *far, parity, count)
    blurred, known = forward(parity, slabs, forward_weights, raw, wzs, wyx)
    current, sums = first_adjoint(estimate, blurred, before, raw, after, adjoint_weights, wzs, wyx, known)

    far = two_slabs_away(current, count)
    bits = [1 << b for b in range(count.bit_length() - 1)]
    rounds = [bits[:1], bits[2:4] + [sum(bits[2:4])], *([b] for b in bits[4:]), bits[1:2]]
    for r, distances in enumerate(rounds):
        others = [lax.ppermute(sums, "slab", [(i, i ^ d) for i in range(count)]) for d in distances]
        if r == 1:
            *far, sums = lax.optimization_barrier((*far, sums + sum(others)))
        elif r < len(rounds) - 1:
            sums = sums + sum(others)
    slabs = with_near(current, *far, parity, count)
    return full_iteration(
        parity, slabs, before, raw, after, forward_weights, adjoint_weights, sums, others[0]
    )


def solution(mesh):
    placed = (P("blocks", "slab", None), P(None, "blocks", "slab", None), P())
    return jax.shard_map(
        per_device, mesh=mesh, in_specs=placed, out_specs=P("blocks", "slab", None), check_vma=False
    )
```

```python
import functools

import jax
import jax.numpy as jnp
import numpy as np
from jax import lax
from jax.experimental import pallas as pl
from jax.experimental.pallas import tpu as pltpu
from jax.sharding import PartitionSpec as P

F32 = jnp.float32
BF16 = jnp.bfloat16
VMEM = pltpu.MemorySpace.VMEM
SMEM = pltpu.MemorySpace.SMEM
FULL = pl.BlockSpec(memory_space=VMEM)
LIMIT = 30 * 1024 * 1024
TINY = float(np.finfo(np.float32).tiny)


def split(value):
    high = value.astype(BF16)
    low = (value - high.astype(F32)).astype(BF16)
    return high, low


def dot(a, b):
    return jnp.dot(a, b, preferred_element_type=F32)


def placed_row(taps, lane_of_tap, width):
    count = taps.shape[1]
    tap = lax.broadcasted_iota(jnp.int32, (count, width), 0)
    lane = lax.broadcasted_iota(jnp.int32, (count, width), 1)
    onehot = jnp.where(lane == lane_of_tap(tap), 1.0, 0.0).astype(F32)
    return jnp.dot(taps, onehot, precision=lax.Precision.HIGHEST, preferred_element_type=F32)


def slanted(row, height):
    full = jnp.broadcast_to(row, (height, row.shape[1]))
    return pltpu.roll(full, 0, 1, stride=1, stride_axis=0)


def weights_kernel(rows, taps_ref, *outs):
    views, _, count = taps_ref.shape
    margin = count // 2
    for flip in (False, True):
        wy, wx, wz = outs[3 * flip : 3 * flip + 3]
        order = (lambda k: count - 1 - k) if flip else (lambda k: k)
        out_rows = rows if flip else 3 * rows
        in_rows = out_rows + 2 * rows
        planes = wz.shape[1] // (1 if flip else 8)
        cols = wx.shape[1] // 2
        row_y = placed_row(taps_ref[:, 1, :], lambda k: order(k) + rows - margin, 256)
        high = row_y.astype(BF16).astype(F32)
        low = row_y - high
        if flip:
            row_y = [part + pltpu.roll(part, in_rows, 1) for part in (high, low)]
        else:
            row_y = high + pltpu.roll(high, in_rows, 1) + pltpu.roll(low, 2 * in_rows, 1)
        row_x = placed_row(taps_ref[:, 2, :], lambda k: lax.rem(margin - order(k) + 2 * cols, 2 * cols), 2 * cols)
        apart = 1 if flip else 8
        width_z = 128 if flip else 16 * planes
        row_z = placed_row(
            taps_ref[:, 0, :], lambda k: lax.rem(apart * (order(k) - margin) + width_z, width_z), width_z
        )
        inside = lax.broadcasted_iota(jnp.int32, (planes, 128), 1) < planes
        for v in range(views):
            if flip:
                for j, row in enumerate(row_y):
                    wy[v, j * rows : (j + 1) * rows, :] = slanted(row[v : v + 1], rows)[:, : 2 * in_rows].astype(BF16)
            else:
                band = slanted(row_y[v : v + 1], out_rows)
                wy[v * out_rows : (v + 1) * out_rows, :] = band[:, : 3 * in_rows].astype(BF16)
            high, low = split(slanted(row_x[v : v + 1], cols)[:, :cols])
            wx[v, :cols, :cols] = high
            wx[v, cols:, :cols] = high
            wx[v, :cols, cols:] = low
            wx[v, cols:, cols:] = low
            if flip:
                band = jnp.where(inside, slanted(row_z[v : v + 1], planes), 0.0)
                high = band.astype(BF16).astype(F32)
                band = high + pltpu.roll(high, planes, 1) + pltpu.roll(band - high, 2 * planes, 1)
                wz[v] = band[:, : 3 * planes].astype(BF16)
            else:
                size = 8 * planes
                high, low = split(slanted(row_z[v : v + 1], size)[:, :size])
                wz[v, :, :size] = high
                wz[v, :, size : 2 * size] = high
                wz[v, :, 2 * size :] = low


def call(kernel, outs, smem, arrays, scratch, name, flops):
    arrays = [pltpu.with_memory_space_constraint(a, VMEM) for a in arrays]
    return pl.pallas_call(
        kernel,
        out_shape=outs,
        in_specs=[pl.BlockSpec(memory_space=SMEM)] * len(smem) + [FULL] * len(arrays),
        out_specs=jax.tree.map(lambda _: FULL, outs),
        scratch_shapes=scratch,
        compiler_params=pltpu.CompilerParams(vmem_limit_bytes=LIMIT),
        cost_estimate=pl.CostEstimate(flops=flops, bytes_accessed=10**7, transcendentals=10**5),
        name=name,
    )(*smem, *arrays)


def make_weights(taps, planes, rows, cols):
    views = taps.shape[0]
    outs = [
        pltpu.VMEM((views * 3 * rows, 15 * rows), BF16),
        pltpu.VMEM((views, 2 * cols, 2 * cols), BF16),
        pltpu.VMEM((views, 8 * planes, 24 * planes), BF16),
        pltpu.VMEM((views, 2 * rows, 6 * rows), BF16),
        pltpu.VMEM((views, 2 * cols, 2 * cols), BF16),
        pltpu.VMEM((views, planes, 3 * planes), BF16),
    ]
    made = call(functools.partial(weights_kernel, rows), outs, [], [taps], [], "weights", 10**7)
    return made[:3], made[3:]


def stacked(pieces):
    columns = []
    for piece in pieces:
        high, low = split(piece)
        columns.append(jnp.concatenate([high, low, high], axis=0))
    return jnp.concatenate(columns, axis=1)


def two_groups(rows_ref, wx, wz, planes, cols):
    both = dot(rows_ref.reshape(planes * 16, 2 * cols), wx)
    value = (both[:, :cols] + both[:, cols:]).reshape(planes, 16, cols)
    return dot(wz, stacked([value[:, 8 * g : 8 * g + 8, :].reshape(planes * 8, cols) for g in range(2)]))


def interleaved(*streams):
    keyed = [((i + 0.5) / len(s), n, piece) for n, s in enumerate(streams) for i, piece in enumerate(s)]
    for _, _, piece in sorted(keyed, key=lambda k: k[:2]):
        piece()


def along_x(rows_ref, wx, out):
    planes, height, lanes = rows_ref.shape
    cols, part = lanes // 2, planes // 4

    def piece(z):
        both = dot(rows_ref[z : z + part].reshape(part * height, lanes), wx[...])
        out[z * height : (z + part) * height, :] = both[:, :cols] + both[:, cols:]

    return [functools.partial(piece, z) for z in range(0, planes, part)]


def forward_rows(parity, far_before, near, own, far_after, wy, ys):
    planes, rows, cols = far_before.shape
    views = ys.shape[0]
    height = 3 * rows
    side = parity[0]

    def plane(z):
        return jnp.concatenate(
            [far_before[z], near[1 - side, z], own[pl.ds(z * rows, rows), :], near[side, z], far_after[z]], axis=0
        )

    def some_planes(start, _):
        for z in range(0, 8, 2):
            at = 8 * start + z
            high, low = split(dot(wy[...], stacked([plane(at), plane(at + 1)])))
            for j in range(2):
                for v in range(views):
                    there = (slice(v * height, (v + 1) * height), slice(j * cols, (j + 1) * cols))
                    ys[v, at + j, :, :cols] = high[there]
                    ys[v, at + j, :, cols:] = low[there]
        return 0

    lax.fori_loop(0, planes // 8, some_planes, 0)


def forward_view(ys, wx, wz, out):
    planes, height, lanes = ys.shape
    cols = lanes // 2
    for pair in range(height // 16):
        result = two_groups(ys[:, 16 * pair : 16 * pair + 16, :], wx, wz, planes, cols)
        for j in range(2):
            at = 16 * pair + 8 * j
            out[:, at : at + 8, :] = result[:, j * cols : (j + 1) * cols].reshape(planes, 8, cols)


def adjoint_rows(blurred, before, raw, after, wy, ya):
    planes, rows, cols = raw.shape

    def quotient(z):
        counts = jnp.concatenate([before[z], raw[z], after[z]], axis=0)
        return counts * pl.reciprocal(jnp.maximum(blurred[z], TINY), approx=True)

    def piece(z):
        high, low = split(jnp.concatenate([quotient(z), quotient(z + 1)], axis=1))
        both = dot(wy[...], jnp.concatenate([high, low], axis=0))
        high, low = split(both[:rows] + both[rows:])
        for j in range(2):
            ya[z + j, :, :cols] = high[:, j * cols : (j + 1) * cols]
            ya[z + j, :, cols:] = low[:, j * cols : (j + 1) * cols]

    return [functools.partial(piece, z) for z in range(0, planes, 2)]


def adjoint_logs(first, ya, wx, wz, xs, acc):
    planes, rows, lanes = ya.shape

    def piece(y):
        result = jnp.log(dot(wz[...], stacked([xs[pl.ds(y + j, planes, stride=rows), :] for j in range(2)])))
        acc[y // 2] = result if first else acc[y // 2] + result

    return along_x(ya, wx, xs) + [functools.partial(piece, y) for y in range(0, rows, 2)]


def updated(current, exponents, out):
    pairs, planes, lanes = exponents.shape
    cols = lanes // 2
    for y in range(2 * pairs):
        at = pl.ds(y, planes, stride=2 * pairs)
        half = slice((y % 2) * cols, (y % 2 + 1) * cols)
        out[at, :] = current[at, :] * jnp.exp(exponents[y // 2, :, half])


def each_step(steps, body):
    def run(step, _):
        body(step)
        return 0

    lax.fori_loop(0, steps, run, 0)


def forward_kernel(parity, wzs, far_before, near, own, far_after, wy, wx, wz, raw, wyx, out, sums, ys):
    views = ys.shape[0]
    forward_rows(parity, far_before, near, own, far_after, wy, ys)
    each_step(views, lambda v: forward_view(ys.at[v], wx[v], wz[v], out.at[v]))
    sums[...] = jnp.zeros_like(sums)
    for v in range(views):
        sums[v : v + 1, :] = jnp.sum(jnp.sum(raw[v], axis=0), axis=0, keepdims=True)
    weighted_sums(own, wzs, wyx, sums, sums.shape[0] // 3)


def weighted_sums(values, wzs, wyx, sums, at):
    planes, (_, rows, cols) = wzs.shape[1], wyx.shape
    for v in range(wyx.shape[0]):
        total = jnp.zeros((rows, cols), F32)
        for z in range(planes):
            total = total + wzs[v, z] * values[z * rows : (z + 1) * rows, :]
        sums[at + v : at + v + 1, :] = jnp.sum(total * wyx[v], axis=0, keepdims=True)


def adjoint_all(blurred, before, raw, after, wy, wx, wz, ya, yb, xs, acc):
    views = raw.shape[0]

    def rows_of(v):
        fields = [ref.at[v] for ref in (blurred, before, raw, after, wy)] if v < views else None
        return adjoint_rows(*fields, (ya, yb)[v % 2]) if fields else []

    interleaved(rows_of(0))
    for v in range(views):
        logs = adjoint_logs(v == 0, (ya, yb)[v % 2], wx.at[v], wz.at[v], xs.at[v % 2], acc)
        interleaved(logs, rows_of(v + 1))


def first_adjoint_kernel(
    wzs, current, blurred, before, raw, after, wy, wx, wz, wyx, known, out, sums, ya, yb, xs, acc
):
    adjoint_all(blurred, before, raw, after, wy, wx, wz, ya, yb, xs, acc)
    updated(current, acc[...] * (1.0 / raw.shape[0]), out)
    sums[...] = known[...]
    weighted_sums(out, wzs, wyx, sums, 2 * sums.shape[0] // 3)


def iteration_kernel(
    parity, far_before, near, own, far_after, before, raw, after, wy, wx, wz, wya, wxa, wza, part, rest,
    out, ys, blurred, ya, yb, xs, acc,
):
    views = ys.shape[0]
    forward_rows(parity, far_before, near, own, far_after, wy, ys)
    each_step(views, lambda v: forward_view(ys.at[v], wx[v], wz[v], blurred.at[v]))
    adjoint_all(blurred, before, raw, after, wya, wxa, wza, ya, yb, xs, acc)
    sums = jnp.sum(part[...] + rest[...], axis=1, keepdims=True)
    space = sums.shape[0] // 3
    total, first, second = (sums[i * space : i * space + views] for i in range(3))
    scale = jnp.sum(jnp.log(first / total) + jnp.log(second / total), axis=0, keepdims=True)
    updated(own, (acc[...] + scale[None]) * (1.0 / views), out)


def adjoint_scratch(planes, rows, cols):
    return [
        pltpu.VMEM((planes, rows, 2 * cols), BF16),
        pltpu.VMEM((planes, rows, 2 * cols), BF16),
        pltpu.VMEM((2, planes * 16, cols), F32),
        pltpu.VMEM((rows // 2, planes, 2 * cols), F32),
    ]


def forward(parity, slabs, weights, raw, wzs, wyx):
    planes, rows, cols = slabs[0].shape
    views = raw.shape[0]
    slabs = [s.reshape(-1, cols) if i == 2 else s for i, s in enumerate(slabs)]
    outs = [pltpu.VMEM((views, planes, 3 * rows, cols), F32), pltpu.VMEM((24 * -(-views // 8), cols), F32)]
    scratch = [pltpu.VMEM((views, planes, 3 * rows, 2 * cols), BF16)]
    return call(forward_kernel, outs, [parity, wzs], [*slabs, *weights, raw, wyx], scratch, "forward", 10**10)


def first_adjoint(current, blurred, before, raw, after, weights, wzs, wyx, known):
    planes, rows, cols = current.shape
    current = current.reshape(planes * rows, cols)
    out, sums = call(
        first_adjoint_kernel,
        [pltpu.VMEM(current.shape, F32), pltpu.VMEM(known.shape, F32)],
        [wzs],
        [current, blurred, before, raw, after, *weights, wyx, known],
        adjoint_scratch(planes, rows, cols),
        "adjoint",
        10**10,
    )
    return out.reshape(planes, rows, cols), sums


def full_iteration(parity, slabs, before, raw, after, weights, adjoint_weights, part, rest):
    planes, rows, cols = slabs[0].shape
    views = raw.shape[0]
    slabs = [s.reshape(-1, cols) if i == 2 else s for i, s in enumerate(slabs)]
    scratch = [
        pltpu.VMEM((views, planes, 3 * rows, 2 * cols), BF16),
        pltpu.VMEM((views, planes, 3 * rows, cols), F32),
    ]
    return call(
        iteration_kernel,
        jax.ShapeDtypeStruct((planes * rows, cols), F32),
        [parity],
        [*slabs, before, raw, after, *weights, *adjoint_weights, part, rest],
        scratch + adjoint_scratch(planes, rows, cols),
        "iteration",
        2 * 10**10,
    ).reshape(planes, rows, cols)


def two_slabs_away(value, count):
    up = [(i, i + 2) for i in range(count - 2)]
    down = [(j, i) for i, j in up]
    return lax.ppermute(value, "slab", up), lax.ppermute(value, "slab", down)


def with_near(value, far_before, far_after, parity, count):
    swap = [(i, i + 1 - 2 * (i % 2)) for i in range(count)]
    passed = jnp.stack([value, jnp.where(parity[0] == 0, far_after, far_before)])
    near = lax.ppermute(passed, "slab", swap)
    return far_before, near, value, far_after


def tap_sums(taps, offset, extent, total):
    count = taps.shape[1]
    target = offset + jnp.arange(extent)[None, :] - jnp.arange(count)[:, None] + count // 2
    reach = jnp.where((target >= 0) & (target < total), 1.0, 0.0).astype(F32)
    return jnp.sum(taps[:, :, None] * reach[None], axis=1)


def per_device(estimate, raw, taps):
    views = raw.shape[0]
    planes, rows, cols = estimate.shape
    count = lax.axis_size("slab")
    assert 16 == rows >= taps.shape[2] // 2 and count & (count - 1) == 0
    up = [(i, i + 1) for i in range(count - 1)]
    down = [(j, i) for i, j in up]
    place = lax.axis_index("slab")
    parity = (place % 2).reshape(1)

    far = two_slabs_away(estimate, count)
    before = lax.ppermute(raw, "slab", up)
    after = lax.ppermute(raw, "slab", down)

    wzs = tap_sums(taps[:, 0], 0, planes, planes)
    wy_sums = tap_sums(taps[:, 1], place * rows, rows, count * rows)
    wx_sums = tap_sums(taps[:, 2], 0, cols, cols)
    wyx = wy_sums[:, :, None] * wx_sums[:, None, :]

    forward_weights, adjoint_weights = make_weights(taps, planes, rows, cols)

    slabs = with_near(estimate, *far, parity, count)
    blurred, known = forward(parity, slabs, forward_weights, raw, wzs, wyx)
    current, sums = first_adjoint(estimate, blurred, before, raw, after, adjoint_weights, wzs, wyx, known)

    far = two_slabs_away(current, count)
    bits = [1 << b for b in range(count.bit_length() - 1)]
    rounds = [bits[:1], bits[2:4] + [sum(bits[2:4])], *([b] for b in bits[4:]), bits[1:2]]
    for r, distances in enumerate(rounds):
        others = [lax.ppermute(sums, "slab", [(i, i ^ d) for i in range(count)]) for d in distances]
        if r == 1:
            *far, sums = lax.optimization_barrier((*far, sums + sum(others)))
        elif r < len(rounds) - 1:
            sums = sums + sum(others)
    slabs = with_near(current, *far, parity, count)
    return full_iteration(
        parity, slabs, before, raw, after, forward_weights, adjoint_weights, sums, others[0]
    )


def solution(mesh):
    placed = (P("blocks", "slab", None), P(None, "blocks", "slab", None), P())
    return jax.shard_map(
        per_device, mesh=mesh, in_specs=placed, out_specs=P("blocks", "slab", None), check_vma=False
    )
```

```python
import functools

import jax
import jax.numpy as jnp
import numpy as np
from jax import lax
from jax.experimental import pallas as pl
from jax.experimental.pallas import tpu as pltpu
from jax.sharding import PartitionSpec as P

F32 = jnp.float32
BF16 = jnp.bfloat16
VMEM = pltpu.MemorySpace.VMEM
SMEM = pltpu.MemorySpace.SMEM
FULL = pl.BlockSpec(memory_space=VMEM)
LIMIT = 30 * 1024 * 1024
WIDE = 4
TINY = float(np.finfo(np.float32).tiny)


def split(value):
    high = value.astype(BF16)
    low = (value - high.astype(F32)).astype(BF16)
    return high, low


def dot(a, b):
    return jnp.dot(a, b, preferred_element_type=F32)


def placed_row(taps, lane_of_tap, width):
    count = taps.shape[1]
    tap = lax.broadcasted_iota(jnp.int32, (count, width), 0)
    lane = lax.broadcasted_iota(jnp.int32, (count, width), 1)
    onehot = jnp.where(lane == lane_of_tap(tap), 1.0, 0.0).astype(F32)
    return jnp.dot(taps, onehot, precision=lax.Precision.HIGHEST, preferred_element_type=F32)


def slanted(row, height):
    full = jnp.broadcast_to(row, (height, row.shape[1]))
    return pltpu.roll(full, 0, 1, stride=1, stride_axis=0)


def weights_kernel(rows, taps_ref, *outs):
    views, _, count = taps_ref.shape
    margin = count // 2
    for flip in (False, True):
        wy, wx, wz = outs[3 * flip : 3 * flip + 3]
        order = (lambda k: count - 1 - k) if flip else (lambda k: k)
        out_rows = rows if flip else 3 * rows
        in_rows = out_rows + 2 * rows
        planes = wz.shape[1] // (1 if flip else 8)
        cols = wx.shape[1] // 2
        row_y = placed_row(taps_ref[:, 1, :], lambda k: order(k) + rows - margin, 256)
        high = row_y.astype(BF16).astype(F32)
        low = row_y - high
        if flip:
            row_y = [part + pltpu.roll(part, in_rows, 1) for part in (high, low)]
        else:
            row_y = high + pltpu.roll(high, in_rows, 1) + pltpu.roll(low, 2 * in_rows, 1)
        row_x = placed_row(taps_ref[:, 2, :], lambda k: lax.rem(margin - order(k) + 2 * cols, 2 * cols), 2 * cols)
        apart = 1 if flip else 8
        width_z = 128 if flip else 16 * planes
        row_z = placed_row(
            taps_ref[:, 0, :], lambda k: lax.rem(apart * (order(k) - margin) + width_z, width_z), width_z
        )
        inside = lax.broadcasted_iota(jnp.int32, (planes, 128), 1) < planes
        for v in range(views):
            if flip:
                for j, row in enumerate(row_y):
                    wy[v, j * rows : (j + 1) * rows, :] = slanted(row[v : v + 1], rows)[:, : 2 * in_rows].astype(BF16)
            else:
                band = slanted(row_y[v : v + 1], out_rows)
                wy[v * out_rows : (v + 1) * out_rows, :] = band[:, : 3 * in_rows].astype(BF16)
            high, low = split(slanted(row_x[v : v + 1], cols)[:, :cols])
            wx[v, :cols, :cols] = high
            wx[v, cols:, :cols] = high
            wx[v, :cols, cols:] = low
            wx[v, cols:, cols:] = low
            if flip:
                band = jnp.where(inside, slanted(row_z[v : v + 1], planes), 0.0)
                high = band.astype(BF16).astype(F32)
                band = high + pltpu.roll(high, planes, 1) + pltpu.roll(band - high, 2 * planes, 1)
                wz[v] = band[:, : 3 * planes].astype(BF16)
            else:
                size = 8 * planes
                high, low = split(slanted(row_z[v : v + 1], size)[:, :size])
                wz[v, :, :size] = high
                wz[v, :, size : 2 * size] = high
                wz[v, :, 2 * size :] = low


def call(kernel, outs, smem, arrays, scratch, name, flops):
    arrays = [pltpu.with_memory_space_constraint(a, VMEM) for a in arrays]
    return pl.pallas_call(
        kernel,
        out_shape=outs,
        in_specs=[pl.BlockSpec(memory_space=SMEM)] * len(smem) + [FULL] * len(arrays),
        out_specs=jax.tree.map(lambda _: FULL, outs),
        scratch_shapes=scratch,
        compiler_params=pltpu.CompilerParams(vmem_limit_bytes=LIMIT),
        cost_estimate=pl.CostEstimate(flops=flops, bytes_accessed=10**7, transcendentals=10**5),
        name=name,
    )(*smem, *arrays)


def make_weights(taps, planes, rows, cols):
    views = taps.shape[0]
    outs = [
        pltpu.VMEM((views * 3 * rows, 15 * rows), BF16),
        pltpu.VMEM((views, 2 * cols, 2 * cols), BF16),
        pltpu.VMEM((views, 8 * planes, 24 * planes), BF16),
        pltpu.VMEM((views, 2 * rows, 6 * rows), BF16),
        pltpu.VMEM((views, 2 * cols, 2 * cols), BF16),
        pltpu.VMEM((views, planes, 3 * planes), BF16),
    ]
    made = call(functools.partial(weights_kernel, rows), outs, [], [taps], [], "weights", 10**7)
    return made[:3], made[3:]


def stacked(pieces):
    columns = []
    for piece in pieces:
        high, low = split(piece)
        columns.append(jnp.concatenate([high, low, high], axis=0))
    return jnp.concatenate(columns, axis=1)


def interleaved(*streams):
    keyed = [((i + 0.5) / len(s), n, piece) for n, s in enumerate(streams) for i, piece in enumerate(s)]
    for _, _, piece in sorted(keyed, key=lambda k: k[:2]):
        piece()


def along_x(rows_ref, wx, out):
    planes, height, lanes = rows_ref.shape
    cols, part = lanes // 2, planes // 4

    def piece(z):
        both = dot(rows_ref[z : z + part].reshape(part * height, lanes), wx[...])
        out[z * height : (z + part) * height, :] = both[:, :cols] + both[:, cols:]

    return [functools.partial(piece, z) for z in range(0, planes, part)]


def forward_rows(parity, far_before, near, own, far_after, wy, ys):
    planes, rows, cols = far_before.shape
    views = ys.shape[0]
    height = 3 * rows
    side = parity[0]

    def plane(z):
        return jnp.concatenate(
            [far_before[z], near[1 - side, z], own[pl.ds(z * rows, rows), :], near[side, z], far_after[z]], axis=0
        )

    for z in range(0, planes, 2):
        high, low = split(dot(wy[...], stacked([plane(z), plane(z + 1)])))
        for j in range(2):
            for v in range(views):
                there = (slice(v * height, (v + 1) * height), slice(j * cols, (j + 1) * cols))
                ys[v, z + j, :, :cols] = high[there]
                ys[v, z + j, :, cols:] = low[there]


def forward_view(ys, wx, wz, out):
    planes, height, lanes = ys.shape
    cols = lanes // 2
    groups = []
    for pair in range(height // 16):
        rows_in = ys[:, 16 * pair : 16 * pair + 16, :].reshape(planes * 16, lanes)
        both = dot(rows_in, wx)
        value = (both[:, :cols] + both[:, cols:]).reshape(planes, 16, cols)
        groups += [value[:, 8 * g : 8 * g + 8, :].reshape(planes * 8, cols) for g in range(2)]
    result = dot(wz, stacked(groups))
    for g in range(len(groups)):
        out[:, 8 * g : 8 * g + 8, :] = result[:, g * cols : (g + 1) * cols].reshape(planes, 8, cols)


def adjoint_rows(blurred, before, raw, after, wy, ya):
    planes, rows, cols = raw.shape

    def quotient(z):
        counts = jnp.concatenate([before[z], raw[z], after[z]], axis=0)
        return counts * pl.reciprocal(jnp.maximum(blurred[z], TINY), approx=True)

    def piece(z):
        high, low = split(jnp.concatenate([quotient(z + j) for j in range(WIDE)], axis=1))
        both = dot(wy[...], jnp.concatenate([high, low], axis=0))
        high, low = split(both[:rows] + both[rows:])
        for j in range(WIDE):
            ya[z + j, :, :cols] = high[:, j * cols : (j + 1) * cols]
            ya[z + j, :, cols:] = low[:, j * cols : (j + 1) * cols]

    return [functools.partial(piece, z) for z in range(0, planes, WIDE)]


def adjoint_logs(first, ya, wx, wz, xs, acc):
    planes, rows, lanes = ya.shape

    def piece(y):
        values = stacked([xs[pl.ds(y + j, planes, stride=rows), :] for j in range(WIDE)])
        result = jnp.log(dot(wz[...], values))
        acc[y // WIDE] = result if first else acc[y // WIDE] + result

    return along_x(ya, wx, xs) + [functools.partial(piece, y) for y in range(0, rows, WIDE)]


def updated(current, exponents, out):
    count, planes, lanes = exponents.shape
    cols, rows = lanes // WIDE, count * WIDE
    for y in range(rows):
        at = pl.ds(y, planes, stride=rows)
        part = slice((y % WIDE) * cols, (y % WIDE + 1) * cols)
        out[at, :] = current[at, :] * jnp.exp(exponents[y // WIDE, :, part])


def each_step(steps, body):
    def run(step, _):
        body(step)
        return 0

    lax.fori_loop(0, steps, run, 0)


def forward_kernel(parity, wzs, far_before, near, own, far_after, wy, wx, wz, raw, wyx, out, sums, ys):
    views = ys.shape[0]
    forward_rows(parity, far_before, near, own, far_after, wy, ys)
    each_step(views, lambda v: forward_view(ys.at[v], wx[v], wz[v], out.at[v]))
    sums[...] = jnp.zeros_like(sums)
    for v in range(views):
        sums[v : v + 1, :] = jnp.sum(jnp.sum(raw[v], axis=0), axis=0, keepdims=True)
    weighted_sums(own, wzs, wyx, sums, sums.shape[0] // 3)


def weighted_sums(values, wzs, wyx, sums, at):
    planes, (_, rows, cols) = wzs.shape[1], wyx.shape
    for v in range(wyx.shape[0]):
        total = jnp.zeros((rows, cols), F32)
        for z in range(planes):
            total = total + wzs[v, z] * values[z * rows : (z + 1) * rows, :]
        sums[at + v : at + v + 1, :] = jnp.sum(total * wyx[v], axis=0, keepdims=True)


def adjoint_all(blurred, before, raw, after, wy, wx, wz, ya, yb, xs, acc):
    views = raw.shape[0]

    def rows_of(v):
        fields = [ref.at[v] for ref in (blurred, before, raw, after, wy)] if v < views else None
        return adjoint_rows(*fields, (ya, yb)[v % 2]) if fields else []

    interleaved(rows_of(0))
    for v in range(views):
        logs = adjoint_logs(v == 0, (ya, yb)[v % 2], wx.at[v], wz.at[v], xs.at[v % 2], acc)
        interleaved(logs, rows_of(v + 1))


def first_adjoint_kernel(
    wzs, current, blurred, before, raw, after, wy, wx, wz, wyx, known, out, sums, ya, yb, xs, acc
):
    adjoint_all(blurred, before, raw, after, wy, wx, wz, ya, yb, xs, acc)
    updated(current, acc[...] * (1.0 / raw.shape[0]), out)
    sums[...] = known[...]
    weighted_sums(out, wzs, wyx, sums, 2 * sums.shape[0] // 3)


def iteration_kernel(
    parity, far_before, near, own, far_after, before, raw, after, wy, wx, wz, wya, wxa, wza, part, rest,
    out, ys, blurred, ya, yb, xs, acc,
):
    views = ys.shape[0]
    forward_rows(parity, far_before, near, own, far_after, wy, ys)
    each_step(views, lambda v: forward_view(ys.at[v], wx[v], wz[v], blurred.at[v]))
    adjoint_all(blurred, before, raw, after, wya, wxa, wza, ya, yb, xs, acc)
    sums = jnp.sum(part[...] + rest[...], axis=1, keepdims=True)
    space = sums.shape[0] // 3
    total, first, second = (sums[i * space : i * space + views] for i in range(3))
    scale = jnp.sum(jnp.log(first / total) + jnp.log(second / total), axis=0, keepdims=True)
    updated(own, (acc[...] + scale[None]) * (1.0 / views), out)


def adjoint_scratch(planes, rows, cols):
    return [
        pltpu.VMEM((planes, rows, 2 * cols), BF16),
        pltpu.VMEM((planes, rows, 2 * cols), BF16),
        pltpu.VMEM((2, planes * 16, cols), F32),
        pltpu.VMEM((rows // WIDE, planes, WIDE * cols), F32),
    ]


def forward(parity, slabs, weights, raw, wzs, wyx):
    planes, rows, cols = slabs[0].shape
    views = raw.shape[0]
    slabs = [s.reshape(-1, cols) if i == 2 else s for i, s in enumerate(slabs)]
    outs = [pltpu.VMEM((views, planes, 3 * rows, cols), F32), pltpu.VMEM((24 * -(-views // 8), cols), F32)]
    scratch = [pltpu.VMEM((views, planes, 3 * rows, 2 * cols), BF16)]
    return call(forward_kernel, outs, [parity, wzs], [*slabs, *weights, raw, wyx], scratch, "forward", 10**10)


def first_adjoint(current, blurred, before, raw, after, weights, wzs, wyx, known):
    planes, rows, cols = current.shape
    current = current.reshape(planes * rows, cols)
    out, sums = call(
        first_adjoint_kernel,
        [pltpu.VMEM(current.shape, F32), pltpu.VMEM(known.shape, F32)],
        [wzs],
        [current, blurred, before, raw, after, *weights, wyx, known],
        adjoint_scratch(planes, rows, cols),
        "adjoint",
        10**10,
    )
    return out.reshape(planes, rows, cols), sums


def full_iteration(parity, slabs, before, raw, after, weights, adjoint_weights, part, rest):
    planes, rows, cols = slabs[0].shape
    views = raw.shape[0]
    slabs = [s.reshape(-1, cols) if i == 2 else s for i, s in enumerate(slabs)]
    scratch = [
        pltpu.VMEM((views, planes, 3 * rows, 2 * cols), BF16),
        pltpu.VMEM((views, planes, 3 * rows, cols), F32),
    ]
    return call(
        iteration_kernel,
        jax.ShapeDtypeStruct((planes * rows, cols), F32),
        [parity],
        [*slabs, before, raw, after, *weights, *adjoint_weights, part, rest],
        scratch + adjoint_scratch(planes, rows, cols),
        "iteration",
        2 * 10**10,
    ).reshape(planes, rows, cols)


def two_slabs_away(value, count):
    up = [(i, i + 2) for i in range(count - 2)]
    down = [(j, i) for i, j in up]
    return lax.ppermute(value, "slab", up), lax.ppermute(value, "slab", down)


def with_near(value, far_before, far_after, parity, count):
    swap = [(i, i + 1 - 2 * (i % 2)) for i in range(count)]
    passed = jnp.stack([value, jnp.where(parity[0] == 0, far_after, far_before)])
    near = lax.ppermute(passed, "slab", swap)
    return far_before, near, value, far_after


def tap_sums(taps, offset, extent, total):
    count = taps.shape[1]
    target = offset + jnp.arange(extent)[None, :] - jnp.arange(count)[:, None] + count // 2
    reach = jnp.where((target >= 0) & (target < total), 1.0, 0.0).astype(F32)
    return jnp.sum(taps[:, :, None] * reach[None], axis=1)


def per_device(estimate, raw, taps):
    views = raw.shape[0]
    planes, rows, cols = estimate.shape
    count = lax.axis_size("slab")
    assert 16 == rows >= taps.shape[2] // 2 and count & (count - 1) == 0
    up = [(i, i + 1) for i in range(count - 1)]
    down = [(j, i) for i, j in up]
    place = lax.axis_index("slab")
    parity = (place % 2).reshape(1)

    far = two_slabs_away(estimate, count)
    before = lax.ppermute(raw, "slab", up)
    after = lax.ppermute(raw, "slab", down)

    wzs = tap_sums(taps[:, 0], 0, planes, planes)
    wy_sums = tap_sums(taps[:, 1], place * rows, rows, count * rows)
    wx_sums = tap_sums(taps[:, 2], 0, cols, cols)
    wyx = wy_sums[:, :, None] * wx_sums[:, None, :]

    forward_weights, adjoint_weights = make_weights(taps, planes, rows, cols)

    slabs = with_near(estimate, *far, parity, count)
    blurred, known = forward(parity, slabs, forward_weights, raw, wzs, wyx)
    current, sums = first_adjoint(estimate, blurred, before, raw, after, adjoint_weights, wzs, wyx, known)

    far = two_slabs_away(current, count)
    bits = [1 << b for b in range(count.bit_length() - 1)]
    rounds = [bits[:1], bits[2:4] + [sum(bits[2:4])], *([b] for b in bits[4:]), bits[1:2]]
    for r, distances in enumerate(rounds):
        others = [lax.ppermute(sums, "slab", [(i, i ^ d) for i in range(count)]) for d in distances]
        if r == 1:
            *far, sums = lax.optimization_barrier((*far, sums + sum(others)))
        elif r < len(rounds) - 1:
            sums = sums + sum(others)
    slabs = with_near(current, *far, parity, count)
    return full_iteration(
        parity, slabs, before, raw, after, forward_weights, adjoint_weights, sums, others[0]
    )


def solution(mesh):
    placed = (P("blocks", "slab", None), P(None, "blocks", "slab", None), P())
    return jax.shard_map(
        per_device, mesh=mesh, in_specs=placed, out_specs=P("blocks", "slab", None), check_vma=False
    )
```

```python
import functools

import jax
import jax.numpy as jnp
import numpy as np
from jax import lax
from jax.experimental import pallas as pl
from jax.experimental.pallas import tpu as pltpu
from jax.sharding import PartitionSpec as P

F32 = jnp.float32
BF16 = jnp.bfloat16
VMEM = pltpu.MemorySpace.VMEM
SMEM = pltpu.MemorySpace.SMEM
FULL = pl.BlockSpec(memory_space=VMEM)
LIMIT = 30 * 1024 * 1024
WIDE = 4
TINY = float(np.finfo(np.float32).tiny)


def split(value):
    high = value.astype(BF16)
    low = (value - high.astype(F32)).astype(BF16)
    return high, low


def dot(a, b):
    return jnp.dot(a, b, preferred_element_type=F32)


def placed_row(taps, lane_of_tap, width):
    count = taps.shape[1]
    tap = lax.broadcasted_iota(jnp.int32, (count, width), 0)
    lane = lax.broadcasted_iota(jnp.int32, (count, width), 1)
    onehot = jnp.where(lane == lane_of_tap(tap), 1.0, 0.0).astype(F32)
    return jnp.dot(taps, onehot, precision=lax.Precision.HIGHEST, preferred_element_type=F32)


def slanted(row, height):
    full = jnp.broadcast_to(row, (height, row.shape[1]))
    return pltpu.roll(full, 0, 1, stride=1, stride_axis=0)


def weights_kernel(rows, taps_ref, *outs):
    views, _, count = taps_ref.shape
    margin = count // 2
    for flip in (False, True):
        wy, wx, wz = outs[3 * flip : 3 * flip + 3]
        order = (lambda k: count - 1 - k) if flip else (lambda k: k)
        out_rows = rows if flip else 3 * rows
        in_rows = out_rows + 2 * rows
        planes = wz.shape[1] // (1 if flip else 8)
        cols = wx.shape[1] // 2
        row_y = placed_row(taps_ref[:, 1, :], lambda k: order(k) + rows - margin, 256)
        high = row_y.astype(BF16).astype(F32)
        low = row_y - high
        if flip:
            row_y = (high, low)
        else:
            row_y = high + pltpu.roll(high, in_rows, 1) + pltpu.roll(low, 2 * in_rows, 1)
        row_x = placed_row(taps_ref[:, 2, :], lambda k: lax.rem(margin - order(k) + 2 * cols, 2 * cols), 2 * cols)
        apart = 1 if flip else 8
        width_z = 128 if flip else 16 * planes
        row_z = placed_row(
            taps_ref[:, 0, :], lambda k: lax.rem(apart * (order(k) - margin) + width_z, width_z), width_z
        )
        inside = lax.broadcasted_iota(jnp.int32, (planes, 128), 1) < planes
        for v in range(views):
            if flip:
                lane = lax.broadcasted_iota(jnp.int32, (rows, 256), 1)
                for j, row in enumerate(row_y):
                    band = slanted(row[v : v + 1], rows)
                    shifted = pltpu.roll(band, 256 - (rows - margin), 1)
                    band = jnp.where(lane < margin, shifted, jnp.where(lane < rows, 0.0, band))
                    band = band + pltpu.roll(band, in_rows, 1)
                    wy[v, j * rows : (j + 1) * rows, :] = band[:, : 2 * in_rows].astype(BF16)
            else:
                row = row_y[v : v + 1]
                band = jnp.concatenate(
                    [slanted(pltpu.roll(row, rows - margin, 1), rows), slanted(pltpu.roll(row, rows, 1), 2 * rows)]
                )
                wy[v * out_rows : (v + 1) * out_rows, :] = band[:, : 3 * in_rows].astype(BF16)
            high, low = split(slanted(row_x[v : v + 1], cols)[:, :cols])
            wx[v, :cols, :cols] = high
            wx[v, cols:, :cols] = high
            wx[v, :cols, cols:] = low
            wx[v, cols:, cols:] = low
            if flip:
                band = jnp.where(inside, slanted(row_z[v : v + 1], planes), 0.0)
                high = band.astype(BF16).astype(F32)
                band = high + pltpu.roll(high, planes, 1) + pltpu.roll(band - high, 2 * planes, 1)
                wz[v] = band[:, : 3 * planes].astype(BF16)
            else:
                size = 8 * planes
                high, low = split(slanted(row_z[v : v + 1], size)[:, :size])
                wz[v, :, :size] = high
                wz[v, :, size : 2 * size] = high
                wz[v, :, 2 * size :] = low


def call(kernel, outs, smem, arrays, scratch, name, flops):
    arrays = [pltpu.with_memory_space_constraint(a, VMEM) for a in arrays]
    return pl.pallas_call(
        kernel,
        out_shape=outs,
        in_specs=[pl.BlockSpec(memory_space=SMEM)] * len(smem) + [FULL] * len(arrays),
        out_specs=jax.tree.map(lambda _: FULL, outs),
        scratch_shapes=scratch,
        compiler_params=pltpu.CompilerParams(vmem_limit_bytes=LIMIT),
        cost_estimate=pl.CostEstimate(flops=flops, bytes_accessed=10**7, transcendentals=10**5),
        name=name,
    )(*smem, *arrays)


def make_weights(taps, planes, rows, cols):
    views = taps.shape[0]
    outs = [
        pltpu.VMEM((views * 3 * rows, 15 * rows), BF16),
        pltpu.VMEM((views, 2 * cols, 2 * cols), BF16),
        pltpu.VMEM((views, 8 * planes, 24 * planes), BF16),
        pltpu.VMEM((views, 2 * rows, 6 * rows), BF16),
        pltpu.VMEM((views, 2 * cols, 2 * cols), BF16),
        pltpu.VMEM((views, planes, 3 * planes), BF16),
    ]
    made = call(functools.partial(weights_kernel, rows), outs, [], [taps], [], "weights", 10**7)
    return made[:3], made[3:]


def stacked(pieces):
    columns = []
    for piece in pieces:
        high, low = split(piece)
        columns.append(jnp.concatenate([high, low, high], axis=0))
    return jnp.concatenate(columns, axis=1)


def interleaved(*streams):
    keyed = [((i + 0.5) / len(s), n, piece) for n, s in enumerate(streams) for i, piece in enumerate(s)]
    for _, _, piece in sorted(keyed, key=lambda k: k[:2]):
        piece()


def along_x(rows_ref, wx, out):
    planes, height, lanes = rows_ref.shape
    cols, part = lanes // 2, planes // 4

    def piece(z):
        both = dot(rows_ref[z : z + part].reshape(part * height, lanes), wx[...])
        out[z * height : (z + part) * height, :] = both[:, :cols] + both[:, cols:]

    return [functools.partial(piece, z) for z in range(0, planes, part)]


def forward_rows(parity, far_before, near, own, far_after, wy, ys):
    planes, rows, cols = far_before.shape
    views = ys.shape[0]
    height = 3 * rows
    side = parity[0]

    def plane(z):
        return jnp.concatenate(
            [far_before[z], near[1 - side, z], own[pl.ds(z * rows, rows), :], near[side, z], far_after[z]], axis=0
        )

    for z in range(0, planes, 2):
        high, low = split(dot(wy[...], stacked([plane(z), plane(z + 1)])))
        for j in range(2):
            for v in range(views):
                there = (slice(v * height, (v + 1) * height), slice(j * cols, (j + 1) * cols))
                ys[v, z + j, :, :cols] = high[there]
                ys[v, z + j, :, cols:] = low[there]


def forward_view(ys, wx, wz, out):
    planes, height, lanes = ys.shape
    cols = lanes // 2
    groups = []
    for pair in range(height // 16):
        rows_in = ys[:, 16 * pair : 16 * pair + 16, :].reshape(planes * 16, lanes)
        both = dot(rows_in, wx)
        value = (both[:, :cols] + both[:, cols:]).reshape(planes, 16, cols)
        groups += [value[:, 8 * g : 8 * g + 8, :].reshape(planes * 8, cols) for g in range(2)]
    result = dot(wz, stacked(groups))
    for g in range(len(groups)):
        out[:, 8 * g : 8 * g + 8, :] = result[:, g * cols : (g + 1) * cols].reshape(planes, 8, cols)


def adjoint_rows(v, blurred, before, raw, after, wy, ya):
    views, planes, rows, cols = raw.shape
    blurred, raw, wy = blurred.at[v], raw.at[v], wy.at[v]
    margin = before.shape[0] // (views * planes)
    empty = jnp.zeros((rows - margin, cols), F32)

    def quotient(z):
        at = pl.ds(v * planes + z, margin, stride=views * planes)
        counts = jnp.concatenate([before[at, :], empty, raw[z], after[at, :], empty], axis=0)
        return counts * pl.reciprocal(jnp.maximum(blurred[z], TINY), approx=True)

    def piece(z):
        high, low = split(jnp.concatenate([quotient(z + j) for j in range(WIDE)], axis=1))
        both = dot(wy[...], jnp.concatenate([high, low], axis=0))
        high, low = split(both[:rows] + both[rows:])
        for j in range(WIDE):
            ya[z + j, :, :cols] = high[:, j * cols : (j + 1) * cols]
            ya[z + j, :, cols:] = low[:, j * cols : (j + 1) * cols]

    return [functools.partial(piece, z) for z in range(0, planes, WIDE)]


def adjoint_logs(first, ya, wx, wz, xs, acc):
    planes, rows, lanes = ya.shape

    def piece(y):
        values = stacked([xs[pl.ds(y + j, planes, stride=rows), :] for j in range(WIDE)])
        result = jnp.log(dot(wz[...], values))
        acc[y // WIDE] = result if first else acc[y // WIDE] + result

    return along_x(ya, wx, xs) + [functools.partial(piece, y) for y in range(0, rows, WIDE)]


def updated(current, exponents, out):
    count, planes, lanes = exponents.shape
    cols, rows = lanes // WIDE, count * WIDE
    for y in range(rows):
        at = pl.ds(y, planes, stride=rows)
        part = slice((y % WIDE) * cols, (y % WIDE + 1) * cols)
        out[at, :] = current[at, :] * jnp.exp(exponents[y // WIDE, :, part])


def each_step(steps, body):
    def run(step, _):
        body(step)
        return 0

    lax.fori_loop(0, steps, run, 0)


def forward_kernel(parity, wzs, far_before, near, own, far_after, wy, wx, wz, raw, wyx, out, sums, ys):
    views = ys.shape[0]
    forward_rows(parity, far_before, near, own, far_after, wy, ys)
    each_step(views, lambda v: forward_view(ys.at[v], wx[v], wz[v], out.at[v]))
    sums[...] = jnp.zeros_like(sums)
    for v in range(views):
        sums[v : v + 1, :] = jnp.sum(jnp.sum(raw[v], axis=0), axis=0, keepdims=True)
    weighted_sums(own, wzs, wyx, sums, sums.shape[0] // 3)


def weighted_sums(values, wzs, wyx, sums, at):
    planes, (_, rows, cols) = wzs.shape[1], wyx.shape
    for v in range(wyx.shape[0]):
        total = jnp.zeros((rows, cols), F32)
        for z in range(planes):
            total = total + wzs[v, z] * values[z * rows : (z + 1) * rows, :]
        sums[at + v : at + v + 1, :] = jnp.sum(total * wyx[v], axis=0, keepdims=True)


def adjoint_all(blurred, before, raw, after, wy, wx, wz, ya, yb, xs, acc):
    views = raw.shape[0]

    def rows_of(v):
        return adjoint_rows(v, blurred, before, raw, after, wy, (ya, yb)[v % 2]) if v < views else []

    interleaved(rows_of(0))
    for v in range(views):
        logs = adjoint_logs(v == 0, (ya, yb)[v % 2], wx.at[v], wz.at[v], xs.at[v % 2], acc)
        interleaved(logs, rows_of(v + 1))


def first_adjoint_kernel(
    wzs, current, blurred, before, raw, after, wy, wx, wz, wyx, known, out, sums, ya, yb, xs, acc
):
    adjoint_all(blurred, before, raw, after, wy, wx, wz, ya, yb, xs, acc)
    updated(current, acc[...] * (1.0 / raw.shape[0]), out)
    sums[...] = known[...]
    weighted_sums(out, wzs, wyx, sums, 2 * sums.shape[0] // 3)


def iteration_kernel(
    parity, far_before, near, own, far_after, before, raw, after, wy, wx, wz, wya, wxa, wza,
    out, ys, blurred, ya, yb, xs, acc,
):
    views = ys.shape[0]
    forward_rows(parity, far_before, near, own, far_after, wy, ys)
    each_step(views, lambda v: forward_view(ys.at[v], wx[v], wz[v], blurred.at[v]))
    adjoint_all(blurred, before, raw, after, wya, wxa, wza, ya, yb, xs, acc)
    updated(own, acc[...] * (1.0 / views), out)


def pack_kernel(raw, last, leading):
    count, rows = last.shape[0] // raw.shape[0], raw.shape[1]
    flat = raw.reshape(raw.shape[0] * rows, raw.shape[2])
    for y in range(count):
        here = slice(y * raw.shape[0], (y + 1) * raw.shape[0])
        last[here, :] = flat[pl.ds(rows - count + y, raw.shape[0], stride=rows), :]
        leading[here, :] = flat[pl.ds(y, raw.shape[0], stride=rows), :]


def packed(raw, count):
    views, planes, rows, cols = raw.shape
    outs = [pltpu.VMEM((count * views * planes, cols), F32)] * 2
    return call(pack_kernel, outs, [], [raw.reshape(views * planes, rows, cols)], [], "pack", 10**6)


def scaled_kernel(views, values, part, rest, out):
    sums = jnp.sum(part[...] + rest[...], axis=1, keepdims=True)
    space = sums.shape[0] // 3
    total, first, second = (sums[i * space : i * space + views] for i in range(3))
    scale = jnp.sum(jnp.log(first / total) + jnp.log(second / total), axis=0, keepdims=True)
    out[...] = values[...] * jnp.exp(scale * (1.0 / views))


def adjoint_scratch(planes, rows, cols):
    return [
        pltpu.VMEM((planes, rows, 2 * cols), BF16),
        pltpu.VMEM((planes, rows, 2 * cols), BF16),
        pltpu.VMEM((2, planes * 16, cols), F32),
        pltpu.VMEM((rows // WIDE, planes, WIDE * cols), F32),
    ]


def forward(parity, slabs, weights, raw, wzs, wyx):
    planes, rows, cols = slabs[0].shape
    views = raw.shape[0]
    slabs = [s.reshape(-1, cols) if i == 2 else s for i, s in enumerate(slabs)]
    outs = [pltpu.VMEM((views, planes, 3 * rows, cols), F32), pltpu.VMEM((24 * -(-views // 8), cols), F32)]
    scratch = [pltpu.VMEM((views, planes, 3 * rows, 2 * cols), BF16)]
    return call(forward_kernel, outs, [parity, wzs], [*slabs, *weights, raw, wyx], scratch, "forward", 10**10)


def first_adjoint(current, blurred, before, raw, after, weights, wzs, wyx, known):
    planes, rows, cols = current.shape
    current = current.reshape(planes * rows, cols)
    out, sums = call(
        first_adjoint_kernel,
        [pltpu.VMEM(current.shape, F32), pltpu.VMEM(known.shape, F32)],
        [wzs],
        [current, blurred, before, raw, after, *weights, wyx, known],
        adjoint_scratch(planes, rows, cols),
        "adjoint",
        10**10,
    )
    return out.reshape(planes, rows, cols), sums


def full_iteration(parity, slabs, before, raw, after, weights, adjoint_weights):
    planes, rows, cols = slabs[0].shape
    views = raw.shape[0]
    slabs = [s.reshape(-1, cols) if i == 2 else s for i, s in enumerate(slabs)]
    scratch = [
        pltpu.VMEM((views, planes, 3 * rows, 2 * cols), BF16),
        pltpu.VMEM((views, planes, 3 * rows, cols), F32),
    ]
    return call(
        iteration_kernel,
        pltpu.VMEM((planes * rows, cols), F32),
        [parity],
        [*slabs, before, raw, after, *weights, *adjoint_weights],
        scratch + adjoint_scratch(planes, rows, cols),
        "iteration",
        2 * 10**10,
    )


def two_slabs_away(value, count):
    up = [(i, i + 2) for i in range(count - 2)]
    down = [(j, i) for i, j in up]
    return lax.ppermute(value, "slab", up), lax.ppermute(value, "slab", down)


def with_near(value, far_before, far_after, parity, count):
    swap = [(i, i + 1 - 2 * (i % 2)) for i in range(count)]
    passed = jnp.stack([value, jnp.where(parity[0] == 0, far_after, far_before)])
    near = lax.ppermute(passed, "slab", swap)
    return far_before, near, value, far_after


def tap_sums(taps, offset, extent, total):
    count = taps.shape[1]
    target = offset + jnp.arange(extent)[None, :] - jnp.arange(count)[:, None] + count // 2
    reach = jnp.where((target >= 0) & (target < total), 1.0, 0.0).astype(F32)
    return jnp.sum(taps[:, :, None] * reach[None], axis=1)


def per_device(estimate, raw, taps):
    views = raw.shape[0]
    planes, rows, cols = estimate.shape
    count = lax.axis_size("slab")
    assert 16 == rows >= taps.shape[2] // 2 and count & (count - 1) == 0
    up = [(i, i + 1) for i in range(count - 1)]
    down = [(j, i) for i, j in up]
    place = lax.axis_index("slab")
    parity = (place % 2).reshape(1)

    far = two_slabs_away(estimate, count)
    last, leading = packed(raw, taps.shape[2] // 2)
    before = lax.ppermute(last, "slab", up)
    after = lax.ppermute(leading, "slab", down)

    wzs = tap_sums(taps[:, 0], 0, planes, planes)
    wy_sums = tap_sums(taps[:, 1], place * rows, rows, count * rows)
    wx_sums = tap_sums(taps[:, 2], 0, cols, cols)
    wyx = wy_sums[:, :, None] * wx_sums[:, None, :]

    forward_weights, adjoint_weights = make_weights(taps, planes, rows, cols)

    slabs = with_near(estimate, *far, parity, count)
    blurred, known = forward(parity, slabs, forward_weights, raw, wzs, wyx)
    current, sums = first_adjoint(estimate, blurred, before, raw, after, adjoint_weights, wzs, wyx, known)

    far = two_slabs_away(current, count)
    bits = [1 << b for b in range(count.bit_length() - 1)]
    rounds = [bits[:1], bits[2:4] + [sum(bits[2:4])], *([b] for b in bits[4:]), bits[1:2]]
    for r, distances in enumerate(rounds):
        others = [lax.ppermute(sums, "slab", [(i, i ^ d) for i in range(count)]) for d in distances]
        if r == 1:
            *far, sums = lax.optimization_barrier((*far, sums + sum(others)))
        elif r < len(rounds) - 1:
            sums = sums + sum(others)
    slabs = with_near(current, *far, parity, count)
    current = full_iteration(parity, slabs, before, raw, after, forward_weights, adjoint_weights)
    out = jax.ShapeDtypeStruct(current.shape, F32)
    scaled = functools.partial(scaled_kernel, views)
    return call(scaled, out, [], [current, sums, others[0]], [], "scaled", 10**5).reshape(estimate.shape)


def solution(mesh):
    placed = (P("blocks", "slab", None), P(None, "blocks", "slab", None), P())
    return jax.shard_map(
        per_device, mesh=mesh, in_specs=placed, out_specs=P("blocks", "slab", None), check_vma=False
    )
```

```python
import functools

import jax
import jax.numpy as jnp
import numpy as np
from jax import lax
from jax.experimental import pallas as pl
from jax.experimental.pallas import tpu as pltpu
from jax.sharding import PartitionSpec as P

F32 = jnp.float32
BF16 = jnp.bfloat16
VMEM = pltpu.MemorySpace.VMEM
SMEM = pltpu.MemorySpace.SMEM
FULL = pl.BlockSpec(memory_space=VMEM)
LIMIT = 30 * 1024 * 1024
WIDE = 4
TINY = float(np.finfo(np.float32).tiny)


def split(value):
    high = value.astype(BF16)
    low = (value - high.astype(F32)).astype(BF16)
    return high, low


def dot(a, b):
    return jnp.dot(a, b, preferred_element_type=F32)


def placed_row(taps, lane_of_tap, width):
    count = taps.shape[1]
    tap = lax.broadcasted_iota(jnp.int32, (count, width), 0)
    lane = lax.broadcasted_iota(jnp.int32, (count, width), 1)
    onehot = jnp.where(lane == lane_of_tap(tap), 1.0, 0.0).astype(F32)
    return jnp.dot(taps, onehot, precision=lax.Precision.HIGHEST, preferred_element_type=F32)


def slanted(row, height):
    full = jnp.broadcast_to(row, (height, row.shape[1]))
    return pltpu.roll(full, 0, 1, stride=1, stride_axis=0)


def weights_kernel(rows, taps_ref, *outs):
    views, _, count = taps_ref.shape
    margin = count // 2
    for flip in (False, True):
        wy, wx, wz = outs[3 * flip : 3 * flip + 3]
        order = (lambda k: count - 1 - k) if flip else (lambda k: k)
        out_rows = rows if flip else 3 * rows
        in_rows = out_rows + 2 * rows
        planes = wz.shape[1] // 8
        cols = wx.shape[1] // 2
        row_y = placed_row(taps_ref[:, 1, :], lambda k: order(k) + rows - margin, 256)
        high = row_y.astype(BF16).astype(F32)
        low = row_y - high
        if flip:
            row_y = (high, low)
        else:
            row_y = high + pltpu.roll(high, in_rows, 1) + pltpu.roll(low, 2 * in_rows, 1)
        row_x = placed_row(taps_ref[:, 2, :], lambda k: lax.rem(margin - order(k) + 2 * cols, 2 * cols), 2 * cols)
        width_z = 16 * planes
        row_z = placed_row(
            taps_ref[:, 0, :], lambda k: lax.rem(8 * (order(k) - margin) + width_z, width_z), width_z
        )
        for v in range(views):
            if flip:
                lane = lax.broadcasted_iota(jnp.int32, (rows, 256), 1)
                for j, row in enumerate(row_y):
                    band = slanted(row[v : v + 1], rows)
                    shifted = pltpu.roll(band, 256 - (rows - margin), 1)
                    band = jnp.where(lane < margin, shifted, jnp.where(lane < rows, 0.0, band))
                    band = band + pltpu.roll(band, in_rows, 1)
                    wy[v, j * rows : (j + 1) * rows, :] = band[:, : 2 * in_rows].astype(BF16)
            else:
                row = row_y[v : v + 1]
                band = jnp.concatenate(
                    [slanted(pltpu.roll(row, rows - margin, 1), rows), slanted(pltpu.roll(row, rows, 1), 2 * rows)]
                )
                wy[v * out_rows : (v + 1) * out_rows, :] = band[:, : 3 * in_rows].astype(BF16)
            high, low = split(slanted(row_x[v : v + 1], cols)[:, :cols])
            wx[v, :cols, :cols] = high
            wx[v, cols:, :cols] = high
            wx[v, :cols, cols:] = low
            wx[v, cols:, cols:] = low
            size = 8 * planes
            high, low = split(slanted(row_z[v : v + 1], size)[:, :size])
            wz[v, :, :size] = high
            wz[v, :, size : 2 * size] = high
            wz[v, :, 2 * size :] = low


def call(kernel, outs, smem, arrays, scratch, name, flops):
    arrays = [pltpu.with_memory_space_constraint(a, VMEM) for a in arrays]
    return pl.pallas_call(
        kernel,
        out_shape=outs,
        in_specs=[pl.BlockSpec(memory_space=SMEM)] * len(smem) + [FULL] * len(arrays),
        out_specs=jax.tree.map(lambda _: FULL, outs),
        scratch_shapes=scratch,
        compiler_params=pltpu.CompilerParams(vmem_limit_bytes=LIMIT),
        cost_estimate=pl.CostEstimate(flops=flops, bytes_accessed=10**7, transcendentals=10**5),
        name=name,
    )(*smem, *arrays)


def make_weights(taps, planes, rows, cols):
    views = taps.shape[0]
    outs = [
        pltpu.VMEM((views * 3 * rows, 15 * rows), BF16),
        pltpu.VMEM((views, 2 * cols, 2 * cols), BF16),
        pltpu.VMEM((views, 8 * planes, 24 * planes), BF16),
        pltpu.VMEM((views, 2 * rows, 6 * rows), BF16),
        pltpu.VMEM((views, 2 * cols, 2 * cols), BF16),
        pltpu.VMEM((views, 8 * planes, 24 * planes), BF16),
    ]
    made = call(functools.partial(weights_kernel, rows), outs, [], [taps], [], "weights", 10**7)
    return made[:3], made[3:]


def stacked(pieces):
    columns = []
    for piece in pieces:
        high, low = split(piece)
        columns.append(jnp.concatenate([high, low, high], axis=0))
    return jnp.concatenate(columns, axis=1)


def interleaved(*streams):
    keyed = [((i + 0.5) / len(s), n, piece) for n, s in enumerate(streams) for i, piece in enumerate(s)]
    for _, _, piece in sorted(keyed, key=lambda k: k[:2]):
        piece()


def along_x(rows_ref, wx, out):
    planes, height, lanes = rows_ref.shape
    cols, part = lanes // 2, planes // 4

    def piece(z):
        both = dot(rows_ref[z : z + part].reshape(part * height, lanes), wx[...])
        out[z * height : (z + part) * height, :] = both[:, :cols] + both[:, cols:]

    return [functools.partial(piece, z) for z in range(0, planes, part)]


def forward_rows(parity, far_before, near, own, far_after, wy, ys):
    planes, rows, cols = far_before.shape
    views = ys.shape[0]
    height = 3 * rows
    side = parity[0]

    def plane(z):
        return jnp.concatenate(
            [far_before[z], near[1 - side, z], own[z], near[side, z], far_after[z]], axis=0
        )

    for z in range(0, planes, 2):
        high, low = split(dot(wy[...], stacked([plane(z), plane(z + 1)])))
        for j in range(2):
            for v in range(views):
                there = (slice(v * height, (v + 1) * height), slice(j * cols, (j + 1) * cols))
                ys[v, z + j, :, :cols] = high[there]
                ys[v, z + j, :, cols:] = low[there]


def forward_view(ys, wx, wz, out):
    planes, height, lanes = ys.shape
    cols = lanes // 2
    groups = []
    for pair in range(height // 16):
        rows_in = ys[:, 16 * pair : 16 * pair + 16, :].reshape(planes * 16, lanes)
        both = dot(rows_in, wx)
        value = (both[:, :cols] + both[:, cols:]).reshape(planes, 16, cols)
        groups += [value[:, 8 * g : 8 * g + 8, :].reshape(planes * 8, cols) for g in range(2)]
    result = dot(wz, stacked(groups))
    for g in range(len(groups)):
        out[:, 8 * g : 8 * g + 8, :] = result[:, g * cols : (g + 1) * cols].reshape(planes, 8, cols)


def adjoint_rows(halo, raw, blurred, wy, ya):
    planes, rows, cols = raw.shape

    def quotient(z):
        around = halo(z)
        counts = jnp.concatenate([around[:rows], raw[z], around[rows:]], axis=0)
        return counts * pl.reciprocal(jnp.maximum(blurred[z], TINY), approx=True)

    def piece(z):
        high, low = split(jnp.concatenate([quotient(z + j) for j in range(WIDE)], axis=1))
        both = dot(wy[...], jnp.concatenate([high, low], axis=0))
        high, low = split(both[:rows] + both[rows:])
        for j in range(WIDE):
            ya[z + j, :, :cols] = high[:, j * cols : (j + 1) * cols]
            ya[z + j, :, cols:] = low[:, j * cols : (j + 1) * cols]

    return [functools.partial(piece, z) for z in range(0, planes, WIDE)]


def adjoint_logs(first, ya, wx, wz, xs, acc):
    planes, rows, lanes = ya.shape
    cols = lanes // 2

    def piece():
        value = xs[...].reshape(planes, rows, cols)
        groups = [value[:, 8 * g : 8 * g + 8, :].reshape(planes * 8, cols) for g in range(2)]
        result = jnp.log(dot(wz[...], stacked(groups)))
        acc[...] = result if first else acc[...] + result

    return along_x(ya, wx, xs) + [piece]


def adjoint_of(chosen, begun, halo, raw, blurred, wy, wx, wz, ya, yb, xs, acc):
    def rows_of(i):
        if i == len(chosen):
            return []
        v = chosen[i]
        return adjoint_rows(halo(v), raw.at[v], blurred.at[v], wy.at[v], (ya, yb)[i % 2])

    interleaved(rows_of(0))
    for i, v in enumerate(chosen):
        logs = adjoint_logs(i == 0 and not begun, (ya, yb)[i % 2], wx.at[v], wz.at[v], xs.at[i % 2], acc)
        interleaved(logs, rows_of(i + 1))


def updated(current, acc, views, out):
    planes, rows, cols = out.shape
    for g in range(rows // 8):
        here = slice(8 * g, 8 * g + 8)
        exponent = acc[:, g * cols : (g + 1) * cols].reshape(planes, 8, cols) * (1.0 / views)
        out[:, here, :] = current[:, here, :] * jnp.exp(exponent)


def plane_halo(chosen, before, after, halos):
    planes, rows = halos.shape[1], halos.shape[2] // 2
    stride = len(chosen) * planes
    count = before.shape[0] // stride
    empty = jnp.zeros((rows - count, before.shape[1]), F32)

    def of_view(v):
        i = v - chosen[0]

        def of_plane(z):
            at = pl.ds(i * planes + z, count, stride=stride)
            around = jnp.concatenate([before[at, :], empty, after[at, :], empty], axis=0)
            halos[i, z] = around
            return around

        return of_plane

    return of_view


def each_step(steps, body):
    def run(step, _):
        body(step)
        return 0

    lax.fori_loop(0, steps, run, 0)


def forward_kernel(parity, wzs, far_before, near, own, far_after, wy, wx, wz, raw, wyx, out, sums, ys):
    views = ys.shape[0]
    forward_rows(parity, far_before, near, own, far_after, wy, ys)
    each_step(views, lambda v: forward_view(ys.at[v], wx[v], wz[v], out.at[v]))
    sums[...] = jnp.zeros_like(sums)
    for v in range(views):
        sums[v : v + 1, :] = jnp.sum(jnp.sum(raw[v], axis=0), axis=0, keepdims=True)
    weighted_sums(own, wzs, wyx, sums, sums.shape[0] // 3)


def weighted_sums(values, wzs, wyx, sums, at):
    planes, rows, cols = values.shape
    for v in range(wyx.shape[0]):
        total = jnp.zeros((rows, cols), F32)
        for z in range(planes):
            total = total + wzs[v, z] * values[z]
        sums[at + v : at + v + 1, :] = jnp.sum(total * wyx[v], axis=0, keepdims=True)


def early_adjoint_kernel(chosen, before, after, raw, blurred, wy, wx, wz, acc, halos, ya, yb, xs):
    halo = plane_halo(chosen, before, after, halos)
    adjoint_of(chosen, False, halo, raw, blurred, wy, wx, wz, ya, yb, xs, acc)


def late_adjoint_kernel(
    chosen, wzs, before, after, raw, blurred, wy, wx, wz, known_acc, current, wyx, known, out, sums, halos, ya, yb, xs, acc
):
    acc[...] = known_acc[...]
    halo = plane_halo(chosen, before, after, halos)
    adjoint_of(chosen, True, halo, raw, blurred, wy, wx, wz, ya, yb, xs, acc)
    updated(current, acc[...], raw.shape[0], out)
    sums[...] = known[...]
    weighted_sums(out, wzs, wyx, sums, 2 * sums.shape[0] // 3)


def iteration_kernel(
    parity, far_before, near, own, far_after, early, late, raw, wy, wx, wz, wya, wxa, wza,
    out, ys, blurred, ya, yb, xs, acc,
):
    views, split_at = ys.shape[0], early.shape[0]
    forward_rows(parity, far_before, near, own, far_after, wy, ys)
    each_step(views, lambda v: forward_view(ys.at[v], wx[v], wz[v], blurred.at[v]))

    def halo(v):
        return lambda z: early[v, z] if v < split_at else late[v - split_at, z]

    adjoint_of(range(views), False, halo, raw, blurred, wya, wxa, wza, ya, yb, xs, acc)
    updated(own, acc[...], views, out)


def pack_kernel(raw, last, leading):
    count, rows = last.shape[0] // raw.shape[0], raw.shape[1]
    flat = raw.reshape(raw.shape[0] * rows, raw.shape[2])
    for y in range(count):
        here = slice(y * raw.shape[0], (y + 1) * raw.shape[0])
        last[here, :] = flat[pl.ds(rows - count + y, raw.shape[0], stride=rows), :]
        leading[here, :] = flat[pl.ds(y, raw.shape[0], stride=rows), :]


def packed(raw, chosen, count):
    _, planes, rows, cols = raw.shape
    part = raw[chosen[0] : chosen[-1] + 1].reshape(len(chosen) * planes, rows, cols)
    outs = [pltpu.VMEM((count * part.shape[0], cols), F32)] * 2
    return call(pack_kernel, outs, [], [part], [], "pack", 10**6)


def scaled_kernel(views, values, part, rest, out):
    sums = jnp.sum(part[...] + rest[...], axis=1, keepdims=True)
    space = sums.shape[0] // 3
    total, first, second = (sums[i * space : i * space + views] for i in range(3))
    scale = jnp.sum(jnp.log(first / total) + jnp.log(second / total), axis=0, keepdims=True)
    out[...] = values[...] * jnp.exp(scale * (1.0 / views))[None]


def adjoint_scratch(planes, rows, cols):
    return [
        pltpu.VMEM((planes, rows, 2 * cols), BF16),
        pltpu.VMEM((planes, rows, 2 * cols), BF16),
        pltpu.VMEM((2, planes * rows, cols), F32),
    ]


def forward(parity, slabs, weights, raw, wzs, wyx):
    planes, rows, cols = slabs[0].shape
    views = raw.shape[0]
    outs = [pltpu.VMEM((views, planes, 3 * rows, cols), F32), pltpu.VMEM((24 * -(-views // 8), cols), F32)]
    scratch = [pltpu.VMEM((views, planes, 3 * rows, 2 * cols), BF16)]
    return call(forward_kernel, outs, [parity, wzs], [*slabs, *weights, raw, wyx], scratch, "forward", 10**10)


def first_adjoint(groups, current, blurred, befores, raw, afters, weights, wzs, wyx, known):
    planes, rows, cols = current.shape
    shared = (raw, blurred, *weights)
    scratch = adjoint_scratch(planes, rows, cols)
    acc = pltpu.VMEM((planes * 8, rows // 8 * cols), F32)
    halos = [pltpu.VMEM((len(g), planes, 2 * rows, cols), F32) for g in groups]
    kernel = functools.partial(early_adjoint_kernel, groups[0])
    arrays = [befores[0], afters[0], *shared]
    partial, early = call(kernel, [acc, halos[0]], [], arrays, scratch, "early_adjoint", 10**10)
    kernel = functools.partial(late_adjoint_kernel, groups[1])
    arrays = [befores[1], afters[1], *shared, partial, current, wyx, known]
    outs = [pltpu.VMEM(current.shape, F32), pltpu.VMEM(known.shape, F32), halos[1]]
    out, sums, late = call(kernel, outs, [wzs], arrays, scratch + [acc], "late_adjoint", 10**10)
    return out, sums, (early, late)


def full_iteration(parity, slabs, halos, raw, weights, adjoint_weights):
    planes, rows, cols = slabs[0].shape
    views = raw.shape[0]
    scratch = [
        pltpu.VMEM((views, planes, 3 * rows, 2 * cols), BF16),
        pltpu.VMEM((views, planes, 3 * rows, cols), F32),
    ]
    return call(
        iteration_kernel,
        pltpu.VMEM((planes, rows, cols), F32),
        [parity],
        [*slabs, *halos, raw, *weights, *adjoint_weights],
        scratch + adjoint_scratch(planes, rows, cols) + [pltpu.VMEM((planes * 8, rows // 8 * cols), F32)],
        "iteration",
        2 * 10**10,
    )


def two_slabs_away(value, count):
    up = [(i, i + 2) for i in range(count - 2)]
    down = [(j, i) for i, j in up]
    return lax.ppermute(value, "slab", up), lax.ppermute(value, "slab", down)


def with_near(value, far_before, far_after, parity, count):
    swap = [(i, i + 1 - 2 * (i % 2)) for i in range(count)]
    passed = jnp.stack([value, jnp.where(parity[0] == 0, far_after, far_before)])
    near = lax.ppermute(passed, "slab", swap)
    return far_before, near, value, far_after


def tap_sums(taps, offset, extent, total):
    count = taps.shape[1]
    target = offset + jnp.arange(extent)[None, :] - jnp.arange(count)[:, None] + count // 2
    reach = jnp.where((target >= 0) & (target < total), 1.0, 0.0).astype(F32)
    return jnp.sum(taps[:, :, None] * reach[None], axis=1)


def per_device(estimate, raw, taps):
    views = raw.shape[0]
    planes, rows, cols = estimate.shape
    count = lax.axis_size("slab")
    assert 16 == rows >= taps.shape[2] // 2 and count & (count - 1) == 0
    up = [(i, i + 1) for i in range(count - 1)]
    down = [(j, i) for i, j in up]
    place = lax.axis_index("slab")
    parity = (place % 2).reshape(1)

    far = two_slabs_away(estimate, count)
    margin = taps.shape[2] // 2
    groups = (range(0, 2 * views // 3), range(2 * views // 3, views))
    edges = [packed(raw, g, margin) for g in groups]
    befores = [lax.ppermute(edges[0][0], "slab", up)]
    afters = [lax.ppermute(edges[0][1], "slab", down)]

    wzs = tap_sums(taps[:, 0], 0, planes, planes)
    wy_sums = tap_sums(taps[:, 1], place * rows, rows, count * rows)
    wx_sums = tap_sums(taps[:, 2], 0, cols, cols)
    wyx = wy_sums[:, :, None] * wx_sums[:, None, :]

    forward_weights, adjoint_weights = make_weights(taps, planes, rows, cols)

    slabs = with_near(estimate, *far, parity, count)
    blurred, known = forward(parity, slabs, forward_weights, raw, wzs, wyx)
    last, leading, known = lax.optimization_barrier((*edges[1], known))
    befores.append(lax.ppermute(last, "slab", up))
    afters.append(lax.ppermute(leading, "slab", down))
    current, sums, halos = first_adjoint(
        groups, estimate, blurred, befores, raw, afters, adjoint_weights, wzs, wyx, known
    )

    far = two_slabs_away(current, count)
    bits = [1 << b for b in range(count.bit_length() - 1)]
    rounds = [bits[:1], bits[2:4] + [sum(bits[2:4])], *([b] for b in bits[4:]), bits[1:2]]
    for r, distances in enumerate(rounds):
        others = [lax.ppermute(sums, "slab", [(i, i ^ d) for i in range(count)]) for d in distances]
        if r == 1:
            *far, sums = lax.optimization_barrier((*far, sums + sum(others)))
        elif r < len(rounds) - 1:
            sums = sums + sum(others)
    slabs = with_near(current, *far, parity, count)
    current = full_iteration(parity, slabs, halos, raw, forward_weights, adjoint_weights)
    out = jax.ShapeDtypeStruct(current.shape, F32)
    scaled = functools.partial(scaled_kernel, views)
    return call(scaled, out, [], [current, sums, others[0]], [], "scaled", 10**5)


def solution(mesh):
    placed = (P("blocks", "slab", None), P(None, "blocks", "slab", None), P())
    return jax.shard_map(
        per_device, mesh=mesh, in_specs=placed, out_specs=P("blocks", "slab", None), check_vma=False
    )
```

```python
import functools

import jax
import jax.numpy as jnp
import numpy as np
from jax import lax
from jax.experimental import pallas as pl
from jax.experimental.pallas import tpu as pltpu
from jax.sharding import PartitionSpec as P

F32 = jnp.float32
BF16 = jnp.bfloat16
VMEM = pltpu.MemorySpace.VMEM
SMEM = pltpu.MemorySpace.SMEM
FULL = pl.BlockSpec(memory_space=VMEM)
LIMIT = 30 * 1024 * 1024
WIDE = 4
TINY = float(np.finfo(np.float32).tiny)


def split(value):
    high = value.astype(BF16)
    low = (value - high.astype(F32)).astype(BF16)
    return high, low


def dot(a, b):
    return jnp.dot(a, b, preferred_element_type=F32)


def placed_row(taps, lane_of_tap, width):
    count = taps.shape[1]
    tap = lax.broadcasted_iota(jnp.int32, (count, width), 0)
    lane = lax.broadcasted_iota(jnp.int32, (count, width), 1)
    onehot = jnp.where(lane == lane_of_tap(tap), 1.0, 0.0).astype(F32)
    return jnp.dot(taps, onehot, precision=lax.Precision.HIGHEST, preferred_element_type=F32)


def slanted(row, height):
    full = jnp.broadcast_to(row, (height, row.shape[1]))
    return pltpu.roll(full, 0, 1, stride=1, stride_axis=0)


def weights_kernel(rows, taps_ref, *outs):
    views, _, count = taps_ref.shape
    margin = count // 2
    for flip in (False, True):
        wy, wx, wz = outs[3 * flip : 3 * flip + 3]
        order = (lambda k: count - 1 - k) if flip else (lambda k: k)
        out_rows = rows if flip else 3 * rows
        in_rows = out_rows + 2 * rows
        planes = wz.shape[1] // 8
        cols = wx.shape[1] // 2
        row_y = placed_row(taps_ref[:, 1, :], lambda k: order(k) + rows - margin, 256)
        high = row_y.astype(BF16).astype(F32)
        low = row_y - high
        if flip:
            row_y = (high, low)
        else:
            row_y = high + pltpu.roll(high, in_rows, 1) + pltpu.roll(low, 2 * in_rows, 1)
        row_x = placed_row(taps_ref[:, 2, :], lambda k: lax.rem(margin - order(k) + 2 * cols, 2 * cols), 2 * cols)
        width_z = 16 * planes
        row_z = placed_row(
            taps_ref[:, 0, :], lambda k: lax.rem(8 * (order(k) - margin) + width_z, width_z), width_z
        )
        for v in range(views):
            if flip:
                lane = lax.broadcasted_iota(jnp.int32, (rows, 256), 1)
                for j, row in enumerate(row_y):
                    band = slanted(row[v : v + 1], rows)
                    shifted = pltpu.roll(band, 256 - (rows - margin), 1)
                    band = jnp.where(lane < margin, shifted, jnp.where(lane < rows, 0.0, band))
                    band = band + pltpu.roll(band, in_rows, 1)
                    wy[v, j * rows : (j + 1) * rows, :] = band[:, : 2 * in_rows].astype(BF16)
            else:
                row = row_y[v : v + 1]
                band = jnp.concatenate(
                    [slanted(pltpu.roll(row, rows - margin, 1), rows), slanted(pltpu.roll(row, rows, 1), 2 * rows)]
                )
                wy[v * out_rows : (v + 1) * out_rows, :] = band[:, : 3 * in_rows].astype(BF16)
            high, low = split(slanted(row_x[v : v + 1], cols)[:, :cols])
            wx[v, :cols, :cols] = high
            wx[v, cols:, :cols] = high
            wx[v, :cols, cols:] = low
            wx[v, cols:, cols:] = low
            size = 8 * planes
            high, low = split(slanted(row_z[v : v + 1], size)[:, :size])
            wz[v, :, :size] = high
            wz[v, :, size : 2 * size] = high
            wz[v, :, 2 * size :] = low


def call(kernel, outs, smem, arrays, scratch, name, flops):
    arrays = [pltpu.with_memory_space_constraint(a, VMEM) for a in arrays]
    return pl.pallas_call(
        kernel,
        out_shape=outs,
        in_specs=[pl.BlockSpec(memory_space=SMEM)] * len(smem) + [FULL] * len(arrays),
        out_specs=jax.tree.map(lambda _: FULL, outs),
        scratch_shapes=scratch,
        compiler_params=pltpu.CompilerParams(vmem_limit_bytes=LIMIT),
        cost_estimate=pl.CostEstimate(flops=flops, bytes_accessed=10**7, transcendentals=10**5),
        name=name,
    )(*smem, *arrays)


def make_weights(taps, planes, rows, cols):
    views = taps.shape[0]
    outs = [
        pltpu.VMEM((views * 3 * rows, 15 * rows), BF16),
        pltpu.VMEM((views, 2 * cols, 2 * cols), BF16),
        pltpu.VMEM((views, 8 * planes, 24 * planes), BF16),
        pltpu.VMEM((views, 2 * rows, 6 * rows), BF16),
        pltpu.VMEM((views, 2 * cols, 2 * cols), BF16),
        pltpu.VMEM((views, 8 * planes, 24 * planes), BF16),
    ]
    made = call(functools.partial(weights_kernel, rows), outs, [], [taps], [], "weights", 10**7)
    return made[:3], made[3:]


def stacked(pieces):
    columns = []
    for piece in pieces:
        high, low = split(piece)
        columns.append(jnp.concatenate([high, low, high], axis=0))
    return jnp.concatenate(columns, axis=1)


def interleaved(*streams):
    keyed = [((i + 0.5) / len(s), n, piece) for n, s in enumerate(streams) for i, piece in enumerate(s)]
    for _, _, piece in sorted(keyed, key=lambda k: k[:2]):
        piece()


def along_x(rows_ref, wx, out):
    planes, height, lanes = rows_ref.shape
    cols, part = lanes // 2, planes // 4

    def piece(z):
        both = dot(rows_ref[z : z + part].reshape(part * height, lanes), wx[...])
        out[z * height : (z + part) * height, :] = both[:, :cols] + both[:, cols:]

    return [functools.partial(piece, z) for z in range(0, planes, part)]


def forward_rows(parity, far_before, near, own, far_after, wy, ys):
    planes, rows, cols = far_before.shape
    views = ys.shape[0]
    height = 3 * rows
    side = parity[0]

    def plane(z):
        return jnp.concatenate(
            [far_before[z], near[1 - side, z], own[z], near[side, z], far_after[z]], axis=0
        )

    for z in range(0, planes, 2):
        high, low = split(dot(wy[...], stacked([plane(z), plane(z + 1)])))
        for j in range(2):
            for v in range(views):
                there = (slice(v * height, (v + 1) * height), slice(j * cols, (j + 1) * cols))
                ys[v, z + j, :, :cols] = high[there]
                ys[v, z + j, :, cols:] = low[there]


def forward_view(ys, wx, wz, out):
    planes, height, lanes = ys.shape
    cols = lanes // 2
    groups = []
    for pair in range(height // 16):
        rows_in = ys[:, 16 * pair : 16 * pair + 16, :].reshape(planes * 16, lanes)
        both = dot(rows_in, wx)
        value = (both[:, :cols] + both[:, cols:]).reshape(planes, 16, cols)
        groups += [value[:, 8 * g : 8 * g + 8, :].reshape(planes * 8, cols) for g in range(2)]
    result = dot(wz, stacked(groups))
    for g in range(len(groups)):
        out[:, 8 * g : 8 * g + 8, :] = result[:, g * cols : (g + 1) * cols].reshape(planes, 8, cols)


def adjoint_rows(halo, raw, blurred, wy, ya):
    planes, rows, cols = raw.shape

    def quotient(z):
        around = halo(z)
        counts = jnp.concatenate([around[:rows], raw[z], around[rows:]], axis=0)
        return counts * pl.reciprocal(jnp.maximum(blurred[z], TINY), approx=True)

    def piece(z):
        high, low = split(jnp.concatenate([quotient(z + j) for j in range(WIDE)], axis=1))
        both = dot(wy[...], jnp.concatenate([high, low], axis=0))
        high, low = split(both[:rows] + both[rows:])
        for j in range(WIDE):
            ya[z + j, :, :cols] = high[:, j * cols : (j + 1) * cols]
            ya[z + j, :, cols:] = low[:, j * cols : (j + 1) * cols]

    return [functools.partial(piece, z) for z in range(0, planes, WIDE)]


def adjoint_logs(first, ya, wx, wz, xs, acc):
    planes, rows, lanes = ya.shape
    cols = lanes // 2

    def piece():
        value = xs[...].reshape(planes, rows, cols)
        groups = [value[:, 8 * g : 8 * g + 8, :].reshape(planes * 8, cols) for g in range(2)]
        result = jnp.log(dot(wz[...], stacked(groups)))
        acc[...] = result if first else acc[...] + result

    return along_x(ya, wx, xs) + [piece]


def adjoint_of(chosen, begun, halo, raw, blurred, wy, wx, wz, ya, yb, xs, acc):
    def rows_of(i):
        if i == len(chosen):
            return []
        v = chosen[i]
        return adjoint_rows(halo(v), raw.at[v], blurred.at[v], wy.at[v], (ya, yb)[i % 2])

    interleaved(rows_of(0))
    for i, v in enumerate(chosen):
        logs = adjoint_logs(i == 0 and not begun, (ya, yb)[i % 2], wx.at[v], wz.at[v], xs.at[i % 2], acc)
        interleaved(logs, rows_of(i + 1))


def updated(current, acc, views, out):
    planes, rows, cols = out.shape
    for g in range(rows // 8):
        here = slice(8 * g, 8 * g + 8)
        exponent = acc[:, g * cols : (g + 1) * cols].reshape(planes, 8, cols) * (1.0 / views)
        out[:, here, :] = current[:, here, :] * jnp.exp(exponent)


def plane_halo(chosen, before, after, halos):
    planes, rows = halos.shape[1], halos.shape[2] // 2
    stride = len(chosen) * planes
    count = before.shape[0] // stride
    empty = jnp.zeros((rows - count, before.shape[1]), F32)

    def of_view(v):
        i = v - chosen[0]

        def of_plane(z):
            at = pl.ds(i * planes + z, count, stride=stride)
            around = jnp.concatenate([before[at, :], empty, after[at, :], empty], axis=0)
            halos[i, z] = around
            return around

        return of_plane

    return of_view


def each_step(steps, body):
    def run(step, _):
        body(step)
        return 0

    lax.fori_loop(0, steps, run, 0)


def forward_kernel(parity, wzs, far_before, near, own, far_after, wy, wx, wz, raw, wyx, out, sums, ys):
    views = ys.shape[0]
    forward_rows(parity, far_before, near, own, far_after, wy, ys)
    each_step(views, lambda v: forward_view(ys.at[v], wx[v], wz[v], out.at[v]))
    sums[...] = jnp.zeros_like(sums)
    for v in range(views):
        sums[v : v + 1, :] = jnp.sum(jnp.sum(raw[v], axis=0), axis=0, keepdims=True)
    weighted_sums(own, wzs, wyx, sums, sums.shape[0] // 3)


def weighted_sums(values, wzs, wyx, sums, at):
    planes, rows, cols = values.shape
    for v in range(wyx.shape[0]):
        total = jnp.zeros((rows, cols), F32)
        for z in range(planes):
            total = total + wzs[v, z] * values[z]
        sums[at + v : at + v + 1, :] = jnp.sum(total * wyx[v], axis=0, keepdims=True)


def early_adjoint_kernel(chosen, before, after, raw, blurred, wy, wx, wz, acc, halos, ya, yb, xs):
    halo = plane_halo(chosen, before, after, halos)
    adjoint_of(chosen, False, halo, raw, blurred, wy, wx, wz, ya, yb, xs, acc)


def late_adjoint_kernel(
    chosen, wzs, before, after, raw, blurred, wy, wx, wz, known_acc, current, wyx, known, out, sums, halos, ya, yb, xs, acc
):
    acc[...] = known_acc[...]
    halo = plane_halo(chosen, before, after, halos)
    adjoint_of(chosen, True, halo, raw, blurred, wy, wx, wz, ya, yb, xs, acc)
    updated(current, acc[...], raw.shape[0], out)
    sums[...] = known[...]
    weighted_sums(out, wzs, wyx, sums, 2 * sums.shape[0] // 3)


def iteration_kernel(
    parity, far_before, near, own, far_after, early, late, raw, wy, wx, wz, wya, wxa, wza,
    out, ys, blurred, ya, yb, xs, acc,
):
    views, split_at = ys.shape[0], early.shape[0]
    forward_rows(parity, far_before, near, own, far_after, wy, ys)
    each_step(views, lambda v: forward_view(ys.at[v], wx[v], wz[v], blurred.at[v]))

    def halo(v):
        return lambda z: early[v, z] if v < split_at else late[v - split_at, z]

    adjoint_of(range(views), False, halo, raw, blurred, wya, wxa, wza, ya, yb, xs, acc)
    updated(own, acc[...], views, out)


def pack_kernel(raw, last, leading):
    count, rows = last.shape[0] // raw.shape[0], raw.shape[1]
    flat = raw.reshape(raw.shape[0] * rows, raw.shape[2])
    for y in range(count):
        here = slice(y * raw.shape[0], (y + 1) * raw.shape[0])
        last[here, :] = flat[pl.ds(rows - count + y, raw.shape[0], stride=rows), :]
        leading[here, :] = flat[pl.ds(y, raw.shape[0], stride=rows), :]


def packed(raw, chosen, count):
    _, planes, rows, cols = raw.shape
    part = raw[chosen[0] : chosen[-1] + 1].reshape(len(chosen) * planes, rows, cols)
    outs = [pltpu.VMEM((count * part.shape[0], cols), F32)] * 2
    return call(pack_kernel, outs, [], [part], [], "pack", 10**6)


def scaled_kernel(views, values, part, rest, out):
    sums = jnp.sum(part[...] + rest[...], axis=1, keepdims=True)
    space = sums.shape[0] // 3
    total, first, second = (sums[i * space : i * space + views] for i in range(3))
    scale = jnp.sum(jnp.log(first / total) + jnp.log(second / total), axis=0, keepdims=True)
    out[...] = values[...] * jnp.exp(scale * (1.0 / views))[None]


def adjoint_scratch(planes, rows, cols):
    return [
        pltpu.VMEM((planes, rows, 2 * cols), BF16),
        pltpu.VMEM((planes, rows, 2 * cols), BF16),
        pltpu.VMEM((2, planes * rows, cols), F32),
    ]


def forward(parity, slabs, weights, raw, wzs, wyx):
    planes, rows, cols = slabs[0].shape
    views = raw.shape[0]
    outs = [pltpu.VMEM((views, planes, 3 * rows, cols), F32), pltpu.VMEM((24 * -(-views // 8), cols), F32)]
    scratch = [pltpu.VMEM((views, planes, 3 * rows, 2 * cols), BF16)]
    return call(forward_kernel, outs, [parity, wzs], [*slabs, *weights, raw, wyx], scratch, "forward", 10**10)


def first_adjoint(groups, current, blurred, befores, raw, afters, weights, wzs, wyx, known):
    planes, rows, cols = current.shape
    shared = (raw, blurred, *weights)
    scratch = adjoint_scratch(planes, rows, cols)
    acc = pltpu.VMEM((planes * 8, rows // 8 * cols), F32)
    halos = [pltpu.VMEM((len(g), planes, 2 * rows, cols), F32) for g in groups]
    kernel = functools.partial(early_adjoint_kernel, groups[0])
    arrays = [befores[0], afters[0], *shared]
    partial, early = call(kernel, [acc, halos[0]], [], arrays, scratch, "early_adjoint", 10**10)
    kernel = functools.partial(late_adjoint_kernel, groups[1])
    arrays = [befores[1], afters[1], *shared, partial, current, wyx, known]
    outs = [pltpu.VMEM(current.shape, F32), pltpu.VMEM(known.shape, F32), halos[1]]
    out, sums, late = call(kernel, outs, [wzs], arrays, scratch + [acc], "late_adjoint", 10**10)
    return out, sums, (early, late)


def full_iteration(parity, slabs, halos, raw, weights, adjoint_weights):
    planes, rows, cols = slabs[0].shape
    views = raw.shape[0]
    scratch = [
        pltpu.VMEM((views, planes, 3 * rows, 2 * cols), BF16),
        pltpu.VMEM((views, planes, 3 * rows, cols), F32),
    ]
    return call(
        iteration_kernel,
        pltpu.VMEM((planes, rows, cols), F32),
        [parity],
        [*slabs, *halos, raw, *weights, *adjoint_weights],
        scratch + adjoint_scratch(planes, rows, cols) + [pltpu.VMEM((planes * 8, rows // 8 * cols), F32)],
        "iteration",
        2 * 10**10,
    )


def two_slabs_away(value, count):
    up = [(i, i + 2) for i in range(count - 2)]
    down = [(j, i) for i, j in up]
    return lax.ppermute(value, "slab", up), lax.ppermute(value, "slab", down)


def with_near(value, far_before, far_after, parity, count):
    swap = [(i, i + 1 - 2 * (i % 2)) for i in range(count)]
    passed = jnp.stack([value, jnp.where(parity[0] == 0, far_after, far_before)])
    near = lax.ppermute(passed, "slab", swap)
    return far_before, near, value, far_after


def tap_sums(taps, offset, extent, total):
    count = taps.shape[1]
    target = offset + jnp.arange(extent)[None, :] - jnp.arange(count)[:, None] + count // 2
    reach = jnp.where((target >= 0) & (target < total), 1.0, 0.0).astype(F32)
    return jnp.sum(taps[:, :, None] * reach[None], axis=1)


def per_device(estimate, raw, taps):
    views = raw.shape[0]
    planes, rows, cols = estimate.shape
    count = lax.axis_size("slab")
    assert 16 == rows >= taps.shape[2] // 2 and count & (count - 1) == 0
    up = [(i, i + 1) for i in range(count - 1)]
    down = [(j, i) for i, j in up]
    place = lax.axis_index("slab")
    parity = (place % 2).reshape(1)

    far = two_slabs_away(estimate, count)
    margin = taps.shape[2] // 2
    groups = (range(0, 2 * views // 3), range(2 * views // 3, views))
    edges = [packed(raw, g, margin) for g in groups]
    forward_weights, adjoint_weights = make_weights(taps, planes, rows, cols)
    first_edges, forward_weights, adjoint_weights = lax.optimization_barrier(
        (edges[0], forward_weights, adjoint_weights)
    )
    befores = [lax.ppermute(first_edges[0], "slab", up)]
    afters = [lax.ppermute(first_edges[1], "slab", down)]

    wzs = tap_sums(taps[:, 0], 0, planes, planes)
    wy_sums = tap_sums(taps[:, 1], place * rows, rows, count * rows)
    wx_sums = tap_sums(taps[:, 2], 0, cols, cols)
    wyx = wy_sums[:, :, None] * wx_sums[:, None, :]

    far_before, near, own, far_after = with_near(estimate, *far, parity, count)
    near, last, leading = lax.optimization_barrier((near, *edges[1]))
    befores.append(lax.ppermute(last, "slab", up))
    afters.append(lax.ppermute(leading, "slab", down))
    slabs = (far_before, near, own, far_after)
    blurred, known = forward(parity, slabs, forward_weights, raw, wzs, wyx)
    current, sums, halos = first_adjoint(
        groups, estimate, blurred, befores, raw, afters, adjoint_weights, wzs, wyx, known
    )

    far = two_slabs_away(current, count)
    bits = [1 << b for b in range(count.bit_length() - 1)]
    rounds = [bits[:1], bits[2:4] + [sum(bits[2:4])], *([b] for b in bits[4:]), bits[1:2]]
    for r, distances in enumerate(rounds):
        others = [lax.ppermute(sums, "slab", [(i, i ^ d) for i in range(count)]) for d in distances]
        if r == 1:
            *far, sums = lax.optimization_barrier((*far, sums + sum(others)))
        elif r < len(rounds) - 1:
            sums = sums + sum(others)
    slabs = with_near(current, *far, parity, count)
    current = full_iteration(parity, slabs, halos, raw, forward_weights, adjoint_weights)
    out = jax.ShapeDtypeStruct(current.shape, F32)
    scaled = functools.partial(scaled_kernel, views)
    return call(scaled, out, [], [current, sums, others[0]], [], "scaled", 10**5)


def solution(mesh):
    placed = (P("blocks", "slab", None), P(None, "blocks", "slab", None), P())
    return jax.shard_map(
        per_device, mesh=mesh, in_specs=placed, out_specs=P("blocks", "slab", None), check_vma=False
    )
```

```python
import functools

import jax
import jax.numpy as jnp
import numpy as np
from jax import lax
from jax.experimental import pallas as pl
from jax.experimental.pallas import tpu as pltpu
from jax.sharding import PartitionSpec as P

F32 = jnp.float32
BF16 = jnp.bfloat16
VMEM = pltpu.MemorySpace.VMEM
SMEM = pltpu.MemorySpace.SMEM
FULL = pl.BlockSpec(memory_space=VMEM)
LIMIT = 30 * 1024 * 1024
WIDE = 4
TINY = float(np.finfo(np.float32).tiny)


def split(value):
    high = value.astype(BF16)
    low = (value - high.astype(F32)).astype(BF16)
    return high, low


def dot(a, b):
    return jnp.dot(a, b, preferred_element_type=F32)


def placed_row(taps, lane_of_tap, width):
    count = taps.shape[1]
    tap = lax.broadcasted_iota(jnp.int32, (count, width), 0)
    lane = lax.broadcasted_iota(jnp.int32, (count, width), 1)
    onehot = jnp.where(lane == lane_of_tap(tap), 1.0, 0.0).astype(F32)
    return jnp.dot(taps, onehot, precision=lax.Precision.HIGHEST, preferred_element_type=F32)


def slanted(row, height):
    full = jnp.broadcast_to(row, (height, row.shape[1]))
    return pltpu.roll(full, 0, 1, stride=1, stride_axis=0)


def weights_kernel(rows, taps_ref, *outs):
    views, _, count = taps_ref.shape
    margin = count // 2
    for flip in (False, True):
        wy, wx, wz = outs[3 * flip : 3 * flip + 3]
        order = (lambda k: count - 1 - k) if flip else (lambda k: k)
        out_rows = rows if flip else 3 * rows
        in_rows = out_rows + 2 * rows
        planes = wz.shape[1] // 8
        cols = wx.shape[1] // 2
        row_y = placed_row(taps_ref[:, 1, :], lambda k: order(k) + rows - margin, 256)
        high = row_y.astype(BF16).astype(F32)
        low = row_y - high
        if flip:
            row_y = (high, low)
        else:
            row_y = high + pltpu.roll(high, in_rows, 1) + pltpu.roll(low, 2 * in_rows, 1)
        row_x = placed_row(taps_ref[:, 2, :], lambda k: lax.rem(margin - order(k) + 2 * cols, 2 * cols), 2 * cols)
        width_z = 16 * planes
        row_z = placed_row(
            taps_ref[:, 0, :], lambda k: lax.rem(8 * (order(k) - margin) + width_z, width_z), width_z
        )
        for v in range(views):
            if flip:
                lane = lax.broadcasted_iota(jnp.int32, (rows, 256), 1)
                for j, row in enumerate(row_y):
                    band = slanted(row[v : v + 1], rows)
                    shifted = pltpu.roll(band, 256 - (rows - margin), 1)
                    band = jnp.where(lane < margin, shifted, jnp.where(lane < rows, 0.0, band))
                    band = band + pltpu.roll(band, in_rows, 1)
                    wy[v, j * rows : (j + 1) * rows, :] = band[:, : 2 * in_rows].astype(BF16)
            else:
                row = row_y[v : v + 1]
                band = jnp.concatenate(
                    [slanted(pltpu.roll(row, rows - margin, 1), rows), slanted(pltpu.roll(row, rows, 1), 2 * rows)]
                )
                wy[v * out_rows : (v + 1) * out_rows, :] = band[:, : 3 * in_rows].astype(BF16)
            high, low = split(slanted(row_x[v : v + 1], cols)[:, :cols])
            wx[v, :cols, :cols] = high
            wx[v, cols:, :cols] = high
            wx[v, :cols, cols:] = low
            wx[v, cols:, cols:] = low
            size = 8 * planes
            high, low = split(slanted(row_z[v : v + 1], size)[:, :size])
            wz[v, :, :size] = high
            wz[v, :, size : 2 * size] = high
            wz[v, :, 2 * size :] = low


def call(kernel, outs, smem, arrays, scratch, name, flops):
    arrays = [pltpu.with_memory_space_constraint(a, VMEM) for a in arrays]
    return pl.pallas_call(
        kernel,
        out_shape=outs,
        in_specs=[pl.BlockSpec(memory_space=SMEM)] * len(smem) + [FULL] * len(arrays),
        out_specs=jax.tree.map(lambda _: FULL, outs),
        scratch_shapes=scratch,
        compiler_params=pltpu.CompilerParams(vmem_limit_bytes=LIMIT),
        cost_estimate=pl.CostEstimate(flops=flops, bytes_accessed=10**7, transcendentals=10**5),
        name=name,
    )(*smem, *arrays)


def make_weights(taps, planes, rows, cols):
    views = taps.shape[0]
    outs = [
        pltpu.VMEM((views * 3 * rows, 15 * rows), BF16),
        pltpu.VMEM((views, 2 * cols, 2 * cols), BF16),
        pltpu.VMEM((views, 8 * planes, 24 * planes), BF16),
        pltpu.VMEM((views, 2 * rows, 6 * rows), BF16),
        pltpu.VMEM((views, 2 * cols, 2 * cols), BF16),
        pltpu.VMEM((views, 8 * planes, 24 * planes), BF16),
    ]
    made = call(functools.partial(weights_kernel, rows), outs, [], [taps], [], "weights", 10**10)
    return made[:3], made[3:]


def stacked(pieces):
    columns = []
    for piece in pieces:
        high, low = split(piece)
        columns.append(jnp.concatenate([high, low, high], axis=0))
    return jnp.concatenate(columns, axis=1)


def interleaved(*streams):
    keyed = [((i + 0.5) / len(s), n, piece) for n, s in enumerate(streams) for i, piece in enumerate(s)]
    for _, _, piece in sorted(keyed, key=lambda k: k[:2]):
        piece()


def along_x(rows_ref, wx, out):
    planes, height, lanes = rows_ref.shape
    cols, part = lanes // 2, planes // 4

    def piece(z):
        both = dot(rows_ref[z : z + part].reshape(part * height, lanes), wx[...])
        out[z * height : (z + part) * height, :] = both[:, :cols] + both[:, cols:]

    return [functools.partial(piece, z) for z in range(0, planes, part)]


def forward_rows(parity, far_before, near, own, far_after, wy, ys):
    planes, rows, cols = far_before.shape
    views = ys.shape[0]
    height = 3 * rows
    side = parity[0]

    def plane(z):
        return jnp.concatenate(
            [far_before[z], near[1 - side, z], own[z], near[side, z], far_after[z]], axis=0
        )

    for z in range(0, planes, 2):
        high, low = split(dot(wy[...], stacked([plane(z), plane(z + 1)])))
        for j in range(2):
            for v in range(views):
                there = (slice(v * height, (v + 1) * height), slice(j * cols, (j + 1) * cols))
                ys[v, z + j, :, :cols] = high[there]
                ys[v, z + j, :, cols:] = low[there]


def forward_view(ys, wx, wz, out):
    planes, height, lanes = ys.shape
    cols = lanes // 2
    groups = []
    for pair in range(height // 16):
        rows_in = ys[:, 16 * pair : 16 * pair + 16, :].reshape(planes * 16, lanes)
        both = dot(rows_in, wx)
        value = (both[:, :cols] + both[:, cols:]).reshape(planes, 16, cols)
        groups += [value[:, 8 * g : 8 * g + 8, :].reshape(planes * 8, cols) for g in range(2)]
    result = dot(wz, stacked(groups))
    for g in range(len(groups)):
        out[:, 8 * g : 8 * g + 8, :] = result[:, g * cols : (g + 1) * cols].reshape(planes, 8, cols)


def adjoint_rows(halo, raw, blurred, wy, ya):
    planes, rows, cols = raw.shape

    def quotient(z):
        around = halo(z)
        counts = jnp.concatenate([around[:rows], raw[z], around[rows:]], axis=0)
        return counts * pl.reciprocal(jnp.maximum(blurred[z], TINY), approx=True)

    def piece(z):
        high, low = split(jnp.concatenate([quotient(z + j) for j in range(WIDE)], axis=1))
        both = dot(wy[...], jnp.concatenate([high, low], axis=0))
        high, low = split(both[:rows] + both[rows:])
        for j in range(WIDE):
            ya[z + j, :, :cols] = high[:, j * cols : (j + 1) * cols]
            ya[z + j, :, cols:] = low[:, j * cols : (j + 1) * cols]

    return [functools.partial(piece, z) for z in range(0, planes, WIDE)]


def adjoint_logs(first, ya, wx, wz, xs, acc):
    planes, rows, lanes = ya.shape
    cols = lanes // 2

    def piece():
        value = xs[...].reshape(planes, rows, cols)
        groups = [value[:, 8 * g : 8 * g + 8, :].reshape(planes * 8, cols) for g in range(2)]
        result = jnp.log(dot(wz[...], stacked(groups)))
        acc[...] = result if first else acc[...] + result

    return along_x(ya, wx, xs) + [piece]


def adjoint_of(chosen, begun, halo, raw, blurred, wy, wx, wz, ya, yb, xs, acc):
    def rows_of(i):
        if i == len(chosen):
            return []
        v = chosen[i]
        return adjoint_rows(halo(v), raw.at[v], blurred.at[v], wy.at[v], (ya, yb)[i % 2])

    interleaved(rows_of(0))
    for i, v in enumerate(chosen):
        logs = adjoint_logs(i == 0 and not begun, (ya, yb)[i % 2], wx.at[v], wz.at[v], xs.at[i % 2], acc)
        interleaved(logs, rows_of(i + 1))


def updated(current, acc, views, out):
    planes, rows, cols = out.shape
    for g in range(rows // 8):
        here = slice(8 * g, 8 * g + 8)
        exponent = acc[:, g * cols : (g + 1) * cols].reshape(planes, 8, cols) * (1.0 / views)
        out[:, here, :] = current[:, here, :] * jnp.exp(exponent)


def plane_halo(chosen, before, after, halos):
    planes, rows = halos.shape[1], halos.shape[2] // 2
    stride = len(chosen) * planes
    count = before.shape[0] // stride
    empty = jnp.zeros((rows - count, before.shape[1]), F32)

    def of_view(v):
        i = v - chosen[0]

        def of_plane(z):
            at = pl.ds(i * planes + z, count, stride=stride)
            around = jnp.concatenate([before[at, :], empty, after[at, :], empty], axis=0)
            halos[i, z] = around
            return around

        return of_plane

    return of_view


def each_step(steps, body):
    def run(step, _):
        body(step)
        return 0

    lax.fori_loop(0, steps, run, 0)


def forward_kernel(parity, wzs, far_before, near, own, far_after, wy, wx, wz, raw, wyx, out, sums, ys):
    views = ys.shape[0]
    forward_rows(parity, far_before, near, own, far_after, wy, ys)
    each_step(views, lambda v: forward_view(ys.at[v], wx[v], wz[v], out.at[v]))
    sums[...] = jnp.zeros_like(sums)
    for v in range(views):
        sums[v : v + 1, :] = jnp.sum(jnp.sum(raw[v], axis=0), axis=0, keepdims=True)
    weighted_sums(own, wzs, wyx, sums, sums.shape[0] // 3)


def weighted_sums(values, wzs, wyx, sums, at):
    planes, rows, cols = values.shape
    for v in range(wyx.shape[0]):
        total = jnp.zeros((rows, cols), F32)
        for z in range(planes):
            total = total + wzs[v, z] * values[z]
        sums[at + v : at + v + 1, :] = jnp.sum(total * wyx[v], axis=0, keepdims=True)


def early_adjoint_kernel(chosen, before, after, raw, blurred, wy, wx, wz, acc, halos, ya, yb, xs):
    halo = plane_halo(chosen, before, after, halos)
    adjoint_of(chosen, False, halo, raw, blurred, wy, wx, wz, ya, yb, xs, acc)


def late_adjoint_kernel(
    chosen, wzs, before, after, raw, blurred, wy, wx, wz, known_acc, current, wyx, known, out, sums, halos, ya, yb, xs, acc
):
    acc[...] = known_acc[...]
    halo = plane_halo(chosen, before, after, halos)
    adjoint_of(chosen, True, halo, raw, blurred, wy, wx, wz, ya, yb, xs, acc)
    updated(current, acc[...], raw.shape[0], out)
    sums[...] = known[...]
    weighted_sums(out, wzs, wyx, sums, 2 * sums.shape[0] // 3)


def iteration_kernel(
    parity, far_before, near, own, far_after, early, late, raw, wy, wx, wz, wya, wxa, wza,
    out, ys, blurred, ya, yb, xs, acc,
):
    views, split_at = ys.shape[0], early.shape[0]
    forward_rows(parity, far_before, near, own, far_after, wy, ys)
    each_step(views, lambda v: forward_view(ys.at[v], wx[v], wz[v], blurred.at[v]))

    def halo(v):
        return lambda z: early[v, z] if v < split_at else late[v - split_at, z]

    adjoint_of(range(views), False, halo, raw, blurred, wya, wxa, wza, ya, yb, xs, acc)
    updated(own, acc[...], views, out)


def pack_kernel(raw, *refs):
    last, leading = refs[-2:]
    count, rows = last.shape[0] // raw.shape[0], raw.shape[1]
    flat = raw.reshape(raw.shape[0] * rows, raw.shape[2])
    for y in range(count):
        here = slice(y * raw.shape[0], (y + 1) * raw.shape[0])
        last[here, :] = flat[pl.ds(rows - count + y, raw.shape[0], stride=rows), :]
        leading[here, :] = flat[pl.ds(y, raw.shape[0], stride=rows), :]


def packed(raw, chosen, count, *awaited):
    _, planes, rows, cols = raw.shape
    part = raw[chosen[0] : chosen[-1] + 1].reshape(len(chosen) * planes, rows, cols)
    outs = [pltpu.VMEM((count * part.shape[0], cols), F32)] * 2
    return call(pack_kernel, outs, [], [part, *awaited], [], "pack", 10**6)


def scaled_kernel(views, values, part, rest, out):
    sums = jnp.sum(part[...] + rest[...], axis=1, keepdims=True)
    space = sums.shape[0] // 3
    total, first, second = (sums[i * space : i * space + views] for i in range(3))
    scale = jnp.sum(jnp.log(first / total) + jnp.log(second / total), axis=0, keepdims=True)
    out[...] = values[...] * jnp.exp(scale * (1.0 / views))[None]


def adjoint_scratch(planes, rows, cols):
    return [
        pltpu.VMEM((planes, rows, 2 * cols), BF16),
        pltpu.VMEM((planes, rows, 2 * cols), BF16),
        pltpu.VMEM((2, planes * rows, cols), F32),
    ]


def forward(parity, slabs, weights, raw, wzs, wyx):
    planes, rows, cols = slabs[0].shape
    views = raw.shape[0]
    outs = [pltpu.VMEM((views, planes, 3 * rows, cols), F32), pltpu.VMEM((24 * -(-views // 8), cols), F32)]
    scratch = [pltpu.VMEM((views, planes, 3 * rows, 2 * cols), BF16)]
    return call(forward_kernel, outs, [parity, wzs], [*slabs, *weights, raw, wyx], scratch, "forward", 10**10)


def first_adjoint(groups, current, blurred, befores, raw, afters, weights, wzs, wyx, known):
    planes, rows, cols = current.shape
    shared = (raw, blurred, *weights)
    scratch = adjoint_scratch(planes, rows, cols)
    acc = pltpu.VMEM((planes * 8, rows // 8 * cols), F32)
    halos = [pltpu.VMEM((len(g), planes, 2 * rows, cols), F32) for g in groups]
    kernel = functools.partial(early_adjoint_kernel, groups[0])
    arrays = [befores[0], afters[0], *shared]
    partial, early = call(kernel, [acc, halos[0]], [], arrays, scratch, "early_adjoint", 10**10)
    kernel = functools.partial(late_adjoint_kernel, groups[1])
    arrays = [befores[1], afters[1], *shared, partial, current, wyx, known]
    outs = [pltpu.VMEM(current.shape, F32), pltpu.VMEM(known.shape, F32), halos[1]]
    out, sums, late = call(kernel, outs, [wzs], arrays, scratch + [acc], "late_adjoint", 10**10)
    return out, sums, (early, late)


def full_iteration(parity, slabs, halos, raw, weights, adjoint_weights):
    planes, rows, cols = slabs[0].shape
    views = raw.shape[0]
    scratch = [
        pltpu.VMEM((views, planes, 3 * rows, 2 * cols), BF16),
        pltpu.VMEM((views, planes, 3 * rows, cols), F32),
    ]
    return call(
        iteration_kernel,
        pltpu.VMEM((planes, rows, cols), F32),
        [parity],
        [*slabs, *halos, raw, *weights, *adjoint_weights],
        scratch + adjoint_scratch(planes, rows, cols) + [pltpu.VMEM((planes * 8, rows // 8 * cols), F32)],
        "iteration",
        2 * 10**10,
    )


def two_slabs_away(value, count):
    up = [(i, i + 2) for i in range(count - 2)]
    down = [(j, i) for i, j in up]
    return lax.ppermute(value, "slab", up), lax.ppermute(value, "slab", down)


def with_near(value, far_before, far_after, parity, count):
    swap = [(i, i + 1 - 2 * (i % 2)) for i in range(count)]
    passed = jnp.stack([value, jnp.where(parity[0] == 0, far_after, far_before)])
    near = lax.ppermute(passed, "slab", swap)
    return far_before, near, value, far_after


def tap_sums(taps, offset, extent, total):
    count = taps.shape[1]
    target = offset + jnp.arange(extent)[None, :] - jnp.arange(count)[:, None] + count // 2
    reach = jnp.where((target >= 0) & (target < total), 1.0, 0.0).astype(F32)
    return jnp.sum(taps[:, :, None] * reach[None], axis=1)


def per_device(estimate, raw, taps):
    views = raw.shape[0]
    planes, rows, cols = estimate.shape
    count = lax.axis_size("slab")
    assert 16 == rows >= taps.shape[2] // 2 and count & (count - 1) == 0
    up = [(i, i + 1) for i in range(count - 1)]
    down = [(j, i) for i, j in up]
    place = lax.axis_index("slab")
    parity = (place % 2).reshape(1)

    far = two_slabs_away(estimate, count)
    margin = taps.shape[2] // 2
    groups = (range(0, 2 * views // 3), range(2 * views // 3, views))
    edges = packed(raw, groups[0], margin)
    forward_weights, adjoint_weights = make_weights(taps, planes, rows, cols)
    befores = [lax.ppermute(edges[0], "slab", up)]
    afters = [lax.ppermute(edges[1], "slab", down)]

    wzs = tap_sums(taps[:, 0], 0, planes, planes)
    wy_sums = tap_sums(taps[:, 1], place * rows, rows, count * rows)
    wx_sums = tap_sums(taps[:, 2], 0, cols, cols)
    wyx = wy_sums[:, :, None] * wx_sums[:, None, :]

    far_before, near, own, far_after = with_near(estimate, *far, parity, count)
    edges = packed(raw, groups[1], margin, near)
    befores.append(lax.ppermute(edges[0], "slab", up))
    afters.append(lax.ppermute(edges[1], "slab", down))
    slabs = (far_before, near, own, far_after)
    blurred, known = forward(parity, slabs, forward_weights, raw, wzs, wyx)
    current, sums, halos = first_adjoint(
        groups, estimate, blurred, befores, raw, afters, adjoint_weights, wzs, wyx, known
    )

    far = two_slabs_away(current, count)
    bits = [1 << b for b in range(count.bit_length() - 1)]
    rounds = [bits[:1], bits[2:4] + [sum(bits[2:4])], *([b] for b in bits[4:]), bits[1:2]]
    for r, distances in enumerate(rounds):
        others = [lax.ppermute(sums, "slab", [(i, i ^ d) for i in range(count)]) for d in distances]
        if r == 1:
            *far, sums = lax.optimization_barrier((*far, sums + sum(others)))
        elif r < len(rounds) - 1:
            sums = sums + sum(others)
    slabs = with_near(current, *far, parity, count)
    current = full_iteration(parity, slabs, halos, raw, forward_weights, adjoint_weights)
    out = jax.ShapeDtypeStruct(current.shape, F32)
    scaled = functools.partial(scaled_kernel, views)
    return call(scaled, out, [], [current, sums, others[0]], [], "scaled", 10**5)


def solution(mesh):
    placed = (P("blocks", "slab", None), P(None, "blocks", "slab", None), P())
    return jax.shard_map(
        per_device, mesh=mesh, in_specs=placed, out_specs=P("blocks", "slab", None), check_vma=False
    )
```

```python
import functools

import jax
import jax.numpy as jnp
import numpy as np
from jax import lax
from jax.experimental import pallas as pl
from jax.experimental.pallas import tpu as pltpu
from jax.sharding import PartitionSpec as P

F32 = jnp.float32
BF16 = jnp.bfloat16
VMEM = pltpu.MemorySpace.VMEM
SMEM = pltpu.MemorySpace.SMEM
FULL = pl.BlockSpec(memory_space=VMEM)
LIMIT = 20 * 1024 * 1024
WIDE = 4
TINY = float(np.finfo(np.float32).tiny)


def split(value):
    high = value.astype(BF16)
    low = (value - high.astype(F32)).astype(BF16)
    return high, low


def dot(a, b):
    return jnp.dot(a, b, preferred_element_type=F32)


def placed_row(taps, lane_of_tap, width):
    count = taps.shape[1]
    tap = lax.broadcasted_iota(jnp.int32, (count, width), 0)
    lane = lax.broadcasted_iota(jnp.int32, (count, width), 1)
    onehot = jnp.where(lane == lane_of_tap(tap), 1.0, 0.0).astype(F32)
    return jnp.dot(taps, onehot, precision=lax.Precision.HIGHEST, preferred_element_type=F32)


def slanted(row, height):
    full = jnp.broadcast_to(row, (height, row.shape[1]))
    return pltpu.roll(full, 0, 1, stride=1, stride_axis=0)


def weights_kernel(rows, taps_ref, *outs):
    views, _, count = taps_ref.shape
    margin = count // 2
    for flip in (False, True):
        wy, wx, wz = outs[3 * flip : 3 * flip + 3]
        order = (lambda k: count - 1 - k) if flip else (lambda k: k)
        out_rows = rows if flip else 3 * rows
        in_rows = out_rows + 2 * rows
        planes = wz.shape[1] // 8
        cols = wx.shape[1] // 2
        row_y = placed_row(taps_ref[:, 1, :], lambda k: order(k) + rows - margin, 256)
        high = row_y.astype(BF16).astype(F32)
        low = row_y - high
        if flip:
            row_y = (high, low)
        else:
            row_y = high + pltpu.roll(high, in_rows, 1) + pltpu.roll(low, 2 * in_rows, 1)
        row_x = placed_row(taps_ref[:, 2, :], lambda k: lax.rem(margin - order(k) + 2 * cols, 2 * cols), 2 * cols)
        width_z = 16 * planes
        row_z = placed_row(
            taps_ref[:, 0, :], lambda k: lax.rem(8 * (order(k) - margin) + width_z, width_z), width_z
        )
        for v in range(views):
            if flip:
                lane = lax.broadcasted_iota(jnp.int32, (rows, 256), 1)
                for j, row in enumerate(row_y):
                    band = slanted(row[v : v + 1], rows)
                    shifted = pltpu.roll(band, 256 - (rows - margin), 1)
                    band = jnp.where(lane < margin, shifted, jnp.where(lane < rows, 0.0, band))
                    band = band + pltpu.roll(band, in_rows, 1)
                    wy[v, j * rows : (j + 1) * rows, :] = band[:, : 2 * in_rows].astype(BF16)
            else:
                row = row_y[v : v + 1]
                band = jnp.concatenate(
                    [slanted(pltpu.roll(row, rows - margin, 1), rows), slanted(pltpu.roll(row, rows, 1), 2 * rows)]
                )
                wy[v * out_rows : (v + 1) * out_rows, :] = band[:, : 3 * in_rows].astype(BF16)
            high, low = split(slanted(row_x[v : v + 1], cols)[:, :cols])
            wx[v, :cols, :cols] = high
            wx[v, cols:, :cols] = high
            wx[v, :cols, cols:] = low
            wx[v, cols:, cols:] = low
            size = 8 * planes
            high, low = split(slanted(row_z[v : v + 1], size)[:, :size])
            wz[v, :, :size] = high
            wz[v, :, size : 2 * size] = high
            wz[v, :, 2 * size :] = low


def call(kernel, outs, smem, arrays, scratch, name, flops):
    arrays = [pltpu.with_memory_space_constraint(a, VMEM) for a in arrays]
    return pl.pallas_call(
        kernel,
        out_shape=outs,
        in_specs=[pl.BlockSpec(memory_space=SMEM)] * len(smem) + [FULL] * len(arrays),
        out_specs=jax.tree.map(lambda _: FULL, outs),
        scratch_shapes=scratch,
        compiler_params=pltpu.CompilerParams(vmem_limit_bytes=LIMIT),
        cost_estimate=pl.CostEstimate(flops=flops, bytes_accessed=10**7, transcendentals=10**5),
        name=name,
    )(*smem, *arrays)


def make_weights(taps, planes, rows, cols):
    views = taps.shape[0]
    outs = [
        pltpu.VMEM((views * 3 * rows, 15 * rows), BF16),
        pltpu.VMEM((views, 2 * cols, 2 * cols), BF16),
        pltpu.VMEM((views, 8 * planes, 24 * planes), BF16),
        pltpu.VMEM((views, 2 * rows, 6 * rows), BF16),
        pltpu.VMEM((views, 2 * cols, 2 * cols), BF16),
        pltpu.VMEM((views, 8 * planes, 24 * planes), BF16),
    ]
    made = call(functools.partial(weights_kernel, rows), outs, [], [taps], [], "weights", 10**10)
    return made[:3], made[3:]


def stacked(pieces):
    columns = []
    for piece in pieces:
        high, low = split(piece)
        columns.append(jnp.concatenate([high, low, high], axis=0))
    return jnp.concatenate(columns, axis=1)


def interleaved(*streams):
    keyed = [((i + 0.5) / len(s), n, piece) for n, s in enumerate(streams) for i, piece in enumerate(s)]
    for _, _, piece in sorted(keyed, key=lambda k: k[:2]):
        piece()


def along_x(rows_ref, wx, out):
    planes, height, lanes = rows_ref.shape
    cols, part = lanes // 2, planes // 4

    def piece(z):
        both = dot(rows_ref[z : z + part].reshape(part * height, lanes), wx[...])
        out[z * height : (z + part) * height, :] = both[:, :cols] + both[:, cols:]

    return [functools.partial(piece, z) for z in range(0, planes, part)]


def forward_rows(parity, far_before, near, own, far_after, wy, ys):
    planes, rows, cols = far_before.shape
    views = ys.shape[0]
    height = 3 * rows
    side = parity[0]

    def plane(z):
        return jnp.concatenate(
            [far_before[z], near[1 - side, z], own[z], near[side, z], far_after[z]], axis=0
        )

    for z in range(0, planes, 2):
        high, low = split(dot(wy[...], stacked([plane(z), plane(z + 1)])))
        for j in range(2):
            for v in range(views):
                there = (slice(v * height, (v + 1) * height), slice(j * cols, (j + 1) * cols))
                ys[v, z + j, :, :cols] = high[there]
                ys[v, z + j, :, cols:] = low[there]


def forward_view(ys, wx, wz, out):
    planes, height, lanes = ys.shape
    cols = lanes // 2
    groups = []
    for pair in range(height // 16):
        rows_in = ys[:, 16 * pair : 16 * pair + 16, :].reshape(planes * 16, lanes)
        both = dot(rows_in, wx)
        value = (both[:, :cols] + both[:, cols:]).reshape(planes, 16, cols)
        groups += [value[:, 8 * g : 8 * g + 8, :].reshape(planes * 8, cols) for g in range(2)]
    result = dot(wz, stacked(groups))
    for g in range(len(groups)):
        out[:, 8 * g : 8 * g + 8, :] = result[:, g * cols : (g + 1) * cols].reshape(planes, 8, cols)


def adjoint_rows(halo, raw, blurred, wy, ya):
    planes, rows, cols = raw.shape

    def quotient(z):
        around = halo(z)
        counts = jnp.concatenate([around[:rows], raw[z], around[rows:]], axis=0)
        return counts * pl.reciprocal(jnp.maximum(blurred[z], TINY), approx=True)

    def piece(z):
        high, low = split(jnp.concatenate([quotient(z + j) for j in range(WIDE)], axis=1))
        both = dot(wy[...], jnp.concatenate([high, low], axis=0))
        high, low = split(both[:rows] + both[rows:])
        for j in range(WIDE):
            ya[z + j, :, :cols] = high[:, j * cols : (j + 1) * cols]
            ya[z + j, :, cols:] = low[:, j * cols : (j + 1) * cols]

    return [functools.partial(piece, z) for z in range(0, planes, WIDE)]


def adjoint_logs(first, ya, wx, wz, xs, acc):
    planes, rows, lanes = ya.shape
    cols = lanes // 2

    def piece():
        value = xs[...].reshape(planes, rows, cols)
        groups = [value[:, 8 * g : 8 * g + 8, :].reshape(planes * 8, cols) for g in range(2)]
        result = jnp.log(dot(wz[...], stacked(groups)))
        acc[...] = result if first else acc[...] + result

    return along_x(ya, wx, xs) + [piece]


def adjoint_of(chosen, begun, halo, raw, blurred, wy, wx, wz, ya, yb, xs, acc):
    def rows_of(i):
        if i == len(chosen):
            return []
        v = chosen[i]
        return adjoint_rows(halo(v), raw.at[v], blurred.at[v], wy.at[v], (ya, yb)[i % 2])

    interleaved(rows_of(0))
    for i, v in enumerate(chosen):
        logs = adjoint_logs(i == 0 and not begun, (ya, yb)[i % 2], wx.at[v], wz.at[v], xs.at[i % 2], acc)
        interleaved(logs, rows_of(i + 1))


def updated(current, acc, views, out):
    planes, rows, cols = out.shape
    for g in range(rows // 8):
        here = slice(8 * g, 8 * g + 8)
        exponent = acc[:, g * cols : (g + 1) * cols].reshape(planes, 8, cols) * (1.0 / views)
        out[:, here, :] = current[:, here, :] * jnp.exp(exponent)


def plane_halo(chosen, before, after, halos):
    planes, rows = halos.shape[1], halos.shape[2] // 2
    stride = len(chosen) * planes
    count = before.shape[0] // stride
    empty = jnp.zeros((rows - count, before.shape[1]), F32)

    def of_view(v):
        i = v - chosen[0]

        def of_plane(z):
            at = pl.ds(i * planes + z, count, stride=stride)
            around = jnp.concatenate([before[at, :], empty, after[at, :], empty], axis=0)
            halos[i, z] = around
            return around

        return of_plane

    return of_view


def each_step(steps, body):
    def run(step, _):
        body(step)
        return 0

    lax.fori_loop(0, steps, run, 0)


def forward_kernel(parity, wzs, far_before, near, own, far_after, wy, wx, wz, raw, wyx, out, sums, ys):
    views = ys.shape[0]
    forward_rows(parity, far_before, near, own, far_after, wy, ys)
    each_step(views, lambda v: forward_view(ys.at[v], wx[v], wz[v], out.at[v]))
    sums[...] = jnp.zeros_like(sums)
    for v in range(views):
        sums[v : v + 1, :] = jnp.sum(jnp.sum(raw[v], axis=0), axis=0, keepdims=True)
    weighted_sums(own, wzs, wyx, sums, sums.shape[0] // 3)


def weighted_sums(values, wzs, wyx, sums, at):
    planes, rows, cols = values.shape
    for v in range(wyx.shape[0]):
        total = jnp.zeros((rows, cols), F32)
        for z in range(planes):
            total = total + wzs[v, z] * values[z]
        sums[at + v : at + v + 1, :] = jnp.sum(total * wyx[v], axis=0, keepdims=True)


def early_adjoint_kernel(chosen, before, after, raw, blurred, wy, wx, wz, acc, halos, ya, yb, xs):
    halo = plane_halo(chosen, before, after, halos)
    adjoint_of(chosen, False, halo, raw, blurred, wy, wx, wz, ya, yb, xs, acc)


def late_adjoint_kernel(
    chosen, wzs, before, after, raw, blurred, wy, wx, wz, known_acc, current, wyx, known, out, sums, halos, ya, yb, xs, acc
):
    acc[...] = known_acc[...]
    halo = plane_halo(chosen, before, after, halos)
    adjoint_of(chosen, True, halo, raw, blurred, wy, wx, wz, ya, yb, xs, acc)
    updated(current, acc[...], raw.shape[0], out)
    sums[...] = known[...]
    weighted_sums(out, wzs, wyx, sums, 2 * sums.shape[0] // 3)


def iteration_kernel(
    parity, far_before, near, own, far_after, early, late, raw, wy, wx, wz, wya, wxa, wza,
    out, ys, blurred, ya, yb, xs, acc,
):
    views, split_at = ys.shape[0], early.shape[0]
    forward_rows(parity, far_before, near, own, far_after, wy, ys)
    each_step(views, lambda v: forward_view(ys.at[v], wx[v], wz[v], blurred.at[v]))

    def halo(v):
        return lambda z: early[v, z] if v < split_at else late[v - split_at, z]

    adjoint_of(range(views), False, halo, raw, blurred, wya, wxa, wza, ya, yb, xs, acc)
    updated(own, acc[...], views, out)


def pack_kernel(raw, *refs):
    last, leading = refs[-2:]
    count, rows = last.shape[0] // raw.shape[0], raw.shape[1]
    flat = raw.reshape(raw.shape[0] * rows, raw.shape[2])
    for y in range(count):
        here = slice(y * raw.shape[0], (y + 1) * raw.shape[0])
        last[here, :] = flat[pl.ds(rows - count + y, raw.shape[0], stride=rows), :]
        leading[here, :] = flat[pl.ds(y, raw.shape[0], stride=rows), :]


def packed(raw, chosen, count, *awaited):
    _, planes, rows, cols = raw.shape
    part = raw[chosen[0] : chosen[-1] + 1].reshape(len(chosen) * planes, rows, cols)
    outs = [pltpu.VMEM((count * part.shape[0], cols), F32)] * 2
    return call(pack_kernel, outs, [], [part, *awaited], [], "pack", 10**6)


def scaled_kernel(views, values, part, rest, out):
    sums = jnp.sum(part[...] + rest[...], axis=1, keepdims=True)
    space = sums.shape[0] // 3
    total, first, second = (sums[i * space : i * space + views] for i in range(3))
    scale = jnp.sum(jnp.log(first / total) + jnp.log(second / total), axis=0, keepdims=True)
    out[...] = values[...] * jnp.exp(scale * (1.0 / views))[None]


def adjoint_scratch(planes, rows, cols):
    return [
        pltpu.VMEM((planes, rows, 2 * cols), BF16),
        pltpu.VMEM((planes, rows, 2 * cols), BF16),
        pltpu.VMEM((2, planes * rows, cols), F32),
    ]


def forward(parity, slabs, weights, raw, wzs, wyx):
    planes, rows, cols = slabs[0].shape
    views = raw.shape[0]
    outs = [pltpu.VMEM((views, planes, 3 * rows, cols), F32), pltpu.VMEM((24 * -(-views // 8), cols), F32)]
    scratch = [pltpu.VMEM((views, planes, 3 * rows, 2 * cols), BF16)]
    return call(forward_kernel, outs, [parity, wzs], [*slabs, *weights, raw, wyx], scratch, "forward", 10**10)


def first_adjoint(groups, current, blurred, befores, raw, afters, weights, wzs, wyx, known):
    planes, rows, cols = current.shape
    shared = (raw, blurred, *weights)
    scratch = adjoint_scratch(planes, rows, cols)
    acc = pltpu.VMEM((planes * 8, rows // 8 * cols), F32)
    halos = [pltpu.VMEM((len(g), planes, 2 * rows, cols), F32) for g in groups]
    kernel = functools.partial(early_adjoint_kernel, groups[0])
    arrays = [befores[0], afters[0], *shared]
    partial, early = call(kernel, [acc, halos[0]], [], arrays, scratch, "early_adjoint", 10**10)
    kernel = functools.partial(late_adjoint_kernel, groups[1])
    arrays = [befores[1], afters[1], *shared, partial, current, wyx, known]
    outs = [pltpu.VMEM(current.shape, F32), pltpu.VMEM(known.shape, F32), halos[1]]
    out, sums, late = call(kernel, outs, [wzs], arrays, scratch + [acc], "late_adjoint", 10**10)
    return out, sums, (early, late)


def full_iteration(parity, slabs, halos, raw, weights, adjoint_weights):
    planes, rows, cols = slabs[0].shape
    views = raw.shape[0]
    scratch = [
        pltpu.VMEM((views, planes, 3 * rows, 2 * cols), BF16),
        pltpu.VMEM((views, planes, 3 * rows, cols), F32),
    ]
    return call(
        iteration_kernel,
        pltpu.VMEM((planes, rows, cols), F32),
        [parity],
        [*slabs, *halos, raw, *weights, *adjoint_weights],
        scratch + adjoint_scratch(planes, rows, cols) + [pltpu.VMEM((planes * 8, rows // 8 * cols), F32)],
        "iteration",
        2 * 10**10,
    )


def two_slabs_away(value, count):
    up = [(i, i + 2) for i in range(count - 2)]
    down = [(j, i) for i, j in up]
    return lax.ppermute(value, "slab", up), lax.ppermute(value, "slab", down)


def with_near(value, far_before, far_after, parity, count):
    swap = [(i, i + 1 - 2 * (i % 2)) for i in range(count)]
    passed = jnp.stack([value, jnp.where(parity[0] == 0, far_after, far_before)])
    near = lax.ppermute(passed, "slab", swap)
    return far_before, near, value, far_after


def tap_sums(taps, offset, extent, total):
    count = taps.shape[1]
    target = offset + jnp.arange(extent)[None, :] - jnp.arange(count)[:, None] + count // 2
    reach = jnp.where((target >= 0) & (target < total), 1.0, 0.0).astype(F32)
    return jnp.sum(taps[:, :, None] * reach[None], axis=1)


def per_device(estimate, raw, taps):
    views = raw.shape[0]
    planes, rows, cols = estimate.shape
    count = lax.axis_size("slab")
    assert 16 == rows >= taps.shape[2] // 2 and count & (count - 1) == 0
    up = [(i, i + 1) for i in range(count - 1)]
    down = [(j, i) for i, j in up]
    place = lax.axis_index("slab")
    parity = (place % 2).reshape(1)

    far = two_slabs_away(estimate, count)
    margin = taps.shape[2] // 2
    groups = (range(0, 2 * views // 3), range(2 * views // 3, views))
    edges = packed(raw, groups[0], margin)
    forward_weights, adjoint_weights = make_weights(taps, planes, rows, cols)
    befores = [lax.ppermute(edges[0], "slab", up)]
    afters = [lax.ppermute(edges[1], "slab", down)]

    wzs = tap_sums(taps[:, 0], 0, planes, planes)
    wy_sums = tap_sums(taps[:, 1], place * rows, rows, count * rows)
    wx_sums = tap_sums(taps[:, 2], 0, cols, cols)
    wyx = wy_sums[:, :, None] * wx_sums[:, None, :]

    far_before, near, own, far_after = with_near(estimate, *far, parity, count)
    edges = packed(raw, groups[1], margin, near)
    befores.append(lax.ppermute(edges[0], "slab", up))
    afters.append(lax.ppermute(edges[1], "slab", down))
    slabs = (far_before, near, own, far_after)
    blurred, known = forward(parity, slabs, forward_weights, raw, wzs, wyx)
    current, sums, halos = first_adjoint(
        groups, estimate, blurred, befores, raw, afters, adjoint_weights, wzs, wyx, known
    )

    far = two_slabs_away(current, count)
    bits = [1 << b for b in range(count.bit_length() - 1)]
    rounds = [bits[:1], bits[2:4] + [sum(bits[2:4])], *([b] for b in bits[4:]), bits[1:2]]
    for r, distances in enumerate(rounds):
        others = [lax.ppermute(sums, "slab", [(i, i ^ d) for i in range(count)]) for d in distances]
        if r == 1:
            *far, sums = lax.optimization_barrier((*far, sums + sum(others)))
        elif r < len(rounds) - 1:
            sums = sums + sum(others)
    slabs = with_near(current, *far, parity, count)
    current = full_iteration(parity, slabs, halos, raw, forward_weights, adjoint_weights)
    out = jax.ShapeDtypeStruct(current.shape, F32)
    scaled = functools.partial(scaled_kernel, views)
    return call(scaled, out, [], [current, sums, others[0]], [], "scaled", 10**5)


def solution(mesh):
    placed = (P("blocks", "slab", None), P(None, "blocks", "slab", None), P())
    return jax.shard_map(
        per_device, mesh=mesh, in_specs=placed, out_specs=P("blocks", "slab", None), check_vma=False
    )
```

```python
import functools

import jax
import jax.numpy as jnp
import numpy as np
from jax import lax
from jax.experimental import pallas as pl
from jax.experimental.pallas import tpu as pltpu
from jax.sharding import PartitionSpec as P

F32 = jnp.float32
BF16 = jnp.bfloat16
VMEM = pltpu.MemorySpace.VMEM
SMEM = pltpu.MemorySpace.SMEM
FULL = pl.BlockSpec(memory_space=VMEM)
LIMIT = 20 * 1024 * 1024
WIDE = 4
TINY = float(np.finfo(np.float32).tiny)


def split(value):
    high = value.astype(BF16)
    low = (value - high.astype(F32)).astype(BF16)
    return high, low


def dot(a, b):
    return jnp.dot(a, b, preferred_element_type=F32)


def placed_row(taps, lane_of_tap, width):
    count = taps.shape[1]
    tap = lax.broadcasted_iota(jnp.int32, (count, width), 0)
    lane = lax.broadcasted_iota(jnp.int32, (count, width), 1)
    onehot = jnp.where(lane == lane_of_tap(tap), 1.0, 0.0).astype(F32)
    return jnp.dot(taps, onehot, precision=lax.Precision.HIGHEST, preferred_element_type=F32)


def slanted(row, height):
    full = jnp.broadcast_to(row, (height, row.shape[1]))
    return pltpu.roll(full, 0, 1, stride=1, stride_axis=0)


def weights_kernel(rows, taps_ref, *outs):
    views, _, count = taps_ref.shape
    margin = count // 2
    for flip in (False, True):
        wy, wx, wz = outs[3 * flip : 3 * flip + 3]
        order = (lambda k: count - 1 - k) if flip else (lambda k: k)
        out_rows = rows if flip else 3 * rows
        in_rows = out_rows + 2 * rows
        planes = wz.shape[1] // 8
        cols = wx.shape[1] // 2
        row_y = placed_row(taps_ref[:, 1, :], lambda k: order(k) + rows - margin, 256)
        high = row_y.astype(BF16).astype(F32)
        low = row_y - high
        if flip:
            row_y = (high, low)
        else:
            row_y = high + pltpu.roll(high, in_rows, 1) + pltpu.roll(low, 2 * in_rows, 1)
        row_x = placed_row(taps_ref[:, 2, :], lambda k: lax.rem(margin - order(k) + 2 * cols, 2 * cols), 2 * cols)
        width_z = 16 * planes
        row_z = placed_row(
            taps_ref[:, 0, :], lambda k: lax.rem(8 * (order(k) - margin) + width_z, width_z), width_z
        )
        for v in range(views):
            if flip:
                lane = lax.broadcasted_iota(jnp.int32, (rows, 256), 1)
                for j, row in enumerate(row_y):
                    band = slanted(row[v : v + 1], rows)
                    shifted = pltpu.roll(band, 256 - (rows - margin), 1)
                    band = jnp.where(lane < margin, shifted, jnp.where(lane < rows, 0.0, band))
                    band = band + pltpu.roll(band, in_rows, 1)
                    wy[v, j * rows : (j + 1) * rows, :] = band[:, : 2 * in_rows].astype(BF16)
            else:
                row = row_y[v : v + 1]
                band = jnp.concatenate(
                    [slanted(pltpu.roll(row, rows - margin, 1), rows), slanted(pltpu.roll(row, rows, 1), 2 * rows)]
                )
                wy[v * out_rows : (v + 1) * out_rows, :] = band[:, : 3 * in_rows].astype(BF16)
            high, low = split(slanted(row_x[v : v + 1], cols)[:, :cols])
            wx[v, :cols, :cols] = high
            wx[v, cols:, :cols] = high
            wx[v, :cols, cols:] = low
            wx[v, cols:, cols:] = low
            size = 8 * planes
            high, low = split(slanted(row_z[v : v + 1], size)[:, :size])
            wz[v, :, :size] = high
            wz[v, :, size : 2 * size] = high
            wz[v, :, 2 * size :] = low


def call(kernel, outs, smem, arrays, scratch, name, flops):
    arrays = [pltpu.with_memory_space_constraint(a, VMEM) for a in arrays]
    return pl.pallas_call(
        kernel,
        out_shape=outs,
        in_specs=[pl.BlockSpec(memory_space=SMEM)] * len(smem) + [FULL] * len(arrays),
        out_specs=jax.tree.map(lambda _: FULL, outs),
        scratch_shapes=scratch,
        compiler_params=pltpu.CompilerParams(vmem_limit_bytes=LIMIT),
        cost_estimate=pl.CostEstimate(flops=flops, bytes_accessed=10**7, transcendentals=10**5),
        name=name,
    )(*smem, *arrays)


def make_weights(taps, planes, rows, cols):
    views = taps.shape[0]
    outs = [
        pltpu.VMEM((views * 3 * rows, 15 * rows), BF16),
        pltpu.VMEM((views, 2 * cols, 2 * cols), BF16),
        pltpu.VMEM((views, 8 * planes, 24 * planes), BF16),
        pltpu.VMEM((views, 2 * rows, 6 * rows), BF16),
        pltpu.VMEM((views, 2 * cols, 2 * cols), BF16),
        pltpu.VMEM((views, 8 * planes, 24 * planes), BF16),
    ]
    made = call(functools.partial(weights_kernel, rows), outs, [], [taps], [], "weights", 10**10)
    return made[:3], made[3:]


def stacked(pieces):
    columns = []
    for piece in pieces:
        high, low = split(piece)
        columns.append(jnp.concatenate([high, low, high], axis=0))
    return jnp.concatenate(columns, axis=1)


def interleaved(*streams):
    keyed = [((i + 0.5) / len(s), n, piece) for n, s in enumerate(streams) for i, piece in enumerate(s)]
    for _, _, piece in sorted(keyed, key=lambda k: k[:2]):
        piece()


def along_x(rows_ref, wx, out):
    planes, height, lanes = rows_ref.shape
    cols, part = lanes // 2, planes // 4

    def piece(z):
        both = dot(rows_ref[z : z + part].reshape(part * height, lanes), wx[...])
        out[z * height : (z + part) * height, :] = both[:, :cols] + both[:, cols:]

    return [functools.partial(piece, z) for z in range(0, planes, part)]


def forward_rows(parity, far_before, near, own, far_after, wy, ys):
    planes, rows, cols = far_before.shape
    views = ys.shape[0]
    height = 3 * rows
    side = parity[0]

    def plane(z):
        return jnp.concatenate(
            [far_before[z], near[1 - side, z], own[z], near[side, z], far_after[z]], axis=0
        )

    for z in range(0, planes, 2):
        high, low = split(dot(wy[...], stacked([plane(z), plane(z + 1)])))
        for j in range(2):
            for v in range(views):
                there = (slice(v * height, (v + 1) * height), slice(j * cols, (j + 1) * cols))
                ys[v, z + j, :, :cols] = high[there]
                ys[v, z + j, :, cols:] = low[there]


def forward_view(ys, wx, wz, out):
    planes, height, lanes = ys.shape
    cols = lanes // 2
    groups = []
    for pair in range(height // 16):
        rows_in = ys[:, 16 * pair : 16 * pair + 16, :].reshape(planes * 16, lanes)
        both = dot(rows_in, wx)
        value = (both[:, :cols] + both[:, cols:]).reshape(planes, 16, cols)
        groups += [value[:, 8 * g : 8 * g + 8, :].reshape(planes * 8, cols) for g in range(2)]
    result = dot(wz, stacked(groups))
    for g in range(len(groups)):
        out[:, 8 * g : 8 * g + 8, :] = result[:, g * cols : (g + 1) * cols].reshape(planes, 8, cols)


def adjoint_rows(halo, raw, blurred, wy, ya):
    planes, rows, cols = raw.shape

    def quotient(z):
        around = halo(z)
        counts = jnp.concatenate([around[:rows], raw[z], around[rows:]], axis=0)
        return counts * pl.reciprocal(jnp.maximum(blurred[z], TINY), approx=True)

    def piece(z):
        high, low = split(jnp.concatenate([quotient(z + j) for j in range(WIDE)], axis=1))
        both = dot(wy[...], jnp.concatenate([high, low], axis=0))
        high, low = split(both[:rows] + both[rows:])
        for j in range(WIDE):
            ya[z + j, :, :cols] = high[:, j * cols : (j + 1) * cols]
            ya[z + j, :, cols:] = low[:, j * cols : (j + 1) * cols]

    return [functools.partial(piece, z) for z in range(0, planes, WIDE)]


def adjoint_logs(first, ya, wx, wz, xs, acc):
    planes, rows, lanes = ya.shape
    cols = lanes // 2

    def piece():
        value = xs[...].reshape(planes, rows, cols)
        groups = [value[:, 8 * g : 8 * g + 8, :].reshape(planes * 8, cols) for g in range(2)]
        result = jnp.log(dot(wz[...], stacked(groups)))
        acc[...] = result if first else acc[...] + result

    return along_x(ya, wx, xs) + [piece]


def adjoint_of(chosen, begun, halo, raw, blurred, wy, wx, wz, ya, yb, xs, acc):
    def rows_of(i):
        if i == len(chosen):
            return []
        v = chosen[i]
        return adjoint_rows(halo(v), raw.at[v], blurred.at[v], wy.at[v], (ya, yb)[i % 2])

    interleaved(rows_of(0))
    for i, v in enumerate(chosen):
        logs = adjoint_logs(i == 0 and not begun, (ya, yb)[i % 2], wx.at[v], wz.at[v], xs.at[i % 2], acc)
        interleaved(logs, rows_of(i + 1))


def updated(current, acc, views, out):
    planes, rows, cols = out.shape
    for g in range(rows // 8):
        here = slice(8 * g, 8 * g + 8)
        exponent = acc[:, g * cols : (g + 1) * cols].reshape(planes, 8, cols) * (1.0 / views)
        out[:, here, :] = current[:, here, :] * jnp.exp(exponent)


def plane_halo(chosen, before, after, halos):
    planes, rows = halos.shape[1], halos.shape[2] // 2
    stride = len(chosen) * planes
    count = before.shape[0] // stride
    empty = jnp.zeros((rows - count, before.shape[1]), F32)

    def of_view(v):
        i = v - chosen[0]

        def of_plane(z):
            at = pl.ds(i * planes + z, count, stride=stride)
            around = jnp.concatenate([before[at, :], empty, after[at, :], empty], axis=0)
            halos[i, z] = around
            return around

        return of_plane

    return of_view


def each_step(steps, body):
    def run(step, _):
        body(step)
        return 0

    lax.fori_loop(0, steps, run, 0)


def forward_kernel(parity, wzs, far_before, near, own, far_after, wy, wx, wz, raw, wyx, out, sums, ys):
    views = ys.shape[0]
    forward_rows(parity, far_before, near, own, far_after, wy, ys)
    each_step(views, lambda v: forward_view(ys.at[v], wx[v], wz[v], out.at[v]))
    sums[...] = jnp.zeros_like(sums)
    for v in range(views):
        sums[v : v + 1, :] = jnp.sum(jnp.sum(raw[v], axis=0), axis=0, keepdims=True)
    weighted_sums(own, wzs, wyx, sums, sums.shape[0] // 3)


def weighted_sums(values, wzs, wyx, sums, at):
    planes, rows, cols = values.shape
    for v in range(wyx.shape[0]):
        total = jnp.zeros((rows, cols), F32)
        for z in range(planes):
            total = total + wzs[v, z] * values[z]
        sums[at + v : at + v + 1, :] = jnp.sum(total * wyx[v], axis=0, keepdims=True)


def early_adjoint_kernel(chosen, before, after, raw, blurred, wy, wx, wz, acc, halos, ya, yb, xs):
    halo = plane_halo(chosen, before, after, halos)
    adjoint_of(chosen, False, halo, raw, blurred, wy, wx, wz, ya, yb, xs, acc)


def late_adjoint_kernel(
    chosen, wzs, before, after, raw, blurred, wy, wx, wz, known_acc, current, wyx, known, out, sums, halos, ya, yb, xs, acc
):
    acc[...] = known_acc[...]
    halo = plane_halo(chosen, before, after, halos)
    adjoint_of(chosen, True, halo, raw, blurred, wy, wx, wz, ya, yb, xs, acc)
    updated(current, acc[...], raw.shape[0], out)
    sums[...] = known[...]
    weighted_sums(out, wzs, wyx, sums, 2 * sums.shape[0] // 3)


def iteration_kernel(
    parity, far_before, near, own, far_after, early, late, raw, wy, wx, wz, wya, wxa, wza,
    out, ys, blurred, ya, yb, xs, acc,
):
    views, split_at = ys.shape[0], early.shape[0]
    forward_rows(parity, far_before, near, own, far_after, wy, ys)
    each_step(views, lambda v: forward_view(ys.at[v], wx[v], wz[v], blurred.at[v]))

    def halo(v):
        return lambda z: early[v, z] if v < split_at else late[v - split_at, z]

    adjoint_of(range(views), False, halo, raw, blurred, wya, wxa, wza, ya, yb, xs, acc)
    updated(own, acc[...], views, out)


def pack_kernel(raw, *refs):
    last, leading = refs[-2:]
    count, rows = last.shape[0] // raw.shape[0], raw.shape[1]
    flat = raw.reshape(raw.shape[0] * rows, raw.shape[2])
    for y in range(count):
        here = slice(y * raw.shape[0], (y + 1) * raw.shape[0])
        last[here, :] = flat[pl.ds(rows - count + y, raw.shape[0], stride=rows), :]
        leading[here, :] = flat[pl.ds(y, raw.shape[0], stride=rows), :]


def packed(raw, chosen, count, *awaited):
    _, planes, rows, cols = raw.shape
    part = raw[chosen[0] : chosen[-1] + 1].reshape(len(chosen) * planes, rows, cols)
    outs = [pltpu.VMEM((count * part.shape[0], cols), F32)] * 2
    return call(pack_kernel, outs, [], [part, *awaited], [], "pack", 10**6)


def scaled_kernel(views, values, part, rest, out):
    sums = jnp.sum(part[...] + rest[...], axis=1, keepdims=True)
    space = sums.shape[0] // 3
    total, first, second = (sums[i * space : i * space + views] for i in range(3))
    scale = jnp.sum(jnp.log(first / total) + jnp.log(second / total), axis=0, keepdims=True)
    out[...] = values[...] * jnp.exp(scale * (1.0 / views))[None]


def adjoint_scratch(planes, rows, cols):
    return [
        pltpu.VMEM((planes, rows, 2 * cols), BF16),
        pltpu.VMEM((planes, rows, 2 * cols), BF16),
        pltpu.VMEM((2, planes * rows, cols), F32),
    ]


def forward(parity, slabs, weights, raw, wzs, wyx):
    planes, rows, cols = slabs[0].shape
    views = raw.shape[0]
    outs = [pltpu.VMEM((views, planes, 3 * rows, cols), F32), pltpu.VMEM((24 * -(-views // 8), cols), F32)]
    scratch = [pltpu.VMEM((views, planes, 3 * rows, 2 * cols), BF16)]
    return call(forward_kernel, outs, [parity, wzs], [*slabs, *weights, raw, wyx], scratch, "forward", 10**10)


def first_adjoint(groups, current, blurred, befores, raw, afters, weights, wzs, wyx, known):
    planes, rows, cols = current.shape
    shared = (raw, blurred, *weights)
    scratch = adjoint_scratch(planes, rows, cols)
    acc = pltpu.VMEM((planes * 8, rows // 8 * cols), F32)
    halos = [pltpu.VMEM((len(g), planes, 2 * rows, cols), F32) for g in groups]
    kernel = functools.partial(early_adjoint_kernel, groups[0])
    arrays = [befores[0], afters[0], *shared]
    partial, early = call(kernel, [acc, halos[0]], [], arrays, scratch, "early_adjoint", 10**10)
    kernel = functools.partial(late_adjoint_kernel, groups[1])
    arrays = [befores[1], afters[1], *shared, partial, current, wyx, known]
    outs = [pltpu.VMEM(current.shape, F32), pltpu.VMEM(known.shape, F32), halos[1]]
    out, sums, late = call(kernel, outs, [wzs], arrays, scratch + [acc], "late_adjoint", 10**10)
    return out, sums, (early, late)


def full_iteration(parity, slabs, halos, raw, weights, adjoint_weights):
    planes, rows, cols = slabs[0].shape
    views = raw.shape[0]
    scratch = [
        pltpu.VMEM((views, planes, 3 * rows, 2 * cols), BF16),
        pltpu.VMEM((views, planes, 3 * rows, cols), F32),
    ]
    return call(
        iteration_kernel,
        pltpu.VMEM((planes, rows, cols), F32),
        [parity],
        [*slabs, *halos, raw, *weights, *adjoint_weights],
        scratch + adjoint_scratch(planes, rows, cols) + [pltpu.VMEM((planes * 8, rows // 8 * cols), F32)],
        "iteration",
        2 * 10**10,
    )


def two_slabs_away(value, count):
    up = [(i, i + 2) for i in range(count - 2)]
    down = [(j, i) for i, j in up]
    return lax.ppermute(value, "slab", up), lax.ppermute(value, "slab", down)


def with_near(value, far_before, far_after, parity, count):
    swap = [(i, i + 1 - 2 * (i % 2)) for i in range(count)]
    passed = jnp.stack([value, jnp.where(parity[0] == 0, far_after, far_before)])
    near = lax.ppermute(passed, "slab", swap)
    return far_before, near, value, far_after


def tap_sums(taps, offset, extent, total):
    count = taps.shape[1]
    target = offset + jnp.arange(extent)[None, :] - jnp.arange(count)[:, None] + count // 2
    reach = jnp.where((target >= 0) & (target < total), 1.0, 0.0).astype(F32)
    return jnp.sum(taps[:, :, None] * reach[None], axis=1)


def per_device(estimate, raw, taps):
    views = raw.shape[0]
    planes, rows, cols = estimate.shape
    count = lax.axis_size("slab")
    assert 16 == rows >= taps.shape[2] // 2 and count & (count - 1) == 0
    up = [(i, i + 1) for i in range(count - 1)]
    down = [(j, i) for i, j in up]
    place = lax.axis_index("slab")
    parity = (place % 2).reshape(1)

    far = two_slabs_away(estimate, count)
    margin = taps.shape[2] // 2
    groups = (range(0, 2 * views // 3), range(2 * views // 3, views))
    edges = packed(raw, groups[0], margin)
    forward_weights, adjoint_weights = make_weights(taps, planes, rows, cols)
    befores = [lax.ppermute(edges[0], "slab", up)]
    afters = [lax.ppermute(edges[1], "slab", down)]

    wzs = tap_sums(taps[:, 0], 0, planes, planes)
    wy_sums = tap_sums(taps[:, 1], place * rows, rows, count * rows)
    wx_sums = tap_sums(taps[:, 2], 0, cols, cols)
    wyx = wy_sums[:, :, None] * wx_sums[:, None, :]

    far_before, near, own, far_after = with_near(estimate, *far, parity, count)
    edges = packed(raw, groups[1], margin, near)
    befores.append(lax.ppermute(edges[0], "slab", up))
    afters.append(lax.ppermute(edges[1], "slab", down))
    slabs = (far_before, near, own, far_after)
    blurred, known = forward(parity, slabs, forward_weights, raw, wzs, wyx)
    current, sums, halos = first_adjoint(
        groups, estimate, blurred, befores, raw, afters, adjoint_weights, wzs, wyx, known
    )

    far = two_slabs_away(current, count)
    bits = [1 << b for b in range(count.bit_length() - 1)]
    rounds = [bits[:1], [sum(bits[2:4])] + bits[3:1:-1], *([b] for b in bits[4:]), bits[1:2]]
    for r, distances in enumerate(rounds):
        others = [lax.ppermute(sums, "slab", [(i, i ^ d) for i in range(count)]) for d in distances]
        if r == 1:
            *far, sums = lax.optimization_barrier((*far, sums + sum(others)))
        elif r < len(rounds) - 1:
            sums = sums + sum(others)
    slabs = with_near(current, *far, parity, count)
    current = full_iteration(parity, slabs, halos, raw, forward_weights, adjoint_weights)
    out = jax.ShapeDtypeStruct(current.shape, F32)
    scaled = functools.partial(scaled_kernel, views)
    return call(scaled, out, [], [current, sums, others[0]], [], "scaled", 10**5)


def solution(mesh):
    placed = (P("blocks", "slab", None), P(None, "blocks", "slab", None), P())
    return jax.shard_map(
        per_device, mesh=mesh, in_specs=placed, out_specs=P("blocks", "slab", None), check_vma=False
    )
```

```python
import functools

import jax
import jax.numpy as jnp
import numpy as np
from jax import lax
from jax.experimental import pallas as pl
from jax.experimental.pallas import tpu as pltpu
from jax.sharding import PartitionSpec as P

F32 = jnp.float32
BF16 = jnp.bfloat16
VMEM = pltpu.MemorySpace.VMEM
SMEM = pltpu.MemorySpace.SMEM
FULL = pl.BlockSpec(memory_space=VMEM)
LIMIT = 20 * 1024 * 1024
WIDE = 4
TINY = float(np.finfo(np.float32).tiny)


def split(value):
    high = value.astype(BF16)
    low = (value - high.astype(F32)).astype(BF16)
    return high, low


def dot(a, b):
    return jnp.dot(a, b, preferred_element_type=F32)


def placed_row(taps, lane_of_tap, width):
    count = taps.shape[1]
    tap = lax.broadcasted_iota(jnp.int32, (count, width), 0)
    lane = lax.broadcasted_iota(jnp.int32, (count, width), 1)
    onehot = jnp.where(lane == lane_of_tap(tap), 1.0, 0.0).astype(F32)
    return jnp.dot(taps, onehot, precision=lax.Precision.HIGHEST, preferred_element_type=F32)


def slanted(row, height):
    full = jnp.broadcast_to(row, (height, row.shape[1]))
    return pltpu.roll(full, 0, 1, stride=1, stride_axis=0)


def weights_kernel(rows, taps_ref, *outs):
    views, _, count = taps_ref.shape
    margin = count // 2
    for flip in (False, True):
        wy, wx, wz = outs[3 * flip : 3 * flip + 3]
        order = (lambda k: count - 1 - k) if flip else (lambda k: k)
        out_rows = rows if flip else 3 * rows
        in_rows = out_rows + 2 * rows
        planes = wz.shape[1] // 8
        cols = wx.shape[1] // 2
        row_y = placed_row(taps_ref[:, 1, :], lambda k: order(k) + rows - margin, 256)
        high = row_y.astype(BF16).astype(F32)
        low = row_y - high
        if flip:
            row_y = (high, low)
        else:
            row_y = high + pltpu.roll(high, in_rows, 1) + pltpu.roll(low, 2 * in_rows, 1)
        row_x = placed_row(taps_ref[:, 2, :], lambda k: lax.rem(margin - order(k) + 2 * cols, 2 * cols), 2 * cols)
        width_z = 16 * planes
        row_z = placed_row(
            taps_ref[:, 0, :], lambda k: lax.rem(8 * (order(k) - margin) + width_z, width_z), width_z
        )
        for v in range(views):
            if flip:
                lane = lax.broadcasted_iota(jnp.int32, (rows, 256), 1)
                for j, row in enumerate(row_y):
                    band = slanted(row[v : v + 1], rows)
                    shifted = pltpu.roll(band, 256 - (rows - margin), 1)
                    band = jnp.where(lane < margin, shifted, jnp.where(lane < rows, 0.0, band))
                    band = band + pltpu.roll(band, in_rows, 1)
                    wy[v, j * rows : (j + 1) * rows, :] = band[:, : 2 * in_rows].astype(BF16)
            else:
                row = row_y[v : v + 1]
                band = jnp.concatenate(
                    [slanted(pltpu.roll(row, rows - margin, 1), rows), slanted(pltpu.roll(row, rows, 1), 2 * rows)]
                )
                wy[v * out_rows : (v + 1) * out_rows, :] = band[:, : 3 * in_rows].astype(BF16)
            high, low = split(slanted(row_x[v : v + 1], cols)[:, :cols])
            wx[v, :cols, :cols] = high
            wx[v, cols:, :cols] = high
            wx[v, :cols, cols:] = low
            wx[v, cols:, cols:] = low
            size = 8 * planes
            high, low = split(slanted(row_z[v : v + 1], size)[:, :size])
            wz[v, :, :size] = high
            wz[v, :, size : 2 * size] = high
            wz[v, :, 2 * size :] = low


def call(kernel, outs, smem, arrays, scratch, name, flops):
    arrays = [pltpu.with_memory_space_constraint(a, VMEM) for a in arrays]
    return pl.pallas_call(
        kernel,
        out_shape=outs,
        in_specs=[pl.BlockSpec(memory_space=SMEM)] * len(smem) + [FULL] * len(arrays),
        out_specs=jax.tree.map(lambda _: FULL, outs),
        scratch_shapes=scratch,
        compiler_params=pltpu.CompilerParams(vmem_limit_bytes=LIMIT),
        cost_estimate=pl.CostEstimate(flops=flops, bytes_accessed=10**7, transcendentals=10**5),
        name=name,
    )(*smem, *arrays)


def make_weights(taps, planes, rows, cols):
    views = taps.shape[0]
    outs = [
        pltpu.VMEM((views * 3 * rows, 15 * rows), BF16),
        pltpu.VMEM((views, 2 * cols, 2 * cols), BF16),
        pltpu.VMEM((views, 8 * planes, 24 * planes), BF16),
        pltpu.VMEM((views, 2 * rows, 6 * rows), BF16),
        pltpu.VMEM((views, 2 * cols, 2 * cols), BF16),
        pltpu.VMEM((views, 8 * planes, 24 * planes), BF16),
    ]
    made = call(functools.partial(weights_kernel, rows), outs, [], [taps], [], "weights", 10**10)
    return made[:3], made[3:]


def stacked(pieces):
    columns = []
    for piece in pieces:
        high, low = split(piece)
        columns.append(jnp.concatenate([high, low, high], axis=0))
    return jnp.concatenate(columns, axis=1)


def interleaved(*streams):
    keyed = [((i + 0.5) / len(s), n, piece) for n, s in enumerate(streams) for i, piece in enumerate(s)]
    for _, _, piece in sorted(keyed, key=lambda k: k[:2]):
        piece()


def along_x(rows_ref, wx, out):
    planes, height, lanes = rows_ref.shape
    cols, part = lanes // 2, planes // 4

    def piece(z):
        both = dot(rows_ref[z : z + part].reshape(part * height, lanes), wx[...])
        out[z * height : (z + part) * height, :] = both[:, :cols] + both[:, cols:]

    return [functools.partial(piece, z) for z in range(0, planes, part)]


def forward_rows(parity, far_before, near, own, far_after, wy, ys):
    planes, rows, cols = far_before.shape
    views = ys.shape[0]
    height = 3 * rows
    side = parity[0]

    def plane(z):
        return jnp.concatenate(
            [far_before[z], near[1 - side, z], own[z], near[side, z], far_after[z]], axis=0
        )

    for z in range(0, planes, 2):
        high, low = split(dot(wy[...], stacked([plane(z), plane(z + 1)])))
        for j in range(2):
            for v in range(views):
                there = (slice(v * height, (v + 1) * height), slice(j * cols, (j + 1) * cols))
                ys[v, z + j, :, :cols] = high[there]
                ys[v, z + j, :, cols:] = low[there]


def forward_view(ys, wx, wz, out):
    planes, height, lanes = ys.shape
    cols = lanes // 2
    groups = []
    for pair in range(height // 16):
        rows_in = ys[:, 16 * pair : 16 * pair + 16, :].reshape(planes * 16, lanes)
        both = dot(rows_in, wx)
        value = (both[:, :cols] + both[:, cols:]).reshape(planes, 16, cols)
        groups += [value[:, 8 * g : 8 * g + 8, :].reshape(planes * 8, cols) for g in range(2)]
    result = dot(wz, stacked(groups))
    for g in range(len(groups)):
        out[:, 8 * g : 8 * g + 8, :] = result[:, g * cols : (g + 1) * cols].reshape(planes, 8, cols)


def adjoint_rows(halo, raw, blurred, wy, ya):
    planes, rows, cols = raw.shape

    def quotient(z):
        around = halo(z)
        counts = jnp.concatenate([around[:rows], raw[z], around[rows:]], axis=0)
        return counts * pl.reciprocal(jnp.maximum(blurred[z], TINY), approx=True)

    def piece(z):
        high, low = split(jnp.concatenate([quotient(z + j) for j in range(WIDE)], axis=1))
        both = dot(wy[...], jnp.concatenate([high, low], axis=0))
        high, low = split(both[:rows] + both[rows:])
        for j in range(WIDE):
            ya[z + j, :, :cols] = high[:, j * cols : (j + 1) * cols]
            ya[z + j, :, cols:] = low[:, j * cols : (j + 1) * cols]

    return [functools.partial(piece, z) for z in range(0, planes, WIDE)]


def adjoint_logs(first, ya, wx, wz, xs, acc):
    planes, rows, lanes = ya.shape
    cols = lanes // 2

    def piece():
        value = xs[...].reshape(planes, rows, cols)
        groups = [value[:, 8 * g : 8 * g + 8, :].reshape(planes * 8, cols) for g in range(2)]
        result = jnp.log(dot(wz[...], stacked(groups)))
        acc[...] = result if first else acc[...] + result

    return along_x(ya, wx, xs) + [piece]


def adjoint_of(chosen, begun, halo, raw, blurred, wy, wx, wz, ya, yb, xs, acc):
    def rows_of(i):
        if i == len(chosen):
            return []
        v = chosen[i]
        return adjoint_rows(halo(v), raw.at[v], blurred.at[v], wy.at[v], (ya, yb)[i % 2])

    interleaved(rows_of(0))
    for i, v in enumerate(chosen):
        logs = adjoint_logs(i == 0 and not begun, (ya, yb)[i % 2], wx.at[v], wz.at[v], xs.at[i % 2], acc)
        interleaved(logs, rows_of(i + 1))


def updated(current, acc, views, out):
    planes, rows, cols = out.shape
    for g in range(rows // 8):
        here = slice(8 * g, 8 * g + 8)
        exponent = acc[:, g * cols : (g + 1) * cols].reshape(planes, 8, cols) * (1.0 / views)
        out[:, here, :] = current[:, here, :] * jnp.exp(exponent)


def plane_halo(chosen, before, after, halos):
    planes, rows = halos.shape[1], halos.shape[2] // 2
    stride = len(chosen) * planes
    count = before.shape[0] // stride
    empty = jnp.zeros((rows - count, before.shape[1]), F32)

    def of_view(v):
        i = v - chosen[0]

        def of_plane(z):
            at = pl.ds(i * planes + z, count, stride=stride)
            around = jnp.concatenate([before[at, :], empty, after[at, :], empty], axis=0)
            halos[i, z] = around
            return around

        return of_plane

    return of_view


def each_step(steps, body):
    def run(step, _):
        body(step)
        return 0

    lax.fori_loop(0, steps, run, 0)


def forward_kernel(parity, wzs, far_before, near, own, far_after, wy, wx, wz, raw, wyx, out, sums, ys):
    views = ys.shape[0]
    forward_rows(parity, far_before, near, own, far_after, wy, ys)
    each_step(views, lambda v: forward_view(ys.at[v], wx[v], wz[v], out.at[v]))
    sums[...] = jnp.zeros_like(sums)
    for v in range(views):
        sums[v : v + 1, :] = jnp.sum(jnp.sum(raw[v], axis=0), axis=0, keepdims=True)
    weighted_sums(own, wzs, wyx, sums, sums.shape[0] // 3)


def weighted_sums(values, wzs, wyx, sums, at):
    planes, rows, cols = values.shape
    views = wyx.shape[0]
    totals = [jnp.zeros((rows, cols), F32)] * views
    for z in range(planes):
        plane = values[z]
        totals = [totals[v] + wzs[v, z] * plane for v in range(views)]
    for v in range(views):
        sums[at + v : at + v + 1, :] = jnp.sum(totals[v] * wyx[v], axis=0, keepdims=True)


def early_adjoint_kernel(chosen, before, after, raw, blurred, wy, wx, wz, acc, halos, ya, yb, xs):
    halo = plane_halo(chosen, before, after, halos)
    adjoint_of(chosen, False, halo, raw, blurred, wy, wx, wz, ya, yb, xs, acc)


def late_adjoint_kernel(
    chosen, wzs, before, after, raw, blurred, wy, wx, wz, known_acc, current, wyx, known, out, sums, halos, ya, yb, xs, acc
):
    acc[...] = known_acc[...]
    halo = plane_halo(chosen, before, after, halos)
    adjoint_of(chosen, True, halo, raw, blurred, wy, wx, wz, ya, yb, xs, acc)
    updated(current, acc[...], raw.shape[0], out)
    sums[...] = known[...]
    weighted_sums(out, wzs, wyx, sums, 2 * sums.shape[0] // 3)


def iteration_kernel(
    parity, far_before, near, own, far_after, early, late, raw, wy, wx, wz, wya, wxa, wza,
    out, ys, blurred, ya, yb, xs, acc,
):
    views, split_at = ys.shape[0], early.shape[0]
    forward_rows(parity, far_before, near, own, far_after, wy, ys)
    each_step(views, lambda v: forward_view(ys.at[v], wx[v], wz[v], blurred.at[v]))

    def halo(v):
        return lambda z: early[v, z] if v < split_at else late[v - split_at, z]

    adjoint_of(range(views), False, halo, raw, blurred, wya, wxa, wza, ya, yb, xs, acc)
    updated(own, acc[...], views, out)


def pack_kernel(raw, *refs):
    last, leading = refs[-2:]
    count, rows = last.shape[0] // raw.shape[0], raw.shape[1]
    flat = raw.reshape(raw.shape[0] * rows, raw.shape[2])
    for y in range(count):
        here = slice(y * raw.shape[0], (y + 1) * raw.shape[0])
        last[here, :] = flat[pl.ds(rows - count + y, raw.shape[0], stride=rows), :]
        leading[here, :] = flat[pl.ds(y, raw.shape[0], stride=rows), :]


def packed(raw, chosen, count, *awaited):
    _, planes, rows, cols = raw.shape
    part = raw[chosen[0] : chosen[-1] + 1].reshape(len(chosen) * planes, rows, cols)
    outs = [pltpu.VMEM((count * part.shape[0], cols), F32)] * 2
    return call(pack_kernel, outs, [], [part, *awaited], [], "pack", 10**6)


def scaled_kernel(views, values, part, rest, out):
    sums = jnp.sum(part[...] + rest[...], axis=1, keepdims=True)
    space = sums.shape[0] // 3
    total, first, second = (sums[i * space : i * space + views] for i in range(3))
    scale = jnp.sum(jnp.log(first / total) + jnp.log(second / total), axis=0, keepdims=True)
    out[...] = values[...] * jnp.exp(scale * (1.0 / views))[None]


def adjoint_scratch(planes, rows, cols):
    return [
        pltpu.VMEM((planes, rows, 2 * cols), BF16),
        pltpu.VMEM((planes, rows, 2 * cols), BF16),
        pltpu.VMEM((2, planes * rows, cols), F32),
    ]


def forward(parity, slabs, weights, raw, wzs, wyx):
    planes, rows, cols = slabs[0].shape
    views = raw.shape[0]
    outs = [pltpu.VMEM((views, planes, 3 * rows, cols), F32), pltpu.VMEM((24 * -(-views // 8), cols), F32)]
    scratch = [pltpu.VMEM((views, planes, 3 * rows, 2 * cols), BF16)]
    return call(forward_kernel, outs, [parity, wzs], [*slabs, *weights, raw, wyx], scratch, "forward", 10**10)


def first_adjoint(groups, current, blurred, befores, raw, afters, weights, wzs, wyx, known):
    planes, rows, cols = current.shape
    shared = (raw, blurred, *weights)
    scratch = adjoint_scratch(planes, rows, cols)
    acc = pltpu.VMEM((planes * 8, rows // 8 * cols), F32)
    halos = [pltpu.VMEM((len(g), planes, 2 * rows, cols), F32) for g in groups]
    kernel = functools.partial(early_adjoint_kernel, groups[0])
    arrays = [befores[0], afters[0], *shared]
    partial, early = call(kernel, [acc, halos[0]], [], arrays, scratch, "early_adjoint", 10**10)
    kernel = functools.partial(late_adjoint_kernel, groups[1])
    arrays = [befores[1], afters[1], *shared, partial, current, wyx, known]
    outs = [pltpu.VMEM(current.shape, F32), pltpu.VMEM(known.shape, F32), halos[1]]
    out, sums, late = call(kernel, outs, [wzs], arrays, scratch + [acc], "late_adjoint", 10**10)
    return out, sums, (early, late)


def full_iteration(parity, slabs, halos, raw, weights, adjoint_weights):
    planes, rows, cols = slabs[0].shape
    views = raw.shape[0]
    scratch = [
        pltpu.VMEM((views, planes, 3 * rows, 2 * cols), BF16),
        pltpu.VMEM((views, planes, 3 * rows, cols), F32),
    ]
    return call(
        iteration_kernel,
        pltpu.VMEM((planes, rows, cols), F32),
        [parity],
        [*slabs, *halos, raw, *weights, *adjoint_weights],
        scratch + adjoint_scratch(planes, rows, cols) + [pltpu.VMEM((planes * 8, rows // 8 * cols), F32)],
        "iteration",
        2 * 10**10,
    )


def two_slabs_away(value, count):
    up = [(i, i + 2) for i in range(count - 2)]
    down = [(j, i) for i, j in up]
    return lax.ppermute(value, "slab", up), lax.ppermute(value, "slab", down)


def with_near(value, far_before, far_after, parity, count):
    swap = [(i, i + 1 - 2 * (i % 2)) for i in range(count)]
    passed = jnp.stack([value, jnp.where(parity[0] == 0, far_after, far_before)])
    near = lax.ppermute(passed, "slab", swap)
    return far_before, near, value, far_after


def tap_sums(taps, offset, extent, total):
    count = taps.shape[1]
    target = offset + jnp.arange(extent)[None, :] - jnp.arange(count)[:, None] + count // 2
    reach = jnp.where((target >= 0) & (target < total), 1.0, 0.0).astype(F32)
    return jnp.sum(taps[:, :, None] * reach[None], axis=1)


def per_device(estimate, raw, taps):
    views = raw.shape[0]
    planes, rows, cols = estimate.shape
    count = lax.axis_size("slab")
    assert 16 == rows >= taps.shape[2] // 2 and count & (count - 1) == 0
    up = [(i, i + 1) for i in range(count - 1)]
    down = [(j, i) for i, j in up]
    place = lax.axis_index("slab")
    parity = (place % 2).reshape(1)

    far = two_slabs_away(estimate, count)
    margin = taps.shape[2] // 2
    groups = (range(0, 2 * views // 3), range(2 * views // 3, views))
    edges = packed(raw, groups[0], margin)
    forward_weights, adjoint_weights = make_weights(taps, planes, rows, cols)
    befores = [lax.ppermute(edges[0], "slab", up)]
    afters = [lax.ppermute(edges[1], "slab", down)]

    wzs = tap_sums(taps[:, 0], 0, planes, planes)
    wy_sums = tap_sums(taps[:, 1], place * rows, rows, count * rows)
    wx_sums = tap_sums(taps[:, 2], 0, cols, cols)
    wyx = wy_sums[:, :, None] * wx_sums[:, None, :]

    far_before, near, own, far_after = with_near(estimate, *far, parity, count)
    edges = packed(raw, groups[1], margin, near)
    befores.append(lax.ppermute(edges[0], "slab", up))
    afters.append(lax.ppermute(edges[1], "slab", down))
    slabs = (far_before, near, own, far_after)
    blurred, known = forward(parity, slabs, forward_weights, raw, wzs, wyx)
    current, sums, halos = first_adjoint(
        groups, estimate, blurred, befores, raw, afters, adjoint_weights, wzs, wyx, known
    )

    far = two_slabs_away(current, count)
    bits = [1 << b for b in range(count.bit_length() - 1)]
    rounds = [bits[:1], [sum(bits[2:4])] + bits[3:1:-1], *([b] for b in bits[4:]), bits[1:2]]
    for r, distances in enumerate(rounds):
        others = [lax.ppermute(sums, "slab", [(i, i ^ d) for i in range(count)]) for d in distances]
        if r == 1:
            *far, sums = lax.optimization_barrier((*far, sums + sum(others)))
        elif r < len(rounds) - 1:
            sums = sums + sum(others)
    slabs = with_near(current, *far, parity, count)
    current = full_iteration(parity, slabs, halos, raw, forward_weights, adjoint_weights)
    out = jax.ShapeDtypeStruct(current.shape, F32)
    scaled = functools.partial(scaled_kernel, views)
    return call(scaled, out, [], [current, sums, others[0]], [], "scaled", 10**5)


def solution(mesh):
    placed = (P("blocks", "slab", None), P(None, "blocks", "slab", None), P())
    return jax.shard_map(
        per_device, mesh=mesh, in_specs=placed, out_specs=P("blocks", "slab", None), check_vma=False
    )
```
